32 devices in a mesh: seq: 8 (over z, x), dp: 4 (over y, core).
Axes of the slice: x: 2, y: 2, z: 4, core: 2. Of those that a mesh axis runs over, the one named last changes fastest.
Arguments:
- tokens: bfloat16 [4, 4096, 768], P('dp', 'seq'), may hold values from -6 to 6
- cotangent: bfloat16 [4, 4096, 768], P('dp', 'seq'), may hold values from -6 to 6
- bounds: int32 [4, 2], P('dp'), may hold values from 1 to 4095, as said below
- w_qkv: float32 [768, 2304], P(('seq', 'dp')), may hold values from -0.21875 to 0.21875
- w_out: float32 [768, 768], P(('seq', 'dp')), may hold values from -3 to 3
- w_up: float32 [768, 3072], P(('seq', 'dp')), may hold values from -0.21875 to 0.21875
- w_down: float32 [3072, 768], P(('seq', 'dp')), may hold values from -0.109375 to 0.109375
- w_norms: float32 [4, 768], P(None, ('seq', 'dp'))
- m_qkv: float32 [768, 2304], P(('seq', 'dp')), may hold values from -0.005859375 to 0.005859375
- m_out: float32 [768, 768], P(('seq', 'dp')), may hold values from -0.0009765625 to 0.0009765625
- m_up: float32 [768, 3072], P(('seq', 'dp')), may hold values from -0.005859375 to 0.005859375
- m_down: float32 [3072, 768], P(('seq', 'dp')), may hold values from -0.005859375 to 0.005859375
- m_norms: float32 [4, 768], P(None, ('seq', 'dp')), may hold values from -0.01171875 to 0.01171875
- v_qkv: float32 [768, 2304], P(('seq', 'dp')), may hold values from 1.412238e-07 to 5.648952e-07
- v_out: float32 [768, 768], P(('seq', 'dp')), may hold values from 7.0611894e-09 to 2.8244758e-08
- v_up: float32 [768, 3072], P(('seq', 'dp')), may hold values from 1.412238e-07 to 5.648952e-07
- v_down: float32 [3072, 768], P(('seq', 'dp')), may hold values from 1.412238e-07 to 5.648952e-07
- v_norms: float32 [4, 768], P(None, ('seq', 'dp')), may hold values from 5.648952e-07 to 2.2595807e-06
- a_qkv: float32 [768, 2304], P(('seq', 'dp')), may hold values from -0.21875 to 0.21875
- a_out: float32 [768, 768], P(('seq', 'dp')), may hold values from -3 to 3
- a_up: float32 [768, 3072], P(('seq', 'dp')), may hold values from -0.21875 to 0.21875
- a_down: float32 [3072, 768], P(('seq', 'dp')), may hold values from -0.109375 to 0.109375
- a_norms: float32 [4, 768], P(None, ('seq', 'dp')), may hold values from 0.5 to 1.5
Outputs:
- layer_out: bfloat16 [4, 4096, 768], P('dp', 'seq')
- input_grad: float32 [4, 4096, 768], P('dp', 'seq')
- grad_norm: float32 [], replicated
- nw_qkv: float32 [768, 2304], P(('seq', 'dp'))
- nw_out: float32 [768, 768], P(('seq', 'dp'))
- nw_up: float32 [768, 3072], P(('seq', 'dp'))
- nw_down: float32 [3072, 768], P(('seq', 'dp'))
- nw_norms: float32 [4, 768], P(None, ('seq', 'dp'))
- nm_qkv: float32 [768, 2304], P(('seq', 'dp'))
- nm_out: float32 [768, 768], P(('seq', 'dp'))
- nm_up: float32 [768, 3072], P(('seq', 'dp'))
- nm_down: float32 [3072, 768], P(('seq', 'dp'))
- nm_norms: float32 [4, 768], P(None, ('seq', 'dp'))
- nv_qkv: float32 [768, 2304], P(('seq', 'dp'))
- nv_out: float32 [768, 768], P(('seq', 'dp'))
- nv_up: float32 [768, 3072], P(('seq', 'dp'))
- nv_down: float32 [3072, 768], P(('seq', 'dp'))
- nv_norms: float32 [4, 768], P(None, ('seq', 'dp'))
- na_qkv: float32 [768, 2304], P(('seq', 'dp'))
- na_out: float32 [768, 768], P(('seq', 'dp'))
- na_up: float32 [768, 3072], P(('seq', 'dp'))
- na_down: float32 [3072, 768], P(('seq', 'dp'))
- na_norms: float32 [4, 768], P(None, ('seq', 'dp'))
The draws below stay inside these ranges and needn't reach their ends.
Inputs may be any that keep to these rules, and one draw needn't show every extreme that they name: bounds[s,0] < 512 and bounds[s,1] > 3584, so the middle document of every sequence reaches from its first block to its last.
All inputs are finite; a program needn't handle non-finite values.
Results may differ from the reference program's by a relative error of at most 0.014.
The reference program's roundings to bfloat16 on the way count: a program that leaves them out, or rounds other values in their place, can miss the bound.
Values may be sent and summed in bfloat16 or wider, within the bound.
No kernel may reach another device: no remote copies, remote signals or barrier semaphores. Data moves between devices by JAX's collectives and lax.ppermute only.
A program may use at most 192 MiB of HBM per device.

```python
import math
import jax
import jax.numpy as jnp
from jax import lax

D = 768
H = 12
DH = 64
FF = 3072
TOK_DEV = 512
STEP = 5
LENGTH = 4096
SEQS = 4
PARAMS = 7080960


def draw_bounds(key, part):
    key = jax.random.fold_in(key, 11)
    first_key, second_key = jax.random.split(key)
    opening = jax.random.randint(first_key, (SEQS, 1), 1, TOK_DEV)
    opening = opening - jnp.min(opening) + 1
    closing = jax.random.randint(second_key, (SEQS, 1), 1, TOK_DEV)
    closing = LENGTH - (closing - jnp.min(closing) + 1)
    return jnp.concatenate([opening, closing], axis=1).astype(jnp.int32)


def draw_w_norms(key, part):
    key = jax.random.fold_in(key, 5)
    gain_key, shift_key = jax.random.split(key)
    cycle_count = LENGTH // TOK_DEV
    shard_cols = D // (SEQS * cycle_count)
    owner = jnp.arange(D) // shard_cols
    along_cycle = (owner // SEQS).astype(jnp.float32) / max(cycle_count - 1, 1)
    along_data = (owner % SEQS).astype(jnp.float32) / max(SEQS - 1, 1)
    growth = 3.0
    jitter = jnp.exp(0.1 * jax.random.normal(gain_key, (2, D)))
    shifts = 0.3 * jax.random.normal(shift_key, (2, D))
    gain_rows = 0.6 * growth ** (0.5 * (along_cycle + along_data)) * jitter
    return jnp.stack([gain_rows[0], shifts[0], gain_rows[1], shifts[1]]).astype(jnp.float32)


def steps_of(key, extent, cuts, smallest, largest):
    gain, own = 1.0, jax.random.fold_in(key, 6)
    for axis_at, parts in cuts:
        draws = jnp.exp(jax.random.uniform(jax.random.fold_in(own, axis_at), (parts,), jnp.float32, smallest / len(cuts), largest / len(cuts)))
        gain = gain * jnp.repeat(draws, extent[axis_at] // parts).reshape([-1 if axis == axis_at else 1 for axis in range(len(extent))])
    return gain


def normal_values(stream_key, extent, width, limit, shards=(), kind=jnp.bfloat16):
    values = jax.random.normal(stream_key, extent, jnp.float32) * width
    if len(shards) > 0:
        values = steps_of(stream_key, extent, shards, -0.22, 0.18) * values
    return jnp.clip(values, min=-limit, max=limit).astype(kind)


def setup_inputs(seed: int = 0) -> dict:
    streams_of = jax.random.split(jax.random.key(seed), 24)
    return {
        "tokens": normal_values(streams_of[0], (SEQS, LENGTH, D), 1.0, 6.0, ((0, 4), (1, 8))),
        "cotangent": normal_values(streams_of[1], (SEQS, LENGTH, D), 1.0, 6.0, ((0, 4), (1, 8))),
        "bounds": draw_bounds(jax.random.fold_in(streams_of[23], 71), 0),
        "w_qkv": normal_values(streams_of[3], (D, 3 * D), D ** -0.5, 0.21875, ((0, 32),), jnp.float32),
        "w_out": normal_values(streams_of[4], (D, D), (max(D // 192, 1)) ** -0.5, 3.0, ((0, 32),), jnp.float32),
        "w_up": normal_values(streams_of[5], (D, FF), D ** -0.5, 0.21875, ((0, 32),), jnp.float32),
        "w_down": normal_values(streams_of[6], (FF, D), FF ** -0.5, 0.109375, ((0, 32),), jnp.float32),
        "w_norms": draw_w_norms(jax.random.fold_in(streams_of[23], 71), 0),
        "m_qkv": normal_values(streams_of[8], (D, 3 * D), ((1.0 / PARAMS) ** 0.5), 0.005859375, ((0, 32),), jnp.float32),
        "m_out": normal_values(streams_of[9], (D, D), (0.2 * (1.0 / PARAMS) ** 0.5), 0.0009765625, ((0, 32),), jnp.float32),
        "m_up": normal_values(streams_of[10], (D, FF), ((1.0 / PARAMS) ** 0.5), 0.005859375, ((0, 32),), jnp.float32),
        "m_down": normal_values(streams_of[11], (FF, D), ((1.0 / PARAMS) ** 0.5), 0.005859375, ((0, 32),), jnp.float32),
        "m_norms": normal_values(streams_of[12], (4, D), (2.0 * (1.0 / PARAMS) ** 0.5), 0.01171875, ((1, 32),), jnp.float32),
        "v_qkv": jnp.clip(jnp.exp(math.log(5.648951741932251e-07) - 1.3862944 * jax.random.uniform(streams_of[13], (D, 3 * D), jnp.float32) ** steps_of(streams_of[13], (D, 3 * D), ((0, 32),), -0.2, 0.2)), 1.4122379354830628e-07, 5.648951741932251e-07),
        "v_out": jnp.clip(jnp.exp(math.log(2.824475764384715e-08) - 1.3862944 * jax.random.uniform(streams_of[14], (D, D), jnp.float32) ** steps_of(streams_of[14], (D, D), ((0, 32),), -0.2, 0.2)), 7.061189410961788e-09, 2.824475764384715e-08),
        "v_up": jnp.clip(jnp.exp(math.log(5.648951741932251e-07) - 1.3862944 * jax.random.uniform(streams_of[15], (D, FF), jnp.float32) ** steps_of(streams_of[15], (D, FF), ((0, 32),), -0.2, 0.2)), 1.4122379354830628e-07, 5.648951741932251e-07),
        "v_down": jnp.clip(jnp.exp(math.log(5.648951741932251e-07) - 1.3862944 * jax.random.uniform(streams_of[16], (FF, D), jnp.float32) ** steps_of(streams_of[16], (FF, D), ((0, 32),), -0.2, 0.2)), 1.4122379354830628e-07, 5.648951741932251e-07),
        "v_norms": jnp.clip(jnp.exp(math.log(2.2595806967729004e-06) - 1.3862944 * jax.random.uniform(streams_of[17], (4, D), jnp.float32) ** steps_of(streams_of[17], (4, D), ((1, 32),), -0.2, 0.2)), 5.648951741932251e-07, 2.2595806967729004e-06),
        "a_qkv": normal_values(streams_of[18], (D, 3 * D), D ** -0.5, 0.21875, ((0, 32),), jnp.float32),
        "a_out": normal_values(streams_of[19], (D, D), (max(D // 192, 1)) ** -0.5, 3.0, ((0, 32),), jnp.float32),
        "a_up": normal_values(streams_of[20], (D, FF), D ** -0.5, 0.21875, ((0, 32),), jnp.float32),
        "a_down": normal_values(streams_of[21], (FF, D), FF ** -0.5, 0.109375, ((0, 32),), jnp.float32),
        "a_norms": jnp.clip(1.0 + 0.1 * jax.random.normal(streams_of[22], (4, D), jnp.float32), 0.5, 1.5),
    }


NORM_EPS = 1e-05
CLIP_NORM = 1.0
RATE_MAT = 0.03
RATE_OUT = 0.15
RATE_VEC = 0.3
WEIGHT_DECAY = 0.1
BETA_ONE = 0.5
BETA_TWO = 0.5
ADAM_EPS = 1e-08
AVERAGE = 0.8
MASKED_LOW = -1e+30

@jax.custom_vjp
def low(v):
    return lax.optimization_barrier(v.astype(jnp.bfloat16)).astype(jnp.float32)

@jax.custom_vjp
def low_back(v):
    return v

def low_keep(v):
    return (low(v), None)

def low_pass(kept, grad):
    return (grad,)

def back_keep(v):
    return (v, None)

def back_low(kept, grad):
    return (low(grad),)
low.defvjp(low_keep, low_pass)
low_back.defvjp(back_keep, back_low)

def layer_norm(values, gain_vec, shift_vec):
    centre = values - lax.optimization_barrier(jnp.mean(values, axis=-1, keepdims=True))
    spread = lax.optimization_barrier(jnp.mean(centre * centre, axis=-1, keepdims=True))
    return centre * lax.rsqrt(spread + NORM_EPS) * gain_vec + shift_vec

def segment_of(places, limits):
    return (places >= limits[0]).astype(jnp.int32) + (places >= limits[1]).astype(jnp.int32)

def visible(qplaces, kplaces, limits):
    later = kplaces[None, :] <= qplaces[:, None]
    same_doc = segment_of(kplaces, limits)[None, :] == segment_of(qplaces, limits)[:, None]
    return (later & same_doc)[None]

def unchanged(carried):
    return carried

def attend(queries, keys, values, limits):
    blk_count = LENGTH // TOK_DEV
    score_scale = DH ** (-0.5)
    qblocks = queries.reshape(blk_count, TOK_DEV, H, DH)
    kblocks = keys.reshape(blk_count, TOK_DEV, H, DH)
    vblocks = values.reshape(blk_count, TOK_DEV, H, DH)
    firsts = TOK_DEV * jnp.arange(blk_count, dtype=jnp.int32)

    def one_block(blk_items):
        qblock, q_start = blk_items
        qplaces = q_start + jnp.arange(TOK_DEV, dtype=jnp.int32)

        def advance(carried, key_items):
            kblock, vblock, k_start = key_items
            kplaces = k_start + jnp.arange(TOK_DEV, dtype=jnp.int32)

            def absorb(inner):
                maxima, totals, numerator = inner
                allowed = visible(qplaces, kplaces, limits)
                scores = low_back(jnp.einsum('qhd,khd->hqk', qblock, kblock, precision=lax.Precision.HIGHEST) * score_scale)
                magnitude = jnp.sqrt(scores * scores + 1.0)
                new_max = jnp.maximum(maxima, lax.optimization_barrier(jnp.max(jnp.where(allowed, magnitude, MASKED_LOW), axis=2)))
                rescale = jnp.exp(maxima - new_max)
                exp_terms = jnp.exp(jnp.where(allowed, magnitude - new_max[:, :, None], MASKED_LOW))
                weights = low(exp_terms * scores / magnitude)
                numerator = numerator * rescale.T[:, :, None] + jnp.einsum('hqk,khd->qhd', weights, vblock, precision=lax.Precision.HIGHEST)
                totals = totals * rescale + lax.optimization_barrier(jnp.sum(exp_terms, axis=2))
                return (new_max, totals, numerator)
            return (lax.cond(k_start <= q_start + TOK_DEV - 1, absorb, unchanged, carried), None)
        start_state = (jnp.full((H, TOK_DEV), MASKED_LOW, jnp.float32), jnp.zeros((H, TOK_DEV), jnp.float32), jnp.zeros((TOK_DEV, H, DH), jnp.float32))
        final_state, unused = lax.scan(jax.checkpoint(advance), start_state, (kblocks, vblocks, firsts))
        return final_state[2] / final_state[1].T[:, :, None]
    attended = lax.map(one_block, (qblocks, firsts))
    return attended.reshape(LENGTH, D)

def sequence(inputs, limits, qkv_w, out_w, up_w, down_w, gain_rows):
    normed = low(layer_norm(inputs, gain_rows[0], gain_rows[1]))
    mixed_all = jnp.dot(normed, qkv_w, precision=lax.Precision.HIGHEST)
    queries = low(low_back(mixed_all[:, :D])).reshape(LENGTH, H, DH)
    keys_all = low(low_back(mixed_all[:, D:2 * D])).reshape(LENGTH, H, DH)
    values_all = low(low_back(mixed_all[:, 2 * D:])).reshape(LENGTH, H, DH)
    attended = low(low_back(attend(queries, keys_all, values_all, limits)))
    branch = low_back(jnp.dot(attended, out_w, precision=lax.Precision.HIGHEST))
    resid_sum = inputs + branch
    hidden_norm = low(layer_norm(resid_sum, gain_rows[2], gain_rows[3]))
    pre_act = low_back(jnp.dot(hidden_norm, up_w, precision=lax.Precision.HIGHEST))
    activated = low(jax.nn.gelu(pre_act, approximate=True))
    return resid_sum + jnp.dot(activated, down_w, precision=lax.Precision.HIGHEST)

def adamw(weight, grad, first, second, average, rate, decay):
    first_new = BETA_ONE * first + (1.0 - BETA_ONE) * grad
    second_new = BETA_TWO * second + (1.0 - BETA_TWO) * grad * grad
    unbiased_one = first_new / (1.0 - BETA_ONE ** STEP)
    unbiased_two = second_new / (1.0 - BETA_TWO ** STEP)
    weight_new = weight - rate * (unbiased_one / (jnp.sqrt(unbiased_two) + ADAM_EPS) + decay * weight)
    average_new = AVERAGE * average + (1.0 - AVERAGE) * weight_new
    return (weight_new, first_new, second_new, average_new)

def reference(tokens, cotangent, bounds, w_qkv, w_out, w_up, w_down, w_norms, m_qkv, m_out, m_up, m_down, m_norms, v_qkv, v_out, v_up, v_down, v_norms, a_qkv, a_out, a_up, a_down, a_norms):

    def forward(inputs, qkv_w, out_w, up_w, down_w, gain_rows):
        qkv_w = low(qkv_w)
        out_w = low(out_w)
        up_w = low(up_w)
        down_w = low(down_w)
        gain_rows = low(gain_rows)

        def per_sequence(seq_items):
            return sequence(seq_items[0], seq_items[1], qkv_w, out_w, up_w, down_w, gain_rows)
        return lax.map(per_sequence, (inputs, bounds))
    result, pullback = jax.vjp(forward, tokens.astype(jnp.float32), w_qkv, w_out, w_up, w_down, w_norms)
    grads = pullback(cotangent.astype(jnp.float32))
    square = sum((jnp.sum(member * member) for member in grads[1:]))
    grad_norm = jnp.sqrt(square)
    factor = CLIP_NORM / jnp.maximum(grad_norm, CLIP_NORM)
    upd_qkv = adamw(w_qkv, grads[1] * factor, m_qkv, v_qkv, a_qkv, RATE_MAT, WEIGHT_DECAY)
    upd_out = adamw(w_out, grads[2] * factor, m_out, v_out, a_out, RATE_OUT, WEIGHT_DECAY)
    upd_up = adamw(w_up, grads[3] * factor, m_up, v_up, a_up, RATE_MAT, WEIGHT_DECAY)
    upd_down = adamw(w_down, grads[4] * factor, m_down, v_down, a_down, RATE_MAT, WEIGHT_DECAY)
    upd_norms = adamw(w_norms, grads[5] * factor, m_norms, v_norms, a_norms, RATE_VEC, 0.0)
    return (result.astype(jnp.bfloat16), grads[0], grad_norm, upd_qkv[0], upd_out[0], upd_up[0], upd_down[0], upd_norms[0], upd_qkv[1], upd_out[1], upd_up[1], upd_down[1], upd_norms[1], upd_qkv[2], upd_out[2], upd_up[2], upd_down[2], upd_norms[2], upd_qkv[3], upd_out[3], upd_up[3], upd_down[3], upd_norms[3])
```

```python
from functools import partial

import jax
import jax.numpy as jnp
import numpy as np
from jax import lax
from jax.experimental import pallas as pl
from jax.experimental.pallas import tpu as pltpu
from jax.sharding import PartitionSpec as P

DH = 64
STEP = 5

NORM_EPS = 1e-05
CLIP_NORM = 1.0
RATE_MAT = 0.03
RATE_OUT = 0.15
RATE_VEC = 0.3
WEIGHT_DECAY = 0.1
BETA_ONE = 0.5
BETA_TWO = 0.5
ADAM_EPS = 1e-08
AVERAGE = 0.8
MASKED_LOW = -1e30

AXES = ("seq", "dp")
GROUPS = 4
F32 = jnp.float32
BF16 = jnp.bfloat16
NN = (((1,), (0,)), ((), ()))
NT = (((1,), (1,)), ((), ()))


class Layout:
    def __init__(self, n_seq, n_dp):
        self.n_seq, self.n_dp, self.size = n_seq, n_dp, n_seq * n_dp
        self.parts = n_seq // GROUPS
        self.n_bits = self.size.bit_length() - 1
        planes = n_seq == 8 and n_dp == 4
        self.moves = planes
        count = self.size
        self.seq_of = np.zeros(count, np.int32)
        self.blk_of = np.zeros(count, np.int32)
        self.grp_of = np.zeros(count, np.int32)
        self.part_of = np.zeros(count, np.int32)
        self.home = np.zeros(count, np.int32)
        for s in range(n_dp):
            for b in range(n_seq):
                source = b * n_dp + s
                if planes:
                    px, py, pc = b & 1, b >> 2, ((b >> 1) ^ b) & 1
                    dev = s * 8 + px * 4 + py * 2 + pc
                    g, r = px * 2 + py, pc
                else:
                    dev = source
                    low = b % (2 * self.parts)
                    r = min(low, 2 * self.parts - 1 - low)
                    g = 2 * (b // (2 * self.parts)) + int(low >= self.parts)
                self.home[source] = dev
                self.seq_of[dev], self.blk_of[dev] = s, b
                self.grp_of[dev], self.part_of[dev] = g, r
        self.dev_at = {
            (int(self.seq_of[i]), int(self.grp_of[i]), int(self.part_of[i])): i for i in range(count)
        }
        if planes:
            self.gather_a, self.gather_b = (4, 3, 1, 2, 0), (4, 3, 2, 1, 0)
            self.reduce_a, self.reduce_b = (0, 2, 1, 3, 4), (0, 1, 2, 3, 4)
        else:
            down = tuple(reversed(range(self.n_bits)))
            self.gather_a = self.gather_b = down
            self.reduce_a = self.reduce_b = down[::-1]
        blocks = np.zeros((count, GROUPS * self.parts), np.int32)
        lists = []
        for i in range(count):
            s, g, r = int(self.seq_of[i]), int(self.grp_of[i]), int(self.part_of[i])
            for mr in range(self.parts):
                for m in range(GROUPS):
                    blocks[i, mr * GROUPS + m] = self.blk_of[self.dev_at[(s, g ^ m, r ^ mr)]]
            pairs = [
                (qs, ks)
                for qs in range(GROUPS)
                for ks in range(GROUPS * self.parts)
                if blocks[i, ks] <= blocks[i, qs]
            ]
            lists.append(pairs)
        self.n_pairs = len(lists[0])
        self.blocks = blocks
        self.pairs = np.array(lists, np.int32).transpose(0, 2, 1)

    def bit_perm(self, bit):
        return [(i, i ^ (1 << bit)) for i in range(self.size)]

    def group_perm(self, mg, mr):
        out = []
        for i in range(self.size):
            s, g, r = int(self.seq_of[i]), int(self.grp_of[i]), int(self.part_of[i])
            out.append((i, self.dev_at[(s, g ^ mg, r ^ mr)]))
        return out

    def home_perm(self):
        return [(i, int(self.home[i])) for i in range(self.size)]

    def back_perm(self):
        return [(int(self.home[i]), i) for i in range(self.size)]


def layer_norm(values, gain_vec, shift_vec):
    centre = values - jnp.mean(values, axis=-1, keepdims=True)
    spread = jnp.mean(centre * centre, axis=-1, keepdims=True)
    return centre * lax.rsqrt(spread + NORM_EPS) * gain_vec + shift_vec


def adamw(weight, grad, first, second, average, rate, decay):
    first_new = BETA_ONE * first + (1.0 - BETA_ONE) * grad
    second_new = BETA_TWO * second + (1.0 - BETA_TWO) * grad * grad
    unbiased_one = first_new / (1.0 - BETA_ONE**STEP)
    unbiased_two = second_new / (1.0 - BETA_TWO**STEP)
    weight_new = weight - rate * (
        unbiased_one / (jnp.sqrt(unbiased_two) + ADAM_EPS) + decay * weight
    )
    average_new = AVERAGE * average + (1.0 - AVERAGE) * weight_new
    return (weight_new, first_new, second_new, average_new)


def mm(a, b, dims):
    return lax.dot_general(a, b, dims, preferred_element_type=F32)


def doc_of(place, low, high):
    return (place >= low).astype(jnp.int32) + (place >= high).astype(jnp.int32)


def seen(kind, rows, cols, qplace, kplace, low, high):
    qi = lax.broadcasted_iota(jnp.int32, (1, cols), 1) + qplace
    opening = jnp.where(qi >= high, high, jnp.where(qi >= low, low, 0)) - kplace
    ki = lax.broadcasted_iota(jnp.int32, (rows, cols), 0)
    ok = ki >= opening
    if kind == 2:
        ok = ok & (ki <= (qi - kplace))
    return ok


def each_pair(info, pos, lim, n_pairs, n_queries, rows, work):
    low, high = lim[0], lim[1]

    def step(p, carried):
        qs, ks = info[0, p], info[1, p]
        qplace, kplace = pos[qs] * rows, pos[ks] * rows
        same = doc_of(kplace, low, high) == doc_of(qplace + rows - 1, low, high)
        kind = jnp.where(qplace == kplace, 2, jnp.where(same, 0, 1))
        for k in range(3):

            @pl.when(kind == k)
            def _():
                work(k, qs, ks, qplace, kplace)

        return carried

    lax.fori_loop(0, n_pairs, step, 0)


def forward_kernel(parts, nh, n_pairs, info, pos, lim, *refs):
    own = refs[:GROUPS]
    other = refs[GROUPS : GROUPS + parts - 1]
    o_ref, ob_ref, l_ref, q_s, k_s, v_s, m_s, z_s, n_s = refs[GROUPS + parts - 1 :]
    rows = o_ref.shape[3]
    low, high = lim[0], lim[1]
    for j in range(GROUPS):
        q_s[j] = own[j][0]
        v_s[j] = own[j][2]
        for h in range(nh):
            k_s[j, h] = own[j][1, h].T
    for p in range(parts - 1):
        for j in range(GROUPS):
            v_s[(p + 1) * GROUPS + j] = other[p][j, 1]
            for h in range(nh):
                k_s[(p + 1) * GROUPS + j, h] = other[p][j, 0, h].T
    m_s[...] = jnp.full(m_s.shape, MASKED_LOW, F32)
    z_s[...] = jnp.zeros(z_s.shape, F32)
    n_s[...] = jnp.zeros(n_s.shape, F32)

    def work(kind, qs, ks, qplace, kplace):
        for h in range(nh):
            s = mm(k_s[ks, h], q_s[qs, h], NN)
            x = s * s + 1.0
            r = lax.rsqrt(x)
            m = x * r
            if kind > 0:
                m = jnp.where(seen(kind, rows, rows, qplace, kplace, low, high), m, MASKED_LOW)
            m_old = m_s[qs, h]
            m_new = jnp.maximum(m_old, jnp.max(m, axis=0, keepdims=True))
            fade = jnp.exp(m_old - m_new)
            e = jnp.exp(m - (jnp.maximum(m_new, 0.0) if kind > 0 else m_new))
            w = (e * (s * r)).astype(BF16)
            z_s[qs, h] = z_s[qs, h] * fade + jnp.sum(e, axis=0, keepdims=True)
            n_s[qs, h] = n_s[qs, h] * fade + mm(v_s[ks, h], w, NN)
            m_s[qs, h] = m_new

    each_pair(info, pos, lim, n_pairs, GROUPS, rows, work)
    for j in range(GROUPS):
        for h in range(nh):
            z = z_s[j, h]
            o = n_s[j, h] * (1.0 / z)
            o_ref[j, h] = o
            ob_ref[j, h] = o.astype(BF16)
            l_ref[j, h] = m_s[j, h] + jnp.log(z)


def backward_kernel(parts, nh, n_pairs, scale, info, pos, lim, *refs):
    own = refs[:GROUPS]
    other = refs[GROUPS : GROUPS + parts - 1]
    refs = refs[GROUPS + parts - 1 :]
    dob = refs[:GROUPS]
    o_ref, l_ref, dq_ref, dkv_ref, q_s, kt_s, k_s, v_s, do_s, d_s, dq_s, dk_s, dv_s = refs[GROUPS:]
    rows = o_ref.shape[3]
    low, high = lim[0], lim[1]
    for j in range(GROUPS):
        q_s[j] = own[j][0]
        kt_s[j] = own[j][1]
        do_s[j] = dob[j][...]
        for h in range(nh):
            k_s[j, h] = own[j][1, h].T
            v_s[j, h] = own[j][2, h].T
            d_s[j, h] = jnp.sum(dob[j][h].astype(F32) * o_ref[j, h], axis=0, keepdims=True)
    for p in range(parts - 1):
        for j in range(GROUPS):
            kt_s[(p + 1) * GROUPS + j] = other[p][j, 0]
            for h in range(nh):
                k_s[(p + 1) * GROUPS + j, h] = other[p][j, 0, h].T
                v_s[(p + 1) * GROUPS + j, h] = other[p][j, 1, h].T
    dq_s[...] = jnp.zeros(dq_s.shape, F32)
    dk_s[...] = jnp.zeros(dk_s.shape, F32)
    dv_s[...] = jnp.zeros(dv_s.shape, F32)

    def work(kind, qs, ks, qplace, kplace):
        for h in range(nh):
            q = q_s[qs, h]
            do = do_s[qs, h]
            s = mm(k_s[ks, h], q, NN)
            gw = mm(v_s[ks, h], do, NN)
            x = s * s + 1.0
            r = lax.rsqrt(x)
            prob = jnp.exp(x * r - l_ref[qs, h])
            if kind > 0:
                prob = jnp.where(seen(kind, rows, rows, qplace, kplace, low, high), prob, 0.0)
            t = s * r
            gs = (gw * (r * r * r + t * t) - t * d_s[qs, h]) * prob
            gs_low = gs.astype(BF16)
            pt_low = (prob * t).astype(BF16)
            dv_s[ks, h] += mm(do, pt_low, NT)
            dk_s[ks, h] += mm(q, gs_low, NT)
            dq_s[qs, h] += mm(kt_s[ks, h], gs_low, NN)

    each_pair(info, pos, lim, n_pairs, GROUPS, rows, work)
    for j in range(GROUPS):
        for h in range(nh):
            dq_ref[j, h] = (dq_s[j, h] * scale).astype(BF16)
    for j in range(GROUPS * parts):
        for h in range(nh):
            dkv_ref[j, 0, h] = dk_s[j, h].astype(dkv_ref.dtype)
            dkv_ref[j, 1, h] = dv_s[j, h].astype(dkv_ref.dtype)


VMEM_SPEC = pl.BlockSpec(memory_space=pltpu.VMEM)
SMEM_SPEC = pl.BlockSpec(memory_space=pltpu.SMEM)
PARAMS_OF = pltpu.CompilerParams(vmem_limit_bytes=56 * 2**20)


def attend(lay, tables, own, other):
    info, pos, lim = tables
    nh, rows = own[0].shape[1], own[0].shape[3]
    slots = GROUPS * lay.parts
    shape = jax.ShapeDtypeStruct
    return pl.pallas_call(
        partial(forward_kernel, lay.parts, nh, lay.n_pairs),
        out_shape=(
            shape((GROUPS, nh, DH, rows), F32),
            shape((GROUPS, nh, DH, rows), BF16),
            shape((GROUPS, nh, 1, rows), F32),
        ),
        in_specs=[SMEM_SPEC] * 3 + [VMEM_SPEC] * (len(own) + len(other)),
        out_specs=(VMEM_SPEC,) * 3,
        scratch_shapes=[
            pltpu.VMEM((GROUPS, nh, DH, rows), BF16),
            pltpu.VMEM((slots, nh, rows, DH), BF16),
            pltpu.VMEM((slots, nh, DH, rows), BF16),
            pltpu.VMEM((GROUPS, nh, 1, rows), F32),
            pltpu.VMEM((GROUPS, nh, 1, rows), F32),
            pltpu.VMEM((GROUPS, nh, DH, rows), F32),
        ],
        compiler_params=PARAMS_OF,
        cost_estimate=pl.CostEstimate(
            flops=4 * lay.n_pairs * nh * rows * rows * DH,
            bytes_accessed=2 * (slots + GROUPS) * 3 * nh * DH * rows,
            transcendentals=2 * lay.n_pairs * nh * rows * rows,
        ),
        name="attend",
    )(info, pos, lim, *own, *other)


def attend_back(lay, tables, own, other, dob, o, lse):
    info, pos, lim = tables
    nh, rows = own[0].shape[1], own[0].shape[3]
    slots = GROUPS * lay.parts
    shape = jax.ShapeDtypeStruct
    return pl.pallas_call(
        partial(backward_kernel, lay.parts, nh, lay.n_pairs, DH**-0.5),
        out_shape=(
            shape((GROUPS, nh, DH, rows), BF16),
            shape((slots, 2, nh, DH, rows), BF16 if lay.parts > 1 else F32),
        ),
        in_specs=[SMEM_SPEC] * 3 + [VMEM_SPEC] * (len(own) + len(other) + len(dob) + 2),
        out_specs=(VMEM_SPEC,) * 2,
        scratch_shapes=[
            pltpu.VMEM((GROUPS, nh, DH, rows), BF16),
            pltpu.VMEM((slots, nh, DH, rows), BF16),
            pltpu.VMEM((slots, nh, rows, DH), BF16),
            pltpu.VMEM((slots, nh, rows, DH), BF16),
            pltpu.VMEM((GROUPS, nh, DH, rows), BF16),
            pltpu.VMEM((GROUPS, nh, 1, rows), F32),
            pltpu.VMEM((GROUPS, nh, DH, rows), F32),
            pltpu.VMEM((slots, nh, DH, rows), F32),
            pltpu.VMEM((slots, nh, DH, rows), F32),
        ],
        compiler_params=PARAMS_OF,
        cost_estimate=pl.CostEstimate(
            flops=10 * lay.n_pairs * nh * rows * rows * DH,
            bytes_accessed=2 * (slots + GROUPS) * 5 * nh * DH * rows,
            transcendentals=2 * lay.n_pairs * nh * rows * rows,
        ),
        name="attend_back",
    )(info, pos, lim, *own, *other, *dob, o, lse)


def gather_rows(lay, index, order, shard):
    held = shard[None]
    for bit in order:
        came = lax.ppermute(held, AXES, lay.bit_perm(bit))
        upper = ((index >> bit) & 1) == 1
        held = jnp.where(upper, jnp.stack([came, held]), jnp.stack([held, came]))
    n = len(order)
    axis_of = {bit: n - 1 - k for k, bit in enumerate(order)}
    bits = tuple(axis_of[b] for b in reversed(range(n)))
    held = held.transpose(bits + tuple(range(n, held.ndim)))
    return held.reshape((lay.size * shard.shape[0],) + shard.shape[1:])


def scatter_rows(lay, index, order, full):
    n = lay.n_bits
    rows = full.shape[0] // lay.size
    held = full.reshape((2,) * n + (rows,) + full.shape[1:])
    left = list(reversed(range(n)))
    for bit in order:
        axis = left.index(bit)
        left.pop(axis)
        mine = (index >> bit) & 1
        keep = lax.dynamic_index_in_dim(held, mine, axis, keepdims=False)
        give = lax.dynamic_index_in_dim(held, 1 - mine, axis, keepdims=False)
        came = lax.ppermute(give.astype(BF16), AXES, lay.bit_perm(bit))
        held = keep + came.astype(F32)
    return held


def unxor(items, mask):
    for bit in range((len(items) - 1).bit_length()):
        on = ((mask >> bit) & 1) == 1
        items = [jnp.where(on, items[k ^ (1 << bit)], items[k]) for k in range(len(items))]
    return items


def per_device(
    lay,
    tokens,
    cotangent,
    bounds,
    w_qkv,
    w_out,
    w_up,
    w_down,
    w_norms,
    m_qkv,
    m_out,
    m_up,
    m_down,
    m_norms,
    v_qkv,
    v_out,
    v_up,
    v_down,
    v_norms,
    a_qkv,
    a_out,
    a_up,
    a_down,
    a_norms,
):
    rows, width = tokens.shape[1], tokens.shape[2]
    n_heads = width // DH
    nh = n_heads // GROUPS
    ff = w_up.shape[1]
    index = lax.axis_index("seq") * lay.n_dp + lax.axis_index("dp")
    group = jnp.asarray(lay.grp_of)[index]
    blocks = jnp.asarray(lay.blocks)[index]
    pairs = jnp.asarray(lay.pairs)[index]

    if lay.moves:
        to_home = partial(lax.ppermute, axis_name=AXES, perm=lay.home_perm())
        to_owner = partial(lax.ppermute, axis_name=AXES, perm=lay.back_perm())
    else:
        to_home = to_owner = lambda v: v
    tokens_here = to_home(tokens[0])
    limits = to_home(bounds[0])
    tables = (pairs, blocks, limits)

    pad = jnp.zeros((w_qkv.shape[0], 128 - w_norms.shape[0]), BF16)
    low_qkv = w_qkv.astype(BF16)
    half = (3 * width // 2) // 128 * 128
    shard_a = low_qkv[:, :half]
    shard_b = jnp.concatenate([low_qkv[:, half:], w_norms.T.astype(BF16), pad], axis=1)
    full_a = gather_rows(lay, index, lay.gather_a, shard_a)
    full_b = gather_rows(lay, index, lay.gather_b, shard_b)
    qkv_full = jnp.concatenate([full_a, full_b[:, : 3 * width - half]], axis=1)
    gain_rows = full_b[:, 3 * width - half : 3 * width - half + 4].astype(F32).T
    full_c = gather_rows(
        lay, index, lay.gather_a, jnp.concatenate([w_out.astype(BF16), w_up.astype(BF16)], axis=1)
    )
    out_full, up_full = full_c[:, :width], full_c[:, width:]
    down_full = gather_rows(lay, index, lay.gather_b, w_down.astype(BF16))

    inputs = tokens_here.astype(F32)
    normed, first_pull = jax.vjp(layer_norm, inputs, gain_rows[0], gain_rows[1])
    normed_low = normed.astype(BF16)
    mixed = lax.dot_general(
        qkv_full, normed_low, (((0,), (1,)), ((), ())), preferred_element_type=F32
    ).astype(BF16)
    mixed = mixed.reshape(3, GROUPS, nh, DH, rows)
    mixed = jnp.concatenate([mixed[:1] * jnp.asarray(DH**-0.5, BF16), mixed[1:]], axis=0)

    def to_groups(items):
        return [items[0]] + [
            lax.ppermute(items[m], AXES, lay.group_perm(m, 0)) for m in range(1, GROUPS)
        ]

    def for_group(array, axis, m):
        return lax.dynamic_index_in_dim(array, group ^ m, axis, keepdims=False)

    own = to_groups([for_group(mixed, 1, m) for m in range(GROUPS)])
    kv_own = jnp.stack([piece[1:] for piece in own])
    other = [lax.ppermute(kv_own, AXES, lay.group_perm(0, mr)) for mr in range(1, lay.parts)]
    attended, att_pieces, lse = attend(lay, tables, own, other)
    att_back = to_groups([att_pieces[m] for m in range(GROUPS)])
    att_low = jnp.stack(unxor(att_back, group)).reshape(width, rows)

    branch = lax.dot_general(
        att_low, out_full, (((0,), (0,)), ((), ())), preferred_element_type=F32
    )
    resid_sum = inputs + branch
    hidden_norm, second_pull = jax.vjp(layer_norm, resid_sum, gain_rows[2], gain_rows[3])
    hidden_low = hidden_norm.astype(BF16)
    pre_act = jnp.dot(hidden_low, up_full, preferred_element_type=F32)
    activated, gelu_pull = jax.vjp(partial(jax.nn.gelu, approximate=True), pre_act)
    act_low = activated.astype(BF16)
    result = resid_sum + jnp.dot(act_low, down_full, preferred_element_type=F32)
    layer_out = to_owner(result.astype(BF16))[None]
    grad_out = to_home(cotangent[0])
    grad_down = jnp.einsum("tf,td->fd", act_low, grad_out, preferred_element_type=F32)
    grad_act = jnp.einsum("td,fd->tf", grad_out, down_full, preferred_element_type=F32)
    grad_pre = gelu_pull(grad_act)[0].astype(BF16)
    grad_up = jnp.einsum("td,tf->df", hidden_low, grad_pre, preferred_element_type=F32)
    grad_hidden = jnp.einsum("tf,df->td", grad_pre, up_full, preferred_element_type=F32)
    back_resid, grad_gain2, grad_shift2 = second_pull(grad_hidden)
    grad_resid = grad_out.astype(F32) + back_resid
    grad_branch = grad_resid.astype(BF16)
    grad_wout = lax.dot_general(
        att_low, grad_branch, (((1,), (0,)), ((), ())), preferred_element_type=F32
    )
    dob = lax.dot_general(
        out_full, grad_branch, (((1,), (1,)), ((), ())), preferred_element_type=F32
    ).astype(BF16)
    dob = dob.reshape(GROUPS, nh, DH, rows)
    dob_pieces = to_groups([for_group(dob, 0, m) for m in range(GROUPS)])
    dq, dkv = attend_back(lay, tables, own, other, dob_pieces, attended, lse)
    dkv_sum = dkv[:GROUPS].astype(F32)
    for mr in range(1, lay.parts):
        dkv_sum = dkv_sum + lax.ppermute(
            dkv[mr * GROUPS : (mr + 1) * GROUPS], AXES, lay.group_perm(0, mr)
        ).astype(F32)
    dkv_low = dkv_sum.astype(BF16)
    mixed_pieces = [
        jnp.concatenate([dq[m][None], dkv_low[m]], axis=0) for m in range(GROUPS)
    ]
    mixed_grad = jnp.stack(unxor(to_groups(mixed_pieces), group), axis=1).reshape(3 * width, rows)
    grad_wqkv = lax.dot_general(
        normed_low, mixed_grad, (((0,), (1,)), ((), ())), preferred_element_type=F32
    )
    grad_normed = lax.dot_general(
        mixed_grad, qkv_full, (((0,), (1,)), ((), ())), preferred_element_type=F32
    )
    back_input, grad_gain1, grad_shift1 = first_pull(grad_normed)
    input_grad = to_owner((grad_resid + back_input).astype(BF16)).astype(F32)[None]
    grad_vec = jnp.stack([grad_gain1, grad_shift1, grad_gain2, grad_shift2]).T

    summed_down = scatter_rows(lay, index, lay.reduce_b, grad_down)
    summed_c = scatter_rows(
        lay, index, lay.reduce_a, jnp.concatenate([grad_wout, grad_up], axis=1)
    )
    summed_a = scatter_rows(lay, index, lay.reduce_a, grad_wqkv[:, :half])
    summed_b = scatter_rows(
        lay,
        index,
        lay.reduce_b,
        jnp.concatenate([grad_wqkv[:, half:], grad_vec, jnp.zeros((width, 124), F32)], axis=1),
    )
    summed_qkv = jnp.concatenate([summed_a, summed_b[:, : 3 * width - half]], axis=1)
    summed_out, summed_up = summed_c[:, :width], summed_c[:, width:]
    summed_norms = summed_b[:, 3 * width - half : 3 * width - half + 4].T

    summed = (summed_qkv, summed_out, summed_up, summed_down, summed_norms)
    square = sum((jnp.sum(member * member) for member in summed))
    for bit in range(lay.n_bits):
        square = square + lax.ppermute(square, AXES, lay.bit_perm(bit))
    grad_norm = jnp.sqrt(square)
    factor = CLIP_NORM / jnp.maximum(grad_norm, CLIP_NORM)
    upd_qkv = adamw(w_qkv, summed_qkv * factor, m_qkv, v_qkv, a_qkv, RATE_MAT, WEIGHT_DECAY)
    upd_out = adamw(w_out, summed_out * factor, m_out, v_out, a_out, RATE_OUT, WEIGHT_DECAY)
    upd_up = adamw(w_up, summed_up * factor, m_up, v_up, a_up, RATE_MAT, WEIGHT_DECAY)
    upd_down = adamw(w_down, summed_down * factor, m_down, v_down, a_down, RATE_MAT, WEIGHT_DECAY)
    upd_norms = adamw(w_norms, summed_norms * factor, m_norms, v_norms, a_norms, RATE_VEC, 0.0)
    updates = (upd_qkv, upd_out, upd_up, upd_down, upd_norms)
    return (layer_out, input_grad, grad_norm) + tuple(u[k] for k in range(4) for u in updates)


def solution(mesh):
    lay = Layout(mesh.shape["seq"], mesh.shape["dp"])
    rows = P(AXES, None)
    vecs = P(None, AXES)
    state = (rows, rows, rows, rows, vecs)
    block = P("dp", "seq", None)
    return jax.shard_map(
        partial(per_device, lay),
        mesh=mesh,
        in_specs=(block, block, P("dp", None)) + state * 4,
        out_specs=(block, block, P()) + state * 4,
        check_vma=False,
    )
```

```python
from functools import partial

import jax
import jax.numpy as jnp
import numpy as np
from jax import lax
from jax.experimental import pallas as pl
from jax.experimental.pallas import tpu as pltpu
from jax.sharding import PartitionSpec as P

DH = 64
STEP = 5

NORM_EPS = 1e-05
CLIP_NORM = 1.0
RATE_MAT = 0.03
RATE_OUT = 0.15
RATE_VEC = 0.3
WEIGHT_DECAY = 0.1
BETA_ONE = 0.5
BETA_TWO = 0.5
ADAM_EPS = 1e-08
AVERAGE = 0.8
MASKED_LOW = -1e30

AXES = ("seq", "dp")
GROUPS = 4
F32 = jnp.float32
BF16 = jnp.bfloat16
NN = (((1,), (0,)), ((), ()))
NT = (((1,), (1,)), ((), ()))


class Layout:
    def __init__(self, n_seq, n_dp):
        self.n_seq, self.n_dp, self.size = n_seq, n_dp, n_seq * n_dp
        self.parts = n_seq // GROUPS
        self.n_bits = self.size.bit_length() - 1
        planes = n_seq == 8 and n_dp == 4
        self.moves = planes
        count = self.size
        self.seq_of = np.zeros(count, np.int32)
        self.blk_of = np.zeros(count, np.int32)
        self.grp_of = np.zeros(count, np.int32)
        self.part_of = np.zeros(count, np.int32)
        self.home = np.zeros(count, np.int32)
        for s in range(n_dp):
            for b in range(n_seq):
                source = b * n_dp + s
                if planes:
                    px, pz, pc = b & 1, (b >> 1) & 1, ((b >> 2) ^ (b >> 1) ^ b) & 1
                    dev = (s & 1) * 16 + pz * 8 + px * 4 + (s >> 1) * 2 + pc
                    g, r = px * 2 + pz, pc
                else:
                    dev = source
                    low = b % (2 * self.parts)
                    r = min(low, 2 * self.parts - 1 - low)
                    g = 2 * (b // (2 * self.parts)) + int(low >= self.parts)
                self.home[source] = dev
                self.seq_of[dev], self.blk_of[dev] = s, b
                self.grp_of[dev], self.part_of[dev] = g, r
        self.dev_at = {
            (int(self.seq_of[i]), int(self.grp_of[i]), int(self.part_of[i])): i for i in range(count)
        }
        if planes:
            self.core, self.near, self.far = (0,), ((2,), (1,)), (3, 4)
        else:
            self.core, self.near, self.far = (0,), ((2, 1), (3,)), tuple(range(4, self.n_bits))
        blocks = np.zeros((count, GROUPS * self.parts), np.int32)
        lists = []
        for i in range(count):
            s, g, r = int(self.seq_of[i]), int(self.grp_of[i]), int(self.part_of[i])
            for mr in range(self.parts):
                for m in range(GROUPS):
                    blocks[i, mr * GROUPS + m] = self.blk_of[self.dev_at[(s, g ^ m, r ^ mr)]]
            pairs = [
                (qs, ks)
                for qs in range(GROUPS)
                for ks in range(GROUPS * self.parts)
                if blocks[i, ks] <= blocks[i, qs]
            ]
            lists.append(pairs)
        self.n_pairs = len(lists[0])
        self.blocks = blocks
        self.pairs = np.array(lists, np.int32).transpose(0, 2, 1)

    def bit_perm(self, bit):
        return [(i, i ^ (1 << bit)) for i in range(self.size)]

    def group_perm(self, mg, mr):
        out = []
        for i in range(self.size):
            s, g, r = int(self.seq_of[i]), int(self.grp_of[i]), int(self.part_of[i])
            out.append((i, self.dev_at[(s, g ^ mg, r ^ mr)]))
        return out

    def home_perm(self):
        return [(i, int(self.home[i])) for i in range(self.size)]

    def back_perm(self):
        return [(int(self.home[i]), i) for i in range(self.size)]


def layer_norm(values, gain_vec, shift_vec):
    centre = values - jnp.mean(values, axis=-1, keepdims=True)
    spread = jnp.mean(centre * centre, axis=-1, keepdims=True)
    return centre * lax.rsqrt(spread + NORM_EPS) * gain_vec + shift_vec


def adamw(weight, grad, first, second, average, rate, decay):
    first_new = BETA_ONE * first + (1.0 - BETA_ONE) * grad
    second_new = BETA_TWO * second + (1.0 - BETA_TWO) * grad * grad
    unbiased_one = first_new / (1.0 - BETA_ONE**STEP)
    unbiased_two = second_new / (1.0 - BETA_TWO**STEP)
    weight_new = weight - rate * (
        unbiased_one / (jnp.sqrt(unbiased_two) + ADAM_EPS) + decay * weight
    )
    average_new = AVERAGE * average + (1.0 - AVERAGE) * weight_new
    return (weight_new, first_new, second_new, average_new)


def mm(a, b, dims):
    return lax.dot_general(a, b, dims, preferred_element_type=F32)


def doc_of(place, low, high):
    return (place >= low).astype(jnp.int32) + (place >= high).astype(jnp.int32)


def seen(kind, rows, cols, qplace, kplace, low, high):
    qi = lax.broadcasted_iota(jnp.int32, (1, cols), 1) + qplace
    opening = jnp.where(qi >= high, high, jnp.where(qi >= low, low, 0)) - kplace
    ki = lax.broadcasted_iota(jnp.int32, (rows, cols), 0)
    ok = ki >= opening
    if kind == 2:
        ok = ok & (ki <= (qi - kplace))
    return ok


def each_pair(info, pos, lim, n_pairs, n_queries, rows, work):
    low, high = lim[0], lim[1]

    def step(p, carried):
        qs, ks = info[0, p], info[1, p]
        qplace, kplace = pos[qs] * rows, pos[ks] * rows
        same = doc_of(kplace, low, high) == doc_of(qplace + rows - 1, low, high)
        kind = jnp.where(qplace == kplace, 2, jnp.where(same, 0, 1))
        for k in range(3):

            @pl.when(kind == k)
            def _():
                work(k, qs, ks, qplace, kplace)

        return carried

    lax.fori_loop(0, n_pairs, step, 0)


def forward_kernel(parts, nh, n_pairs, info, pos, lim, *refs):
    own = refs[:GROUPS]
    other = refs[GROUPS : GROUPS + parts - 1]
    o_ref, ob_ref, l_ref, q_s, k_s, v_s, m_s, z_s, n_s = refs[GROUPS + parts - 1 :]
    rows = o_ref.shape[3]
    low, high = lim[0], lim[1]
    for j in range(GROUPS):
        q_s[j] = own[j][0]
        v_s[j] = own[j][2]
        for h in range(nh):
            k_s[j, h] = own[j][1, h].T
    for p in range(parts - 1):
        for j in range(GROUPS):
            v_s[(p + 1) * GROUPS + j] = other[p][j, 1]
            for h in range(nh):
                k_s[(p + 1) * GROUPS + j, h] = other[p][j, 0, h].T
    m_s[...] = jnp.full(m_s.shape, MASKED_LOW, F32)
    z_s[...] = jnp.zeros(z_s.shape, F32)
    n_s[...] = jnp.zeros(n_s.shape, F32)

    def work(kind, qs, ks, qplace, kplace):
        for h in range(nh):
            s = mm(k_s[ks, h], q_s[qs, h], NN)
            x = s * s + 1.0
            r = lax.rsqrt(x)
            m = x * r
            if kind > 0:
                m = jnp.where(seen(kind, rows, rows, qplace, kplace, low, high), m, MASKED_LOW)
            m_old = m_s[qs, h]
            m_new = jnp.maximum(m_old, jnp.max(m, axis=0, keepdims=True))
            fade = jnp.exp(m_old - m_new)
            e = jnp.exp(m - (jnp.maximum(m_new, 0.0) if kind > 0 else m_new))
            w = (e * (s * r)).astype(BF16)
            z_s[qs, h] = z_s[qs, h] * fade + jnp.sum(e, axis=0, keepdims=True)
            n_s[qs, h] = n_s[qs, h] * fade + mm(v_s[ks, h], w, NN)
            m_s[qs, h] = m_new

    each_pair(info, pos, lim, n_pairs, GROUPS, rows, work)
    for j in range(GROUPS):
        for h in range(nh):
            z = z_s[j, h]
            o = n_s[j, h] * (1.0 / z)
            o_ref[j, h] = o
            ob_ref[j, h] = o.astype(BF16)
            l_ref[j, h] = m_s[j, h] + jnp.log(z)


def backward_kernel(parts, nh, n_pairs, scale, info, pos, lim, *refs):
    own = refs[:GROUPS]
    other = refs[GROUPS : GROUPS + parts - 1]
    refs = refs[GROUPS + parts - 1 :]
    dob = refs[:GROUPS]
    o_ref, l_ref, dq_ref, dkv_ref, q_s, kt_s, k_s, v_s, do_s, d_s, dq_s, dk_s, dv_s = refs[GROUPS:]
    rows = o_ref.shape[3]
    low, high = lim[0], lim[1]
    for j in range(GROUPS):
        q_s[j] = own[j][0]
        kt_s[j] = own[j][1]
        do_s[j] = dob[j][...]
        for h in range(nh):
            k_s[j, h] = own[j][1, h].T
            v_s[j, h] = own[j][2, h].T
            d_s[j, h] = jnp.sum(dob[j][h].astype(F32) * o_ref[j, h], axis=0, keepdims=True)
    for p in range(parts - 1):
        for j in range(GROUPS):
            kt_s[(p + 1) * GROUPS + j] = other[p][j, 0]
            for h in range(nh):
                k_s[(p + 1) * GROUPS + j, h] = other[p][j, 0, h].T
                v_s[(p + 1) * GROUPS + j, h] = other[p][j, 1, h].T
    dq_s[...] = jnp.zeros(dq_s.shape, F32)
    dk_s[...] = jnp.zeros(dk_s.shape, F32)
    dv_s[...] = jnp.zeros(dv_s.shape, F32)

    def work(kind, qs, ks, qplace, kplace):
        for h in range(nh):
            q = q_s[qs, h]
            do = do_s[qs, h]
            s = mm(k_s[ks, h], q, NN)
            gw = mm(v_s[ks, h], do, NN)
            x = s * s + 1.0
            r = lax.rsqrt(x)
            prob = jnp.exp(x * r - l_ref[qs, h])
            if kind > 0:
                prob = jnp.where(seen(kind, rows, rows, qplace, kplace, low, high), prob, 0.0)
            t = s * r
            gs = (gw * (r * r * r + t * t) - t * d_s[qs, h]) * prob
            gs_low = gs.astype(BF16)
            pt_low = (prob * t).astype(BF16)
            dv_s[ks, h] += mm(do, pt_low, NT)
            dk_s[ks, h] += mm(q, gs_low, NT)
            dq_s[qs, h] += mm(kt_s[ks, h], gs_low, NN)

    each_pair(info, pos, lim, n_pairs, GROUPS, rows, work)
    for j in range(GROUPS):
        for h in range(nh):
            dq_ref[j, h] = (dq_s[j, h] * scale).astype(BF16)
    for j in range(GROUPS * parts):
        for h in range(nh):
            dkv_ref[j, 0, h] = dk_s[j, h].astype(dkv_ref.dtype)
            dkv_ref[j, 1, h] = dv_s[j, h].astype(dkv_ref.dtype)


VMEM_SPEC = pl.BlockSpec(memory_space=pltpu.VMEM)
SMEM_SPEC = pl.BlockSpec(memory_space=pltpu.SMEM)
PARAMS_OF = pltpu.CompilerParams(vmem_limit_bytes=56 * 2**20)


def attend(lay, tables, own, other):
    info, pos, lim = tables
    nh, rows = own[0].shape[1], own[0].shape[3]
    slots = GROUPS * lay.parts
    shape = jax.ShapeDtypeStruct
    return pl.pallas_call(
        partial(forward_kernel, lay.parts, nh, lay.n_pairs),
        out_shape=(
            shape((GROUPS, nh, DH, rows), F32),
            shape((GROUPS, nh, DH, rows), BF16),
            shape((GROUPS, nh, 1, rows), F32),
        ),
        in_specs=[SMEM_SPEC] * 3 + [VMEM_SPEC] * (len(own) + len(other)),
        out_specs=(VMEM_SPEC,) * 3,
        scratch_shapes=[
            pltpu.VMEM((GROUPS, nh, DH, rows), BF16),
            pltpu.VMEM((slots, nh, rows, DH), BF16),
            pltpu.VMEM((slots, nh, DH, rows), BF16),
            pltpu.VMEM((GROUPS, nh, 1, rows), F32),
            pltpu.VMEM((GROUPS, nh, 1, rows), F32),
            pltpu.VMEM((GROUPS, nh, DH, rows), F32),
        ],
        compiler_params=PARAMS_OF,
        cost_estimate=pl.CostEstimate(
            flops=4 * lay.n_pairs * nh * rows * rows * DH,
            bytes_accessed=2 * (slots + GROUPS) * 3 * nh * DH * rows,
            transcendentals=2 * lay.n_pairs * nh * rows * rows,
        ),
        name="attend",
    )(info, pos, lim, *own, *other)


def attend_back(lay, tables, own, other, dob, o, lse):
    info, pos, lim = tables
    nh, rows = own[0].shape[1], own[0].shape[3]
    slots = GROUPS * lay.parts
    shape = jax.ShapeDtypeStruct
    return pl.pallas_call(
        partial(backward_kernel, lay.parts, nh, lay.n_pairs, DH**-0.5),
        out_shape=(
            shape((GROUPS, nh, DH, rows), BF16),
            shape((slots, 2, nh, DH, rows), BF16 if lay.parts > 1 else F32),
        ),
        in_specs=[SMEM_SPEC] * 3 + [VMEM_SPEC] * (len(own) + len(other) + len(dob) + 2),
        out_specs=(VMEM_SPEC,) * 2,
        scratch_shapes=[
            pltpu.VMEM((GROUPS, nh, DH, rows), BF16),
            pltpu.VMEM((slots, nh, DH, rows), BF16),
            pltpu.VMEM((slots, nh, rows, DH), BF16),
            pltpu.VMEM((slots, nh, rows, DH), BF16),
            pltpu.VMEM((GROUPS, nh, DH, rows), BF16),
            pltpu.VMEM((GROUPS, nh, 1, rows), F32),
            pltpu.VMEM((GROUPS, nh, DH, rows), F32),
            pltpu.VMEM((slots, nh, DH, rows), F32),
            pltpu.VMEM((slots, nh, DH, rows), F32),
        ],
        compiler_params=PARAMS_OF,
        cost_estimate=pl.CostEstimate(
            flops=10 * lay.n_pairs * nh * rows * rows * DH,
            bytes_accessed=2 * (slots + GROUPS) * 5 * nh * DH * rows,
            transcendentals=2 * lay.n_pairs * nh * rows * rows,
        ),
        name="attend_back",
    )(info, pos, lim, *own, *other, *dob, o, lse)


def after(value, *others):
    return lax.optimization_barrier((value,) + others)[0]


def join(*values):
    return lax.optimization_barrier(values)


class Gather:
    def __init__(self, lay, index, shard):
        self.lay, self.index, self.rows, self.held = lay, index, shard.shape[0], shard
        self.bits, self.came, self.bit = (), None, None

    def start(self, bit, *others):
        if others:
            self.held = after(self.held, *others)
        self.bit = bit
        self.came = lax.ppermute(self.held, AXES, self.lay.bit_perm(bit))

    def finish(self, *others):
        came = after(self.came, *others) if others else self.came
        upper = ((self.index >> self.bit) & 1) == 1
        mine = self.held
        self.held = jnp.where(upper, jnp.stack([came, mine]), jnp.stack([mine, came]))
        self.bits = (self.bit,) + self.bits
        return self.held

    def step(self, bit, *others):
        self.start(bit, *others)
        return self.finish()

    def columns(self, start, stop):
        part = Gather(self.lay, self.index, self.held[..., start:stop])
        part.rows, part.bits = self.rows, self.bits
        return part

    def result(self):
        axes = tuple(self.bits.index(b) for b in reversed(range(self.lay.n_bits)))
        held = self.held.transpose(axes + tuple(range(len(axes), self.held.ndim)))
        return held.reshape((self.lay.size * self.rows,) + self.held.shape[len(axes) + 1 :])


class Scatter:
    def __init__(self, lay, index, arrays, left=None):
        self.lay, self.index = lay, index
        self.left = list(reversed(range(lay.n_bits))) if left is None else list(left)
        if left is None:
            arrays = [
                a.reshape((2,) * lay.n_bits + (a.shape[0] // lay.size,) + a.shape[1:])
                for a in arrays
            ]
        self.held, self.came, self.keep = list(arrays), None, None

    def start(self, bit, *others):
        if others:
            self.held = [after(h, *others) for h in self.held]
        axis = self.left.index(bit)
        self.left.pop(axis)
        mine = (self.index >> bit) & 1
        self.keep = [lax.dynamic_index_in_dim(h, mine, axis, keepdims=False) for h in self.held]
        give = [
            lax.dynamic_index_in_dim(h, 1 - mine, axis, keepdims=False).astype(BF16)
            for h in self.held
        ]
        give = jnp.concatenate(give, axis=-1) if len(give) > 1 else give[0]
        self.came = lax.ppermute(give, AXES, self.lay.bit_perm(bit))

    def finish(self, *others):
        came = after(self.came, *others) if others else self.came
        at, held = 0, []
        for keep in self.keep:
            held.append(keep + came[..., at : at + keep.shape[-1]].astype(F32))
            at += keep.shape[-1]
        self.held = held
        return held

    def step(self, bit, *others):
        self.start(bit, *others)
        return self.finish()


def unxor(items, mask):
    for bit in range((len(items) - 1).bit_length()):
        on = ((mask >> bit) & 1) == 1
        items = [jnp.where(on, items[k ^ (1 << bit)], items[k]) for k in range(len(items))]
    return items


def per_device(
    lay,
    tokens,
    cotangent,
    bounds,
    w_qkv,
    w_out,
    w_up,
    w_down,
    w_norms,
    m_qkv,
    m_out,
    m_up,
    m_down,
    m_norms,
    v_qkv,
    v_out,
    v_up,
    v_down,
    v_norms,
    a_qkv,
    a_out,
    a_up,
    a_down,
    a_norms,
):
    rows, width = tokens.shape[1], tokens.shape[2]
    n_heads = width // DH
    nh = n_heads // GROUPS
    index = lax.axis_index("seq") * lay.n_dp + lax.axis_index("dp")
    group = jnp.asarray(lay.grp_of)[index]
    blocks = jnp.asarray(lay.blocks)[index]
    pairs = jnp.asarray(lay.pairs)[index]

    if lay.moves:
        to_home = partial(lax.ppermute, axis_name=AXES, perm=lay.home_perm())
        to_owner = partial(lax.ppermute, axis_name=AXES, perm=lay.back_perm())
    else:
        to_home = to_owner = lambda v: v

    def to_groups(items):
        return [items[0]] + [
            lax.ppermute(items[m], AXES, lay.group_perm(m, 0)) for m in range(1, GROUPS)
        ]

    def for_group(array, axis, m):
        return lax.dynamic_index_in_dim(array, group ^ m, axis, keepdims=False)

    def across(array, mr):
        return lax.ppermute(array, AXES, lay.group_perm(0, mr))

    def by_head(shard):
        cut = shard.reshape(-1, 3, GROUPS, nh, DH).transpose(0, 3, 1, 2, 4)
        return cut.reshape(shard.shape)

    def from_by_head(shard):
        cut = shard.reshape(-1, nh, 3, GROUPS, DH).transpose(0, 2, 3, 1, 4)
        return cut.reshape(shard.shape)

    far, core = lay.far, lay.core
    near_a = lay.near[0] + lay.near[1]
    near_b = lay.near[1] + lay.near[0]

    pad = jnp.zeros((w_qkv.shape[0], 128 - w_norms.shape[0]), BF16)
    low_qkv = by_head(w_qkv.astype(BF16))
    half = (3 * width // 2) // 128 * 128
    gather = Gather(
        lay, index, jnp.concatenate([low_qkv, w_norms.T.astype(BF16), pad], axis=1)
    )
    gather.step(far[-1])
    tokens_here = to_home(after(tokens[0], gather.held))
    limits = to_home(bounds[0])
    tables = (pairs, blocks, limits)
    for bit in reversed(far[:-1]):
        gather.step(bit)
    gather_a, gather_b = gather.columns(0, half), gather.columns(half, 3 * width + 128)
    for bit_a, bit_b in zip(near_a, near_b):
        gather_a.start(bit_a)
        gather_b.start(bit_b)
        gather_a.finish()
        gather_b.finish()
    for bit in core:
        gather_a.start(bit)
        gather_b.start(bit)
        gather_a.finish()
        gather_b.finish()
    full_a, full_b = gather_a.result(), gather_b.result()
    qkv_full = jnp.concatenate([full_a, full_b[:, : 3 * width - half]], axis=1)
    gain_rows = full_b[:, 3 * width - half : 3 * width - half + 4].astype(F32).T

    gather_c = Gather(
        lay, index, jnp.concatenate([w_out.astype(BF16), w_up.astype(BF16)], axis=1)
    )
    gather_d = Gather(lay, index, w_down.astype(BF16))
    inputs = tokens_here.astype(F32)
    normed, first_pull = jax.vjp(layer_norm, inputs, gain_rows[0], gain_rows[1])
    normed_low = normed.astype(BF16)
    gather_c.start(far[-1], tokens_here)
    gather_d.start(far[-1], tokens_here)
    mixed = lax.dot_general(
        qkv_full, normed_low, (((0,), (1,)), ((), ())), preferred_element_type=F32
    ).astype(BF16)
    mixed = mixed.reshape(nh, 3, GROUPS, DH, rows)
    mixed = jnp.concatenate([mixed[:, :1] * jnp.asarray(DH**-0.5, BF16), mixed[:, 1:]], axis=1)

    def spread(cut):
        return to_groups([for_group(cut, 2, m) for m in range(GROUPS)])

    def both_parts(own):
        kv = jnp.stack([piece[:, 1:] for piece in own])
        return [across(kv, mr) for mr in range(1, lay.parts)]

    first_own = spread(mixed[:1])
    gather_c.finish(*first_own)
    gather_d.finish(*first_own)
    later_own = spread(after(mixed[1:], *first_own))
    first_other = both_parts(first_own)
    for bit in reversed(far[1:-1]):
        gather_c.step(bit)
        gather_d.step(bit)
    gather_c.start(far[0])
    gather_d.start(far[0])
    heads = [([p[0][:, None] for p in first_own], [p[:, 0][:, :, None] for p in first_other])]
    saved = [attend(lay, tables, *heads[0])]
    saved[0], later_own, gather_c.came, gather_d.came = join(
        saved[0], later_own, gather_c.came, gather_d.came
    )
    later_other = both_parts(later_own)
    for h in range(nh - 1):
        heads.append(
            ([p[h][:, None] for p in later_own], [p[:, h][:, :, None] for p in later_other])
        )
    gather_c.finish()
    gather_d.finish()
    gather_c.start(near_a[0])
    gather_d.start(near_b[0])
    grad_out = to_home(after(cotangent[0], gather_c.held))
    saved.append(attend(lay, tables, *heads[1]))
    saved[1], grad_out, gather_c.came, gather_d.came = join(
        saved[1], grad_out, gather_c.came, gather_d.came
    )
    gather_c.finish()
    gather_d.finish()
    for bit_a, bit_b in zip(near_a[1:-1], near_b[1:-1]):
        gather_c.step(bit_a)
        gather_d.step(bit_b)
    gather_c.start(near_a[-1])
    gather_d.start(near_b[-1])
    first_pieces = [jnp.concatenate([saved[h][1][m] for h in range(2)]) for m in range(GROUPS)]
    att_back = to_groups(first_pieces)
    own = [after(heads[2][0][0], gather_c.held, gather_d.held, *first_pieces)] + heads[2][0][1:]
    heads[2] = (own, heads[2][1])
    saved.append(attend(lay, tables, *heads[2]))
    saved[2], att_back, gather_c.came, gather_d.came = join(
        saved[2], att_back, gather_c.came, gather_d.came
    )
    last_pieces = to_groups([saved[2][1][m] for m in range(GROUPS)])
    gather_c.finish()
    gather_d.finish()
    for bit in core:
        gather_c.step(bit)
        gather_d.step(bit)
    full_c, down_full = gather_c.result(), gather_d.result()
    out_full, up_full = full_c[:, :width], full_c[:, width:]
    att_low = jnp.concatenate(
        [jnp.stack(unxor(att_back, group)), jnp.stack(unxor(last_pieces, group))], axis=1
    ).reshape(width, rows)

    branch = lax.dot_general(
        att_low, out_full, (((0,), (0,)), ((), ())), preferred_element_type=F32
    )
    resid_sum = inputs + branch
    hidden_norm, second_pull = jax.vjp(layer_norm, resid_sum, gain_rows[2], gain_rows[3])
    hidden_low = hidden_norm.astype(BF16)
    pre_act = jnp.dot(hidden_low, up_full, preferred_element_type=F32)
    activated, gelu_pull = jax.vjp(partial(jax.nn.gelu, approximate=True), pre_act)
    act_low = activated.astype(BF16)
    result = resid_sum + jnp.dot(act_low, down_full, preferred_element_type=F32)
    result_low = result.astype(BF16)
    grad_down = jnp.einsum("tf,td->fd", act_low, grad_out, preferred_element_type=F32)
    scatter_d = Scatter(lay, index, [grad_down])
    scatter_d.start(core[0])
    grad_act = jnp.einsum("td,fd->tf", grad_out, down_full, preferred_element_type=F32)
    grad_pre = gelu_pull(grad_act)[0].astype(BF16)
    grad_up = jnp.einsum("td,tf->df", hidden_low, grad_pre, preferred_element_type=F32)
    grad_hidden = jnp.einsum("tf,df->td", grad_pre, up_full, preferred_element_type=F32)
    back_resid, grad_gain2, grad_shift2 = second_pull(grad_hidden)
    grad_resid = grad_out.astype(F32) + back_resid
    grad_branch = grad_resid.astype(BF16)
    grad_wout = lax.dot_general(
        att_low, grad_branch, (((1,), (0,)), ((), ())), preferred_element_type=F32
    )
    scatter_c = Scatter(lay, index, [grad_wout, grad_up])
    scatter_c.start(core[0])
    dob = lax.dot_general(
        out_full, grad_branch, (((1,), (1,)), ((), ())), preferred_element_type=F32
    ).astype(BF16)
    dob = dob.reshape(GROUPS, nh, DH, rows)
    dob_pieces = to_groups([for_group(dob, 0, m) for m in range(GROUPS)])
    scatter_d.finish()
    scatter_c.finish()
    for bit in core[1:]:
        scatter_d.step(bit)
        scatter_c.step(bit)
    scatter_d.start(near_b[0])
    scatter_c.start(near_a[0], *dob_pieces)
    layer_out = to_owner(after(result_low, *dob_pieces))

    def back(h, *others):
        pieces = [p[h : h + 1] for p in dob_pieces]
        pieces[0] = after(pieces[0], *others)
        return attend_back(lay, tables, *heads[h], pieces, saved[h][0], saved[h][2])

    def share(dkv):
        return [across(dkv[mr * GROUPS : (mr + 1) * GROUPS], mr) for mr in range(1, lay.parts)]

    def summed_pieces(dq, dkv, came):
        total = dkv[:GROUPS].astype(F32)
        for piece in came:
            total = total + piece.astype(F32)
        low = total.astype(BF16)[:, :, 0]
        return [jnp.concatenate([dq[m], low[m]], axis=0) for m in range(GROUPS)]

    def rejoin(pieces):
        return jnp.stack(unxor(pieces, group), axis=1).reshape(3 * width // nh, rows)

    first = back(0, *scatter_c.held, *scatter_d.held)
    first, layer_out, scatter_c.came, scatter_d.came = join(
        first, layer_out, scatter_c.came, scatter_d.came
    )
    shared = share(first[1])
    scatter_d.finish()
    scatter_c.finish()
    for bit_a, bit_b in zip(near_a[1:-1], near_b[1:-1]):
        scatter_c.step(bit_a)
        scatter_d.step(bit_b)
    second = back(1, *scatter_c.held, *scatter_d.held)
    scatter_d.start(near_b[-1])
    scatter_c.start(near_a[-1])
    second, shared, scatter_c.came, scatter_d.came = join(
        second, shared, scatter_c.came, scatter_d.came
    )
    pieces_one = summed_pieces(*first, shared)
    returned = [to_groups(pieces_one)]
    shared = share(second[1])
    scatter_d.finish()
    scatter_c.finish()
    pieces_two = summed_pieces(*second, shared)
    returned.append(to_groups(pieces_two))
    scatter_d.start(far[0])
    scatter_c.start(far[0])
    third = back(2, *scatter_c.held, *scatter_d.held, *pieces_one, *pieces_two)
    third, returned, scatter_c.came, scatter_d.came = join(
        third, returned, scatter_c.came, scatter_d.came
    )
    shared = share(third[1])
    scatter_d.finish()
    scatter_c.finish()
    for bit in far[1:-1]:
        scatter_c.step(bit)
        scatter_d.step(bit)
    scatter_d.start(far[-1])
    scatter_c.start(far[-1])
    returned.append(to_groups(summed_pieces(*third, shared)))
    mixed_grads = [rejoin(pieces) for pieces in returned]
    mixed_grad = jnp.concatenate(mixed_grads, axis=0)

    def weight_grad(piece):
        return lax.dot_general(
            normed_low, piece, (((0,), (1,)), ((), ())), preferred_element_type=F32
        )

    grad_normed = lax.dot_general(
        mixed_grad, qkv_full, (((0,), (1,)), ((), ())), preferred_element_type=F32
    )
    back_input, grad_gain1, grad_shift1 = first_pull(grad_normed)
    grad_vec = jnp.stack([grad_gain1, grad_shift1, grad_gain2, grad_shift2]).T
    grad_vec = jnp.concatenate([grad_vec, jnp.zeros((width, 124), F32)], axis=1)
    wqkv_grads = [weight_grad(piece) for piece in mixed_grads]
    scatter = Scatter(lay, index, wqkv_grads + [grad_vec])
    for bit in core:
        scatter.step(bit)
    one, two, three, vec = scatter.held
    split = half - 3 * width // nh
    scatter_a = Scatter(lay, index, [one, two[..., :split]], scatter.left)
    scatter_b = Scatter(lay, index, [two[..., split:], three, vec], scatter.left)
    for bit_a, bit_b in zip(near_a, near_b):
        scatter_a.start(bit_a)
        scatter_b.start(bit_b)
        scatter_a.finish()
        scatter_b.finish()
    scatter = Scatter(lay, index, scatter_a.held + scatter_b.held, scatter_a.left)
    for bit in far:
        scatter.step(bit)
    input_low = to_owner(after((grad_resid + back_input).astype(BF16), *scatter.held))
    summed_down, summed_c = scatter_d.finish()[0], scatter_c.finish()
    summed_qkv = from_by_head(jnp.concatenate(scatter.held[:4], axis=1))
    summed_out, summed_up = summed_c
    summed_norms = scatter.held[4][:, :4].T
    layer_out, input_grad = layer_out[None], input_low.astype(F32)[None]

    summed = (summed_qkv, summed_out, summed_up, summed_down, summed_norms)
    square = sum((jnp.sum(member * member) for member in summed))
    for bit in range(lay.n_bits):
        square = square + lax.ppermute(square, AXES, lay.bit_perm(bit))
    grad_norm = jnp.sqrt(square)
    factor = CLIP_NORM / jnp.maximum(grad_norm, CLIP_NORM)
    upd_qkv = adamw(w_qkv, summed_qkv * factor, m_qkv, v_qkv, a_qkv, RATE_MAT, WEIGHT_DECAY)
    upd_out = adamw(w_out, summed_out * factor, m_out, v_out, a_out, RATE_OUT, WEIGHT_DECAY)
    upd_up = adamw(w_up, summed_up * factor, m_up, v_up, a_up, RATE_MAT, WEIGHT_DECAY)
    upd_down = adamw(w_down, summed_down * factor, m_down, v_down, a_down, RATE_MAT, WEIGHT_DECAY)
    upd_norms = adamw(w_norms, summed_norms * factor, m_norms, v_norms, a_norms, RATE_VEC, 0.0)
    updates = (upd_qkv, upd_out, upd_up, upd_down, upd_norms)
    return (layer_out, input_grad, grad_norm) + tuple(u[k] for k in range(4) for u in updates)


def solution(mesh):
    lay = Layout(mesh.shape["seq"], mesh.shape["dp"])
    rows = P(AXES, None)
    vecs = P(None, AXES)
    state = (rows, rows, rows, rows, vecs)
    block = P("dp", "seq", None)
    return jax.shard_map(
        partial(per_device, lay),
        mesh=mesh,
        in_specs=(block, block, P("dp", None)) + state * 4,
        out_specs=(block, block, P()) + state * 4,
        check_vma=False,
    )
```

```python
from functools import partial

import jax
import jax.numpy as jnp
import numpy as np
from jax import lax
from jax.experimental import pallas as pl
from jax.experimental.pallas import tpu as pltpu
from jax.sharding import PartitionSpec as P

DH = 64
STEP = 5

NORM_EPS = 1e-05
CLIP_NORM = 1.0
RATE_MAT = 0.03
RATE_OUT = 0.15
RATE_VEC = 0.3
WEIGHT_DECAY = 0.1
BETA_ONE = 0.5
BETA_TWO = 0.5
ADAM_EPS = 1e-08
AVERAGE = 0.8
MASKED_LOW = -1e30

AXES = ("seq", "dp")
GROUPS = 4
F32 = jnp.float32
BF16 = jnp.bfloat16
NN = (((1,), (0,)), ((), ()))
NT = (((1,), (1,)), ((), ()))


class Layout:
    def __init__(self, n_seq, n_dp):
        self.n_seq, self.n_dp, self.size = n_seq, n_dp, n_seq * n_dp
        self.parts = n_seq // GROUPS
        self.n_bits = self.size.bit_length() - 1
        planes = n_seq == 8 and n_dp == 4
        self.moves = planes
        count = self.size
        self.seq_of = np.zeros(count, np.int32)
        self.blk_of = np.zeros(count, np.int32)
        self.grp_of = np.zeros(count, np.int32)
        self.part_of = np.zeros(count, np.int32)
        self.home = np.zeros(count, np.int32)
        for s in range(n_dp):
            for b in range(n_seq):
                source = b * n_dp + s
                if planes:
                    px, pz, pc = b & 1, (b >> 1) & 1, ((b >> 2) ^ (b >> 1) ^ b) & 1
                    dev = (s & 1) * 16 + pz * 8 + px * 4 + (s >> 1) * 2 + pc
                    g, r = px * 2 + pz, pc
                else:
                    dev = source
                    low = b % (2 * self.parts)
                    r = min(low, 2 * self.parts - 1 - low)
                    g = 2 * (b // (2 * self.parts)) + int(low >= self.parts)
                self.home[source] = dev
                self.seq_of[dev], self.blk_of[dev] = s, b
                self.grp_of[dev], self.part_of[dev] = g, r
        self.dev_at = {
            (int(self.seq_of[i]), int(self.grp_of[i]), int(self.part_of[i])): i for i in range(count)
        }
        if planes:
            self.core, self.near, self.far = (0,), ((2,), (1,)), (3, 4)
        else:
            self.core, self.near, self.far = (0,), ((2, 1), (3,)), tuple(range(4, self.n_bits))
        blocks = np.zeros((count, GROUPS * self.parts), np.int32)
        lists = []
        for i in range(count):
            s, g, r = int(self.seq_of[i]), int(self.grp_of[i]), int(self.part_of[i])
            for mr in range(self.parts):
                for m in range(GROUPS):
                    blocks[i, mr * GROUPS + m] = self.blk_of[self.dev_at[(s, g ^ m, r ^ mr)]]
            pairs = [
                (qs, ks)
                for qs in range(GROUPS)
                for ks in range(GROUPS * self.parts)
                if blocks[i, ks] <= blocks[i, qs]
            ]
            lists.append(
                [p for p in pairs if p[0] != p[1]] + [p for p in pairs if p[0] == p[1]]
            )
        self.n_pairs = len(lists[0])
        self.blocks = blocks
        self.pairs = np.array(lists, np.int32).transpose(0, 2, 1)

    def bit_perm(self, bit):
        return [(i, i ^ (1 << bit)) for i in range(self.size)]

    def group_perm(self, mg, mr):
        out = []
        for i in range(self.size):
            s, g, r = int(self.seq_of[i]), int(self.grp_of[i]), int(self.part_of[i])
            out.append((i, self.dev_at[(s, g ^ mg, r ^ mr)]))
        return out

    def home_perm(self):
        return [(i, int(self.home[i])) for i in range(self.size)]

    def back_perm(self):
        return [(int(self.home[i]), i) for i in range(self.size)]


def layer_norm(values, gain_vec, shift_vec):
    centre = values - jnp.mean(values, axis=-1, keepdims=True)
    spread = jnp.mean(centre * centre, axis=-1, keepdims=True)
    return centre * lax.rsqrt(spread + NORM_EPS) * gain_vec + shift_vec


def adamw(weight, grad, first, second, average, rate, decay):
    first_new = BETA_ONE * first + (1.0 - BETA_ONE) * grad
    second_new = BETA_TWO * second + (1.0 - BETA_TWO) * grad * grad
    unbiased_one = first_new / (1.0 - BETA_ONE**STEP)
    unbiased_two = second_new / (1.0 - BETA_TWO**STEP)
    weight_new = weight - rate * (
        unbiased_one / (jnp.sqrt(unbiased_two) + ADAM_EPS) + decay * weight
    )
    average_new = AVERAGE * average + (1.0 - AVERAGE) * weight_new
    return (weight_new, first_new, second_new, average_new)


def mm(a, b, dims):
    return lax.dot_general(a, b, dims, preferred_element_type=F32)


LOG2E = 1.4426950408889634
TILE = 256
PLAIN_LIMIT, PLAIN_TOP = 90.0, 30.0


def seen(diagonal, rows, cols, qplace, kplace, low, high):
    qi = lax.broadcasted_iota(jnp.int32, (1, cols), 1) + qplace
    opening = jnp.where(qi >= high, high, jnp.where(qi >= low, low, 0)) - kplace
    ki = lax.broadcasted_iota(jnp.int32, (rows, cols), 0)
    ok = ki >= opening
    if diagonal:
        ok = ok & (ki <= (qi - kplace))
    return ok


def each_pair(info, pos, n_pairs, rows, count, work):
    def run(first, steps, size, diagonal):
        def step(p, carried):
            pairs = []
            for u in range(size):
                qs, ks = info[0, first + p * size + u], info[1, first + p * size + u]
                pairs.append((qs, ks, pos[qs] * rows, pos[ks] * rows))
            work(diagonal, pairs)
            return carried

        lax.fori_loop(0, steps, step, 0)

    plain = n_pairs - GROUPS
    run(0, plain // count, count, False)
    if plain % count:
        run(plain - plain % count, 1, plain % count, False)
    run(plain, GROUPS // count, count, True)


def tiles_of(rows, diagonal, size):
    return [
        (u, c, j)
        for u in range(size)
        for j in range(0, rows, TILE)
        for c in range(0, rows, TILE)
        if not (diagonal and j >= c + TILE)
    ]


def forward_kernel(parts, n_pairs, info, pos, lim, *refs):
    own = refs[:GROUPS]
    other = refs[GROUPS : GROUPS + parts - 1]
    o_ref, ob_ref, l_ref, q_s, k_s, v_s, m_s, z_s, n_s = refs[GROUPS + parts - 1 :]
    rows = o_ref.shape[2]
    low, high = lim[0], lim[1]
    q_top = jnp.zeros((1, rows), F32)
    k_top = jnp.zeros((1, rows), F32)

    def squares(a):
        a = a.astype(F32)
        return jnp.sum(a * a, axis=0, keepdims=True)

    for j in range(GROUPS):
        q_s[j] = own[j][0, 0]
        v_s[j] = own[j][0, 2]
        k_s[j] = own[j][0, 1].T
        q_top = jnp.maximum(q_top, squares(own[j][0, 0]))
        k_top = jnp.maximum(k_top, squares(own[j][0, 1]))
    for p in range(parts - 1):
        for j in range(GROUPS):
            at = (p + 1) * GROUPS + j
            v_s[at] = other[p][j, 0, 1]
            k_s[at] = other[p][j, 0, 0].T
            k_top = jnp.maximum(k_top, squares(other[p][j, 0, 0]))
    z_s[...] = jnp.zeros(z_s.shape, F32)
    n_s[...] = jnp.zeros(n_s.shape, F32)
    top = jnp.sqrt(jnp.max(q_top, keepdims=True) * jnp.max(k_top, keepdims=True) + 1.0)
    base = jnp.maximum(top - PLAIN_TOP, 0.0)
    base_two = base * LOG2E
    plain = jnp.max(top) <= PLAIN_LIMIT

    def work_plain(diagonal, pairs):
        tiles = tiles_of(rows, diagonal, len(pairs))

        def score(tile):
            u, c, j = tile
            qs, ks, _, _ = pairs[u]
            return mm(k_s[ks, pl.ds(j, TILE)], q_s[qs, :, pl.ds(c, TILE)], NN)

        totals, sums = {}, {}
        ahead = [score(tile) for tile in tiles[:2]]
        for at, (u, c, j) in enumerate(tiles):
            if at + 2 < len(tiles):
                ahead.append(score(tiles[at + 2]))
            s = ahead[at]
            ahead[at] = None
            qs, ks, qplace, kplace = pairs[u]
            x = s * s + 1.0
            r = lax.rsqrt(x)
            e = jnp.exp2(x * r * LOG2E - base_two)
            ok = seen(diagonal and j == c, TILE, TILE, qplace + c, kplace + j, low, high)
            e = jnp.where(ok, e, 0.0)
            w = (e * (s * r)).astype(BF16)
            z = jnp.sum(e, axis=0, keepdims=True)
            n = mm(v_s[ks, :, pl.ds(j, TILE)], w, NN)
            totals[u, c] = totals[u, c] + z if (u, c) in totals else z
            sums[u, c] = sums[u, c] + n if (u, c) in sums else n
        for u, c in totals:
            qs = pairs[u][0]
            z_s[qs, :, pl.ds(c, TILE)] += totals[u, c]
            n_s[qs, :, pl.ds(c, TILE)] += sums[u, c]

    def work_running(diagonal, pairs):
        for qs, ks, qplace, kplace in pairs:
            s = mm(k_s[ks], q_s[qs], NN)
            x = s * s + 1.0
            r = lax.rsqrt(x)
            ok = seen(diagonal, rows, rows, qplace, kplace, low, high)
            m = jnp.where(ok, x * r, MASKED_LOW)
            m_old = m_s[qs]
            m_new = jnp.maximum(m_old, jnp.max(m, axis=0, keepdims=True))
            fade = jnp.exp(m_old - m_new)
            e = jnp.exp(m - jnp.maximum(m_new, 0.0))
            w = (e * (s * r)).astype(BF16)
            z_s[qs] = z_s[qs] * fade + jnp.sum(e, axis=0, keepdims=True)
            n_s[qs] = n_s[qs] * fade + mm(v_s[ks], w, NN)
            m_s[qs] = m_new

    @pl.when(plain)
    def _():
        m_s[...] = jnp.broadcast_to(base, m_s.shape)
        each_pair(info, pos, n_pairs, rows, 2, work_plain)

    @pl.when(jnp.logical_not(plain))
    def _():
        m_s[...] = jnp.full(m_s.shape, MASKED_LOW, F32)
        each_pair(info, pos, n_pairs, rows, 1, work_running)

    for j in range(GROUPS):
        z = z_s[j]
        o = n_s[j] * (1.0 / z)
        o_ref[j] = o
        ob_ref[j] = o.astype(BF16)
        l_ref[j] = m_s[j] + jnp.log(z)


def backward_kernel(parts, n_pairs, scale, info, pos, lim, *refs):
    own = refs[:GROUPS]
    other = refs[GROUPS : GROUPS + parts - 1]
    refs = refs[GROUPS + parts - 1 :]
    dob = refs[:GROUPS]
    o_ref, l_ref = refs[GROUPS : GROUPS + 2]
    refs = refs[GROUPS + 2 :]
    dq_ref, dkv_ref = refs[:2]
    dkv_other = refs[2 : 1 + parts]
    q_s, kt_s, k_s, v_s, do_s, l_s, d_s, dq_s, dk_s, dv_s = refs[1 + parts :]
    rows = o_ref.shape[2]
    low, high = lim[0], lim[1]
    for j in range(GROUPS):
        q_s[j] = own[j][0, 0]
        kt_s[j] = own[j][0, 1]
        do_s[j] = dob[j][0]
        k_s[j] = own[j][0, 1].T
        v_s[j] = own[j][0, 2].T
        d_s[j] = jnp.sum(dob[j][0].astype(F32) * o_ref[j], axis=0, keepdims=True)
        l_s[j] = l_ref[j] * LOG2E
    for p in range(parts - 1):
        for j in range(GROUPS):
            at = (p + 1) * GROUPS + j
            kt_s[at] = other[p][j, 0, 0]
            k_s[at] = other[p][j, 0, 0].T
            v_s[at] = other[p][j, 0, 1].T
    dq_s[...] = jnp.zeros(dq_s.shape, F32)
    dk_s[...] = jnp.zeros(dk_s.shape, F32)
    dv_s[...] = jnp.zeros(dv_s.shape, F32)

    def work(diagonal, pairs):
        tiles = tiles_of(rows, diagonal, len(pairs))

        def score(tile):
            u, c, j = tile
            qs, ks, _, _ = pairs[u]
            keys, cols = pl.ds(j, TILE), pl.ds(c, TILE)
            return (
                mm(k_s[ks, keys], q_s[qs, :, cols], NN),
                mm(v_s[ks, keys], do_s[qs, :, cols], NN),
            )

        dqs, dks, dvs = {}, {}, {}

        def add(sums, key, value):
            sums[key] = sums[key] + value if key in sums else value

        ahead = [score(tile) for tile in tiles[:2]]
        for at, (u, c, j) in enumerate(tiles):
            if at + 2 < len(tiles):
                ahead.append(score(tiles[at + 2]))
            s, gw = ahead[at]
            ahead[at] = None
            qs, ks, qplace, kplace = pairs[u]
            keys, cols = pl.ds(j, TILE), pl.ds(c, TILE)
            x = s * s + 1.0
            r = lax.rsqrt(x)
            prob = jnp.exp2(x * r * LOG2E - l_s[qs, :, cols])
            ok = seen(diagonal and j == c, TILE, TILE, qplace + c, kplace + j, low, high)
            prob = jnp.where(ok, prob, 0.0)
            pt = prob * (s * r)
            gs = prob * (gw * (1.0 - r * r * (1.0 - r))) - pt * d_s[qs, :, cols]
            gs_low, pt_low = gs.astype(BF16), pt.astype(BF16)
            add(dvs, (u, j), mm(do_s[qs, :, cols], pt_low, NT))
            add(dks, (u, j), mm(q_s[qs, :, cols], gs_low, NT))
            add(dqs, (u, c), mm(kt_s[ks, :, keys], gs_low, NN))
        for u, j in dvs:
            ks = pairs[u][1]
            dv_s[ks, :, pl.ds(j, TILE)] += dvs[u, j]
            dk_s[ks, :, pl.ds(j, TILE)] += dks[u, j]
        for u, c in dqs:
            dq_s[pairs[u][0], :, pl.ds(c, TILE)] += dqs[u, c]

    each_pair(info, pos, n_pairs, rows, 2, work)
    for j in range(GROUPS):
        dq_ref[j] = (dq_s[j] * scale).astype(BF16)
        dkv_ref[j, 0] = dk_s[j]
        dkv_ref[j, 1] = dv_s[j]
        for p in range(parts - 1):
            dkv_other[p][j, 0] = dk_s[(p + 1) * GROUPS + j].astype(BF16)
            dkv_other[p][j, 1] = dv_s[(p + 1) * GROUPS + j].astype(BF16)


SMEM_SPEC = pl.BlockSpec(memory_space=pltpu.SMEM)
KERNEL_VMEM = 56 * 2**20


def whole(shape):
    return pl.BlockSpec(shape, lambda i: (0,) * len(shape))


def head_of(h, shape, axis):
    place = tuple(h if k == axis else 0 for k in range(len(shape)))
    return pl.BlockSpec(tuple(1 if k == axis else n for k, n in enumerate(shape)), lambda i: place)


def attend(lay, tables, h, own, other):
    rows = own[0].shape[3]
    slots = GROUPS * lay.parts
    shape = jax.ShapeDtypeStruct
    return pl.pallas_call(
        partial(forward_kernel, lay.parts, lay.n_pairs),
        grid=(1,),
        out_shape=(
            shape((GROUPS, DH, rows), F32),
            shape((GROUPS, DH, rows), BF16),
            shape((GROUPS, 1, rows), F32),
        ),
        in_specs=[SMEM_SPEC] * 3
        + [head_of(h, a.shape, 0) for a in own]
        + [head_of(h, a.shape, 1) for a in other],
        out_specs=(whole((GROUPS, DH, rows)), whole((GROUPS, DH, rows)), whole((GROUPS, 1, rows))),
        scratch_shapes=[
            pltpu.VMEM((GROUPS, DH, rows), BF16),
            pltpu.VMEM((slots, rows, DH), BF16),
            pltpu.VMEM((slots, DH, rows), BF16),
            pltpu.VMEM((GROUPS, 1, rows), F32),
            pltpu.VMEM((GROUPS, 1, rows), F32),
            pltpu.VMEM((GROUPS, DH, rows), F32),
        ],
        compiler_params=pltpu.CompilerParams(vmem_limit_bytes=KERNEL_VMEM),
        cost_estimate=pl.CostEstimate(
            flops=4 * lay.n_pairs * rows * rows * DH,
            bytes_accessed=2 * (slots + GROUPS) * 3 * DH * rows,
            transcendentals=2 * lay.n_pairs * rows * rows,
        ),
        name="attend",
    )(*tables, *own, *other)


def attend_back(lay, tables, h, own, other, dob_head, dob, o, lse):
    rows = own[0].shape[3]
    slots = GROUPS * lay.parts
    shape = jax.ShapeDtypeStruct
    kv = (GROUPS, 2, DH, rows)
    return pl.pallas_call(
        partial(backward_kernel, lay.parts, lay.n_pairs, DH**-0.5),
        grid=(1,),
        out_shape=(shape((GROUPS, DH, rows), BF16), shape(kv, F32))
        + (shape(kv, BF16),) * (lay.parts - 1),
        in_specs=[SMEM_SPEC] * 3
        + [head_of(h, a.shape, 0) for a in own]
        + [head_of(h, a.shape, 1) for a in other]
        + [head_of(dob_head, a.shape, 0) for a in dob]
        + [whole(o.shape), whole(lse.shape)],
        out_specs=(whole((GROUPS, DH, rows)), whole(kv)) + (whole(kv),) * (lay.parts - 1),
        scratch_shapes=[
            pltpu.VMEM((GROUPS, DH, rows), BF16),
            pltpu.VMEM((slots, DH, rows), BF16),
            pltpu.VMEM((slots, rows, DH), BF16),
            pltpu.VMEM((slots, rows, DH), BF16),
            pltpu.VMEM((GROUPS, DH, rows), BF16),
            pltpu.VMEM((GROUPS, 1, rows), F32),
            pltpu.VMEM((GROUPS, 1, rows), F32),
            pltpu.VMEM((GROUPS, DH, rows), F32),
            pltpu.VMEM((slots, DH, rows), F32),
            pltpu.VMEM((slots, DH, rows), F32),
        ],
        compiler_params=pltpu.CompilerParams(vmem_limit_bytes=KERNEL_VMEM),
        cost_estimate=pl.CostEstimate(
            flops=10 * lay.n_pairs * rows * rows * DH,
            bytes_accessed=2 * (slots + GROUPS) * 5 * DH * rows,
            transcendentals=2 * lay.n_pairs * rows * rows,
        ),
        name="attend_back",
    )(*tables, *own, *other, *dob, o, lse)


TN = (((0,), (0,)), ((), ()))
GELU_ROOT, GELU_CUBE = 0.7978845608028654, 0.044715


def feed_forward_kernel(
    slab, hn_ref, dy_ref, up, packed, y_ref, dhn_ref, gdown_ref, gup_ref, g_s, du_s, down
):
    width = up.shape[0]
    places = [
        (i, b)
        for i in range(packed.shape[0] // slab)
        for b in range(packed.shape[1] // width)
    ]
    if len(places) == 1:
        down[...] = packed[...]
    else:
        cut = [
            packed[:, b * width : (b + 1) * width].astype(F32)
            for b in range(packed.shape[1] // width)
        ]
        for n, (i, b) in enumerate(places):
            if n % 2 == 0:
                pair = [cut[q][p * slab : (p + 1) * slab] for p, q in places[n : n + 2]]
                down[pl.ds(n * slab, 2 * slab)] = jnp.concatenate(pair, axis=0).astype(BF16)

    @pl.when(pl.program_id(0) == 0)
    def _():
        y_ref[...] = jnp.zeros(y_ref.shape, F32)
        dhn_ref[...] = jnp.zeros(dhn_ref.shape, F32)

    step = hn_ref.shape[0] // 2
    for k in range(2):
        part = pl.ds(k * step, step)
        u = mm(hn_ref[part], up[...], NN)
        dg = mm(dy_ref[part], down[...], NT)
        square = u * u
        th = jnp.tanh(u * (GELU_ROOT + (GELU_ROOT * GELU_CUBE) * square))
        half = 0.5 + 0.5 * th
        slope = half + (0.5 * u) * (1.0 - th * th) * (
            GELU_ROOT + (3.0 * GELU_ROOT * GELU_CUBE) * square
        )
        g_s[part] = (u * half).astype(BF16)
        du_s[part] = (slope * dg).astype(BF16)
        y_ref[part] += mm(g_s[part], down[...], NN)
        dhn_ref[part] += mm(du_s[part], up[...], NT)
    grad = mm(g_s[...], dy_ref[...], TN)
    for n, (i, b) in enumerate(places):
        rows_at, cols_at = pl.ds(i * slab, slab), pl.ds(b * width, width)
        gdown_ref[rows_at, cols_at] = grad[n * slab : (n + 1) * slab]
    gup_ref[...] = mm(hn_ref[...], du_s[...], TN)


def feed_forward(hn, dy, weights, slab):
    rows, width = hn.shape
    tiles = weights.shape[1] // width // 2
    if slab:
        down_spec = pl.BlockSpec((width // tiles, tiles * width), lambda t: (t, 0))
    else:
        down_spec = pl.BlockSpec((width, width), lambda t: (0, t))
    shape = jax.ShapeDtypeStruct
    full = pl.BlockSpec((rows, width), lambda t: (0, 0))
    columns = pl.BlockSpec((width, width), lambda t: (0, t))
    return pl.pallas_call(
        partial(feed_forward_kernel, slab or width),
        grid=(tiles,),
        out_shape=(
            shape((rows, width), F32),
            shape((rows, width), F32),
            shape((width, tiles * width), F32),
            shape((width, tiles * width), F32),
        ),
        in_specs=[
            full,
            full,
            pl.BlockSpec((width, width), lambda t: (0, tiles + t)),
            down_spec,
        ],
        out_specs=(full, full, down_spec, columns),
        scratch_shapes=[pltpu.VMEM((rows, width), BF16)] * 2 + [pltpu.VMEM((width, width), BF16)],
        compiler_params=pltpu.CompilerParams(vmem_limit_bytes=KERNEL_VMEM),
        cost_estimate=pl.CostEstimate(
            flops=12 * tiles * rows * width * width,
            bytes_accessed=12 * tiles * width * width,
            transcendentals=tiles * rows * width,
        ),
        name="feed_forward",
    )(hn, dy, weights, weights)


def after(value, *others):
    return lax.optimization_barrier((value,) + others)[0]


def join(*values):
    return lax.optimization_barrier(values)


class Gather:
    def __init__(self, lay, index, shard):
        self.lay, self.index, self.rows, self.held = lay, index, shard.shape[0], shard
        self.bits, self.came, self.bit = (), None, None

    def start(self, bit, *others):
        if others:
            self.held = after(self.held, *others)
        self.bit = bit
        self.came = lax.ppermute(self.held, AXES, self.lay.bit_perm(bit))

    def finish(self, *others):
        came = after(self.came, *others) if others else self.came
        upper = ((self.index >> self.bit) & 1) == 1
        mine = self.held
        self.held = jnp.where(upper, jnp.stack([came, mine]), jnp.stack([mine, came]))
        self.bits = (self.bit,) + self.bits
        return self.held

    def step(self, bit, *others):
        self.start(bit, *others)
        return self.finish()

    def columns(self, start, stop):
        part = Gather(self.lay, self.index, self.held[..., start:stop])
        part.rows, part.bits = self.rows, self.bits
        return part

    def result(self):
        axes = tuple(self.bits.index(b) for b in sorted(self.bits, reverse=True))
        held = self.held.transpose(axes + tuple(range(len(axes), self.held.ndim)))
        return held.reshape((self.rows << len(axes),) + self.held.shape[len(axes) + 1 :])


class Scatter:
    def __init__(self, lay, index, arrays, left=None):
        self.lay, self.index = lay, index
        self.left = list(left)
        self.held, self.came, self.keep = list(arrays), None, None

    def start(self, bit, *others):
        if others:
            self.held = [after(h, *others) for h in self.held]
        axis = self.left.index(bit)
        self.left.pop(axis)
        mine = (self.index >> bit) & 1
        self.keep = [lax.dynamic_index_in_dim(h, mine, axis, keepdims=False) for h in self.held]
        give = [
            lax.dynamic_index_in_dim(h, 1 - mine, axis, keepdims=False).astype(BF16)
            for h in self.held
        ]
        give = jnp.concatenate(give, axis=-1) if len(give) > 1 else give[0]
        self.came = lax.ppermute(give, AXES, self.lay.bit_perm(bit))

    def finish(self, *others):
        came = after(self.came, *others) if others else self.came
        at, held = 0, []
        for keep in self.keep:
            held.append(keep + came[..., at : at + keep.shape[-1]].astype(F32))
            at += keep.shape[-1]
        self.held = held
        return held

    def step(self, bit, *others):
        self.start(bit, *others)
        return self.finish()


def by_owner(array, n_bits):
    return array.reshape((2,) * n_bits + (array.shape[0] >> n_bits,) + array.shape[1:])


def unxor(items, mask):
    for bit in range((len(items) - 1).bit_length()):
        on = ((mask >> bit) & 1) == 1
        items = [jnp.where(on, items[k ^ (1 << bit)], items[k]) for k in range(len(items))]
    return items


def per_device(
    lay,
    tokens,
    cotangent,
    bounds,
    w_qkv,
    w_out,
    w_up,
    w_down,
    w_norms,
    m_qkv,
    m_out,
    m_up,
    m_down,
    m_norms,
    v_qkv,
    v_out,
    v_up,
    v_down,
    v_norms,
    a_qkv,
    a_out,
    a_up,
    a_down,
    a_norms,
):
    rows, width = tokens.shape[1], tokens.shape[2]
    n_heads = width // DH
    nh = n_heads // GROUPS
    index = lax.axis_index("seq") * lay.n_dp + lax.axis_index("dp")
    group = jnp.asarray(lay.grp_of)[index]
    blocks = jnp.asarray(lay.blocks)[index]
    pairs = jnp.asarray(lay.pairs)[index]

    if lay.moves:
        to_home = partial(lax.ppermute, axis_name=AXES, perm=lay.home_perm())
        to_owner = partial(lax.ppermute, axis_name=AXES, perm=lay.back_perm())
    else:
        to_home = to_owner = lambda v: v

    def to_groups(items):
        return [items[0]] + [
            lax.ppermute(items[m], AXES, lay.group_perm(m, 0)) for m in range(1, GROUPS)
        ]

    def for_group(array, axis, m):
        return lax.dynamic_index_in_dim(array, group ^ m, axis, keepdims=False)

    def across(array, mr):
        return lax.ppermute(array, AXES, lay.group_perm(0, mr))

    def by_head(shard):
        cut = shard.reshape(-1, 3, GROUPS, nh, DH).transpose(0, 3, 1, 2, 4)
        return cut.reshape(shard.shape)

    def from_by_head(shard):
        cut = shard.reshape(-1, nh, 3, GROUPS, DH).transpose(0, 2, 3, 1, 4)
        return cut.reshape(shard.shape)

    far, core = lay.far, lay.core

    def across_cores(array):
        return lax.ppermute(array, AXES, lay.bit_perm(core[0]))

    near_a = lay.near[0] + lay.near[1]
    near_b = lay.near[1] + lay.near[0]

    pad = jnp.zeros((w_qkv.shape[0], 128 - w_norms.shape[0]), BF16)
    low_qkv = by_head(w_qkv.astype(BF16))
    half = (3 * width // 2) // 128 * 128
    gather = Gather(
        lay, index, jnp.concatenate([low_qkv, w_norms.T.astype(BF16), pad], axis=1)
    )
    gather.start(far[-1])
    limits, gather.came = join(to_home(bounds[0]), gather.came)
    gather.finish()
    tokens_here = to_home(after(tokens[0], gather.held))
    tables = (pairs, blocks, limits)
    for bit in reversed(far[:-1]):
        gather.step(bit)
    gather_a, gather_b = gather.columns(0, half), gather.columns(half, 3 * width + 128)
    for bit_a, bit_b in zip(near_a, near_b):
        gather_a.start(bit_a)
        gather_b.start(bit_b)
        gather_a.finish()
        gather_b.finish()
    for bit in core:
        gather_a.start(bit)
        gather_b.start(bit)
        gather_a.finish()
        gather_b.finish()
    full_a, full_b = gather_a.result(), gather_b.result()
    qkv_full = jnp.concatenate([full_a, full_b[:, : 3 * width - half]], axis=1)
    gain_rows = full_b[:, 3 * width - half : 3 * width - half + 4].astype(F32).T

    own_rows, tiles = w_up.shape[0], w_up.shape[1] // width
    slab = own_rows if own_rows % 8 == 0 else 0

    def by_tile(shard):
        return shard if slab else shard.reshape(-1, width, tiles).swapaxes(1, 2).reshape(shard.shape)

    def from_by_tile(shard):
        return shard if slab else shard.reshape(-1, tiles, width).swapaxes(1, 2).reshape(shard.shape)

    def pack(shard):
        if slab:
            shard = jnp.swapaxes(shard.reshape(tiles, own_rows, width), 0, 1)
        return shard.reshape(own_rows, tiles * width)

    def unpack(shard):
        if slab:
            shard = jnp.swapaxes(shard.reshape(own_rows, tiles, width), 0, 1)
        return shard.reshape(tiles * own_rows, width)

    rest = jnp.concatenate(
        [pack(w_down.astype(BF16)), by_tile(w_up.astype(BF16)), w_out.astype(BF16)], axis=1
    )
    inputs = tokens_here.astype(F32)
    normed, first_pull = jax.vjp(layer_norm, inputs, gain_rows[0], gain_rows[1])
    normed_low = normed.astype(BF16)
    mixed = lax.dot_general(
        qkv_full, normed_low, (((0,), (1,)), ((), ())), preferred_element_type=F32
    ).astype(BF16)
    mixed = mixed.reshape(nh, 3, GROUPS, DH, rows)
    mixed = jnp.concatenate([mixed[:, :1] * jnp.asarray(DH**-0.5, BF16), mixed[:, 1:]], axis=1)

    def spread(cut):
        return to_groups([for_group(cut, 2, m) for m in range(GROUPS)])

    def both_parts(own):
        kv = jnp.stack([piece[:, 1:] for piece in own])
        return [across(kv, mr) for mr in range(1, lay.parts)]

    first_own = spread(mixed[:1])
    later_own = spread(after(mixed[1:], *first_own))
    rest_full = lax.all_gather(after(rest, *first_own), AXES, axis=0, tiled=True)
    out_full = rest_full[:, 2 * tiles * width :]
    first_other = both_parts(first_own)
    heads = [(0, first_own, first_other)]
    saved = [attend(lay, tables, *heads[0])]
    saved[0], later_own = join(saved[0], later_own)
    later_other = both_parts(later_own)
    for h in range(nh - 1):
        heads.append((h, later_own, later_other))
    grad_out = to_home(after(cotangent[0], saved[0][1]))
    saved.append(attend(lay, tables, *heads[1]))
    saved[1], grad_out = join(saved[1], grad_out)
    first_pieces = [jnp.stack([saved[h][1][m] for h in range(2)]) for m in range(GROUPS)]
    att_back = to_groups(first_pieces)
    own = [after(later_own[0], *first_pieces)] + later_own[1:]
    saved.append(attend(lay, tables, 1, own, later_other))
    saved[2], att_back = join(saved[2], att_back)
    last_pieces = to_groups([saved[2][1][m : m + 1] for m in range(GROUPS)])
    att_low = jnp.concatenate(
        [jnp.stack(unxor(att_back, group)), jnp.stack(unxor(last_pieces, group))], axis=1
    ).reshape(width, rows)

    branch = lax.dot_general(
        att_low, out_full, (((0,), (0,)), ((), ())), preferred_element_type=F32
    )
    resid_sum = inputs + branch
    hidden_norm, second_pull = jax.vjp(layer_norm, resid_sum, gain_rows[2], gain_rows[3])
    hidden_low = hidden_norm.astype(BF16)
    y, dhn, grad_down, grad_up = feed_forward(hidden_low, grad_out, rest_full, slab)
    result_low = (resid_sum + y).astype(BF16)
    descending = list(reversed(range(lay.n_bits)))
    scatter_d = Scatter(lay, index, [by_owner(grad_down, lay.n_bits)], descending)
    scatter_d.start(core[0])
    back_resid, grad_gain2, grad_shift2 = second_pull(dhn)
    grad_resid = grad_out.astype(F32) + back_resid
    grad_branch = grad_resid.astype(BF16)
    dob = lax.dot_general(
        out_full, grad_branch, (((1,), (1,)), ((), ())), preferred_element_type=F32
    ).astype(BF16)
    dob = dob.reshape(GROUPS, nh, DH, rows)
    dob_pieces = to_groups([for_group(dob, 0, m) for m in range(GROUPS)])
    grad_wout = lax.dot_general(
        att_low, grad_branch, (((1,), (0,)), ((), ())), preferred_element_type=F32
    )
    scatter_c = Scatter(
        lay,
        index,
        [by_owner(grad_wout, lay.n_bits), by_owner(grad_up, lay.n_bits)],
        descending,
    )
    scatter_c.start(core[0])
    scatter_d.finish()
    scatter_c.finish()
    for bit in core[1:]:
        scatter_d.step(bit)
        scatter_c.step(bit)
    scatter_d.start(near_b[0])
    scatter_c.start(near_a[0], *dob_pieces)
    layer_out = to_owner(after(result_low[None], *dob_pieces))

    def back(h, *others):
        pieces = [after(dob_pieces[0], *others)] + dob_pieces[1:]
        return attend_back(lay, tables, *heads[h], h, pieces, saved[h][0], saved[h][2])

    def share(grads):
        return [across(grads[1 + mr], mr) for mr in range(1, lay.parts)]

    def summed_pieces(grads, came):
        total = grads[1]
        for piece in came:
            total = total + piece.astype(F32)
        low = total.astype(BF16)
        return [jnp.concatenate([grads[0][m][None], low[m]], axis=0) for m in range(GROUPS)]

    def rejoin(pieces):
        return jnp.stack(unxor(pieces, group), axis=1).reshape(3 * width // nh, rows)

    first = back(0, *scatter_c.held, *scatter_d.held)
    first, layer_out, scatter_c.came, scatter_d.came = join(
        first, layer_out, scatter_c.came, scatter_d.came
    )
    shared = share(first)
    scatter_d.finish()
    scatter_c.finish()
    for bit_a, bit_b in zip(near_a[1:-1], near_b[1:-1]):
        scatter_c.step(bit_a)
        scatter_d.step(bit_b)
    second = back(1, *scatter_c.held, *scatter_d.held)
    scatter_d.start(near_b[-1])
    scatter_c.start(near_a[-1])
    second, shared, scatter_c.came, scatter_d.came = join(
        second, shared, scatter_c.came, scatter_d.came
    )
    pieces_one = summed_pieces(first, shared)
    returned = [to_groups(pieces_one)]
    shared = share(second)
    scatter_d.finish()
    scatter_c.finish()
    pieces_two = summed_pieces(second, shared)
    returned.append(to_groups(pieces_two))
    scatter_d.start(far[0])
    scatter_c.start(far[0])
    third = back(2, *scatter_c.held, *scatter_d.held, *pieces_one, *pieces_two)
    third, returned, scatter_c.came, scatter_d.came = join(
        third, returned, scatter_c.came, scatter_d.came
    )
    shared = share(third)
    scatter_d.finish()
    scatter_c.finish()
    for bit in far[1:-1]:
        scatter_c.step(bit)
        scatter_d.step(bit)
    scatter_d.start(far[-1])
    scatter_c.start(far[-1])
    returned.append(to_groups(summed_pieces(third, shared)))
    mixed_grads = [rejoin(pieces) for pieces in returned]
    mixed_grad = jnp.concatenate(mixed_grads, axis=0)

    def weight_grad(piece):
        return lax.dot_general(
            normed_low, piece, (((0,), (1,)), ((), ())), preferred_element_type=F32
        )

    grad_normed = lax.dot_general(
        mixed_grad, qkv_full, (((0,), (1,)), ((), ())), preferred_element_type=F32
    )
    back_input, grad_gain1, grad_shift1 = first_pull(grad_normed)
    grad_vec = jnp.stack([grad_gain1, grad_shift1, grad_gain2, grad_shift2]).T
    grad_vec = jnp.concatenate([grad_vec, jnp.zeros((width, 124), F32)], axis=1)
    wqkv_grads = [weight_grad(piece) for piece in mixed_grads]
    scatter = Scatter(
        lay, index, [by_owner(a, lay.n_bits) for a in wqkv_grads + [grad_vec]], descending
    )
    for bit in core:
        scatter.step(bit)
    one, two, three, vec = scatter.held
    split = half - 3 * width // nh
    scatter_a = Scatter(lay, index, [one, two[..., :split]], scatter.left)
    scatter_b = Scatter(lay, index, [two[..., split:], three, vec], scatter.left)
    for bit_a, bit_b in zip(near_a, near_b):
        scatter_a.start(bit_a)
        scatter_b.start(bit_b)
        scatter_a.finish()
        scatter_b.finish()
    scatter = Scatter(lay, index, scatter_a.held + scatter_b.held, scatter_a.left)
    for bit in far:
        scatter.step(bit)
    input_low = to_owner(after((grad_resid + back_input).astype(BF16), *scatter.held))
    summed_down, summed_c = scatter_d.finish()[0], scatter_c.finish()
    summed_qkv = from_by_head(jnp.concatenate(scatter.held[:4], axis=1))
    summed_out, summed_up = summed_c[0], from_by_tile(summed_c[1])
    summed_down = unpack(summed_down)
    summed_norms = scatter.held[4][:, :4].T
    input_grad = input_low.astype(F32)[None]

    summed = (summed_qkv, summed_out, summed_up, summed_down, summed_norms)
    square = sum((jnp.sum(member * member) for member in summed))
    for bit in range(lay.n_bits):
        square = square + lax.ppermute(square, AXES, lay.bit_perm(bit))
    grad_norm = jnp.sqrt(square)
    factor = CLIP_NORM / jnp.maximum(grad_norm, CLIP_NORM)
    upd_qkv = adamw(w_qkv, summed_qkv * factor, m_qkv, v_qkv, a_qkv, RATE_MAT, WEIGHT_DECAY)
    upd_out = adamw(w_out, summed_out * factor, m_out, v_out, a_out, RATE_OUT, WEIGHT_DECAY)
    upd_up = adamw(w_up, summed_up * factor, m_up, v_up, a_up, RATE_MAT, WEIGHT_DECAY)
    upd_down = adamw(w_down, summed_down * factor, m_down, v_down, a_down, RATE_MAT, WEIGHT_DECAY)
    upd_norms = adamw(w_norms, summed_norms * factor, m_norms, v_norms, a_norms, RATE_VEC, 0.0)
    updates = (upd_qkv, upd_out, upd_up, upd_down, upd_norms)
    return (layer_out, input_grad, grad_norm) + tuple(u[k] for k in range(4) for u in updates)


def solution(mesh):
    lay = Layout(mesh.shape["seq"], mesh.shape["dp"])
    rows = P(AXES, None)
    vecs = P(None, AXES)
    state = (rows, rows, rows, rows, vecs)
    block = P("dp", "seq", None)
    return jax.shard_map(
        partial(per_device, lay),
        mesh=mesh,
        in_specs=(block, block, P("dp", None)) + state * 4,
        out_specs=(block, block, P()) + state * 4,
        check_vma=False,
    )
```

```python
from functools import partial

import jax
import jax.numpy as jnp
import numpy as np
from jax import lax
from jax.experimental import pallas as pl
from jax.experimental.pallas import tpu as pltpu
from jax.sharding import PartitionSpec as P

DH = 64
STEP = 5

NORM_EPS = 1e-05
CLIP_NORM = 1.0
RATE_MAT = 0.03
RATE_OUT = 0.15
RATE_VEC = 0.3
WEIGHT_DECAY = 0.1
BETA_ONE = 0.5
BETA_TWO = 0.5
ADAM_EPS = 1e-08
AVERAGE = 0.8
MASKED_LOW = -1e30

AXES = ("seq", "dp")
GROUPS = 4
F32 = jnp.float32
BF16 = jnp.bfloat16
NN = (((1,), (0,)), ((), ()))
NT = (((1,), (1,)), ((), ()))


class Layout:
    def __init__(self, n_seq, n_dp):
        self.n_seq, self.n_dp, self.size = n_seq, n_dp, n_seq * n_dp
        self.parts = n_seq // GROUPS
        self.n_bits = self.size.bit_length() - 1
        planes = n_seq == 8 and n_dp == 4
        self.moves = planes
        count = self.size
        self.seq_of = np.zeros(count, np.int32)
        self.blk_of = np.zeros(count, np.int32)
        self.grp_of = np.zeros(count, np.int32)
        self.part_of = np.zeros(count, np.int32)
        self.home = np.zeros(count, np.int32)
        for s in range(n_dp):
            for b in range(n_seq):
                source = b * n_dp + s
                if planes:
                    px, pz, pc = b & 1, (b >> 1) & 1, ((b >> 2) ^ (b >> 1) ^ b) & 1
                    dev = (s & 1) * 16 + pz * 8 + px * 4 + (s >> 1) * 2 + pc
                    g, r = px * 2 + pz, pc
                else:
                    dev = source
                    low = b % (2 * self.parts)
                    r = min(low, 2 * self.parts - 1 - low)
                    g = 2 * (b // (2 * self.parts)) + int(low >= self.parts)
                self.home[source] = dev
                self.seq_of[dev], self.blk_of[dev] = s, b
                self.grp_of[dev], self.part_of[dev] = g, r
        self.dev_at = {
            (int(self.seq_of[i]), int(self.grp_of[i]), int(self.part_of[i])): i for i in range(count)
        }
        if planes:
            self.core, self.near, self.far = (0,), ((2,), (1,)), (3, 4)
        else:
            self.core, self.near, self.far = (0,), ((2, 1), (3,)), tuple(range(4, self.n_bits))
        blocks = np.zeros((count, GROUPS * self.parts), np.int32)
        lists = []
        for i in range(count):
            s, g, r = int(self.seq_of[i]), int(self.grp_of[i]), int(self.part_of[i])
            for mr in range(self.parts):
                for m in range(GROUPS):
                    blocks[i, mr * GROUPS + m] = self.blk_of[self.dev_at[(s, g ^ m, r ^ mr)]]
            pairs = [
                (qs, ks)
                for qs in range(GROUPS)
                for ks in range(GROUPS * self.parts)
                if blocks[i, ks] <= blocks[i, qs]
            ]
            lists.append(
                [p for p in pairs if p[0] != p[1]] + [p for p in pairs if p[0] == p[1]]
            )
        self.n_pairs = len(lists[0])
        self.blocks = blocks
        self.pairs = np.array(lists, np.int32).transpose(0, 2, 1)

    def bit_perm(self, bit):
        return [(i, i ^ (1 << bit)) for i in range(self.size)]

    def group_perm(self, mg, mr):
        out = []
        for i in range(self.size):
            s, g, r = int(self.seq_of[i]), int(self.grp_of[i]), int(self.part_of[i])
            out.append((i, self.dev_at[(s, g ^ mg, r ^ mr)]))
        return out

    def home_perm(self):
        return [(i, int(self.home[i])) for i in range(self.size)]

    def back_perm(self):
        return [(int(self.home[i]), i) for i in range(self.size)]


def layer_norm(values, gain_vec, shift_vec):
    centre = values - jnp.mean(values, axis=-1, keepdims=True)
    spread = jnp.mean(centre * centre, axis=-1, keepdims=True)
    return centre * lax.rsqrt(spread + NORM_EPS) * gain_vec + shift_vec


def adamw(weight, grad, first, second, average, rate, decay):
    first_new = BETA_ONE * first + (1.0 - BETA_ONE) * grad
    second_new = BETA_TWO * second + (1.0 - BETA_TWO) * grad * grad
    unbiased_one = first_new / (1.0 - BETA_ONE**STEP)
    unbiased_two = second_new / (1.0 - BETA_TWO**STEP)
    weight_new = weight - rate * (
        unbiased_one / (jnp.sqrt(unbiased_two) + ADAM_EPS) + decay * weight
    )
    average_new = AVERAGE * average + (1.0 - AVERAGE) * weight_new
    return (weight_new, first_new, second_new, average_new)


def mm(a, b, dims):
    return lax.dot_general(a, b, dims, preferred_element_type=F32)


LOG2E = 1.4426950408889634
TILE = 256
PLAIN_LIMIT, PLAIN_TOP = 90.0, 30.0


def seen(diagonal, rows, cols, qplace, kplace, low, high):
    qi = lax.broadcasted_iota(jnp.int32, (1, cols), 1) + qplace
    opening = jnp.where(qi >= high, high, jnp.where(qi >= low, low, 0)) - kplace
    ki = lax.broadcasted_iota(jnp.int32, (rows, cols), 0)
    ok = ki >= opening
    if diagonal:
        ok = ok & (ki <= (qi - kplace))
    return ok


def each_pair(info, pos, n_pairs, rows, count, work):
    def run(first, steps, size, diagonal):
        def step(p, carried):
            pairs = []
            for u in range(size):
                qs, ks = info[0, first + p * size + u], info[1, first + p * size + u]
                pairs.append((qs, ks, pos[qs] * rows, pos[ks] * rows))
            work(diagonal, pairs)
            return carried

        lax.fori_loop(0, steps, step, 0)

    plain = n_pairs - GROUPS
    run(0, plain // count, count, False)
    if plain % count:
        run(plain - plain % count, 1, plain % count, False)
    run(plain, GROUPS // count, count, True)


def tiles_of(rows, diagonal, size):
    return [
        (u, c, j)
        for u in range(size)
        for j in range(0, rows, TILE)
        for c in range(0, rows, TILE)
        if not (diagonal and j >= c + TILE)
    ]


def forward_kernel(parts, n_pairs, info, pos, lim, *refs):
    own = refs[:GROUPS]
    other = refs[GROUPS : GROUPS + parts - 1]
    o_ref, ob_ref, l_ref, q_s, k_s, v_s, m_s, z_s, n_s = refs[GROUPS + parts - 1 :]
    rows = o_ref.shape[2]
    low, high = lim[0], lim[1]
    q_top = jnp.zeros((1, rows), F32)
    k_top = jnp.zeros((1, rows), F32)

    def squares(a):
        a = a.astype(F32)
        return jnp.sum(a * a, axis=0, keepdims=True)

    for j in range(GROUPS):
        q_s[j] = own[j][0, 0]
        v_s[j] = own[j][0, 2]
        k_s[j] = own[j][0, 1].T
        q_top = jnp.maximum(q_top, squares(own[j][0, 0]))
        k_top = jnp.maximum(k_top, squares(own[j][0, 1]))
    for p in range(parts - 1):
        for j in range(GROUPS):
            at = (p + 1) * GROUPS + j
            v_s[at] = other[p][j, 0, 1]
            k_s[at] = other[p][j, 0, 0].T
            k_top = jnp.maximum(k_top, squares(other[p][j, 0, 0]))
    z_s[...] = jnp.zeros(z_s.shape, F32)
    n_s[...] = jnp.zeros(n_s.shape, F32)
    top = jnp.sqrt(jnp.max(q_top, keepdims=True) * jnp.max(k_top, keepdims=True) + 1.0)
    base = jnp.maximum(top - PLAIN_TOP, 0.0)
    base_two = base * LOG2E
    plain = jnp.max(top) <= PLAIN_LIMIT

    def work_plain(diagonal, pairs):
        tiles = tiles_of(rows, diagonal, len(pairs))

        def score(tile):
            u, c, j = tile
            qs, ks, _, _ = pairs[u]
            return mm(k_s[ks, pl.ds(j, TILE)], q_s[qs, :, pl.ds(c, TILE)], NN)

        totals, sums = {}, {}
        ahead = [score(tile) for tile in tiles[:2]]
        for at, (u, c, j) in enumerate(tiles):
            if at + 2 < len(tiles):
                ahead.append(score(tiles[at + 2]))
            s = ahead[at]
            ahead[at] = None
            qs, ks, qplace, kplace = pairs[u]
            x = s * s + 1.0
            r = lax.rsqrt(x)
            e = jnp.exp2(x * r * LOG2E - base_two)
            ok = seen(diagonal and j == c, TILE, TILE, qplace + c, kplace + j, low, high)
            e = jnp.where(ok, e, 0.0)
            w = (e * (s * r)).astype(BF16)
            z = jnp.sum(e, axis=0, keepdims=True)
            n = mm(v_s[ks, :, pl.ds(j, TILE)], w, NN)
            totals[u, c] = totals[u, c] + z if (u, c) in totals else z
            sums[u, c] = sums[u, c] + n if (u, c) in sums else n
        for u, c in totals:
            qs = pairs[u][0]
            z_s[qs, :, pl.ds(c, TILE)] += totals[u, c]
            n_s[qs, :, pl.ds(c, TILE)] += sums[u, c]

    def work_running(diagonal, pairs):
        for qs, ks, qplace, kplace in pairs:
            s = mm(k_s[ks], q_s[qs], NN)
            x = s * s + 1.0
            r = lax.rsqrt(x)
            ok = seen(diagonal, rows, rows, qplace, kplace, low, high)
            m = jnp.where(ok, x * r, MASKED_LOW)
            m_old = m_s[qs]
            m_new = jnp.maximum(m_old, jnp.max(m, axis=0, keepdims=True))
            fade = jnp.exp(m_old - m_new)
            e = jnp.exp(m - jnp.maximum(m_new, 0.0))
            w = (e * (s * r)).astype(BF16)
            z_s[qs] = z_s[qs] * fade + jnp.sum(e, axis=0, keepdims=True)
            n_s[qs] = n_s[qs] * fade + mm(v_s[ks], w, NN)
            m_s[qs] = m_new

    @pl.when(plain)
    def _():
        m_s[...] = jnp.broadcast_to(base, m_s.shape)
        each_pair(info, pos, n_pairs, rows, 2, work_plain)

    @pl.when(jnp.logical_not(plain))
    def _():
        m_s[...] = jnp.full(m_s.shape, MASKED_LOW, F32)
        each_pair(info, pos, n_pairs, rows, 1, work_running)

    for j in range(GROUPS):
        z = z_s[j]
        o = n_s[j] * (1.0 / z)
        o_ref[j] = o
        ob_ref[j] = o.astype(BF16)
        l_ref[j] = m_s[j] + jnp.log(z)


def backward_kernel(parts, n_pairs, scale, info, pos, lim, *refs):
    own = refs[:GROUPS]
    other = refs[GROUPS : GROUPS + parts - 1]
    refs = refs[GROUPS + parts - 1 :]
    dob = refs[:GROUPS]
    o_ref, l_ref = refs[GROUPS : GROUPS + 2]
    refs = refs[GROUPS + 2 :]
    dq_ref, dkv_ref = refs[:2]
    dkv_other = refs[2 : 1 + parts]
    q_s, kt_s, k_s, v_s, do_s, l_s, d_s, dq_s, dk_s, dv_s = refs[1 + parts :]
    rows = o_ref.shape[2]
    low, high = lim[0], lim[1]
    for j in range(GROUPS):
        q_s[j] = own[j][0, 0]
        kt_s[j] = own[j][0, 1]
        do_s[j] = dob[j][0]
        k_s[j] = own[j][0, 1].T
        v_s[j] = own[j][0, 2].T
        d_s[j] = jnp.sum(dob[j][0].astype(F32) * o_ref[j], axis=0, keepdims=True)
        l_s[j] = l_ref[j] * LOG2E
    for p in range(parts - 1):
        for j in range(GROUPS):
            at = (p + 1) * GROUPS + j
            kt_s[at] = other[p][j, 0, 0]
            k_s[at] = other[p][j, 0, 0].T
            v_s[at] = other[p][j, 0, 1].T
    dq_s[...] = jnp.zeros(dq_s.shape, F32)
    dk_s[...] = jnp.zeros(dk_s.shape, F32)
    dv_s[...] = jnp.zeros(dv_s.shape, F32)

    def work(diagonal, pairs):
        tiles = tiles_of(rows, diagonal, len(pairs))

        def score(tile):
            u, c, j = tile
            qs, ks, _, _ = pairs[u]
            keys, cols = pl.ds(j, TILE), pl.ds(c, TILE)
            return (
                mm(k_s[ks, keys], q_s[qs, :, cols], NN),
                mm(v_s[ks, keys], do_s[qs, :, cols], NN),
            )

        dqs, dks, dvs = {}, {}, {}

        def add(sums, key, value):
            sums[key] = sums[key] + value if key in sums else value

        ahead = [score(tile) for tile in tiles[:2]]
        for at, (u, c, j) in enumerate(tiles):
            if at + 2 < len(tiles):
                ahead.append(score(tiles[at + 2]))
            s, gw = ahead[at]
            ahead[at] = None
            qs, ks, qplace, kplace = pairs[u]
            keys, cols = pl.ds(j, TILE), pl.ds(c, TILE)
            x = s * s + 1.0
            r = lax.rsqrt(x)
            prob = jnp.exp2(x * r * LOG2E - l_s[qs, :, cols])
            ok = seen(diagonal and j == c, TILE, TILE, qplace + c, kplace + j, low, high)
            prob = jnp.where(ok, prob, 0.0)
            pt = prob * (s * r)
            gs = prob * (gw * (1.0 - r * r * (1.0 - r))) - pt * d_s[qs, :, cols]
            gs_low, pt_low = gs.astype(BF16), pt.astype(BF16)
            add(dvs, (u, j), mm(do_s[qs, :, cols], pt_low, NT))
            add(dks, (u, j), mm(q_s[qs, :, cols], gs_low, NT))
            add(dqs, (u, c), mm(kt_s[ks, :, keys], gs_low, NN))
        for u, j in dvs:
            ks = pairs[u][1]
            dv_s[ks, :, pl.ds(j, TILE)] += dvs[u, j]
            dk_s[ks, :, pl.ds(j, TILE)] += dks[u, j]
        for u, c in dqs:
            dq_s[pairs[u][0], :, pl.ds(c, TILE)] += dqs[u, c]

    each_pair(info, pos, n_pairs, rows, 2, work)
    for j in range(GROUPS):
        dq_ref[j] = (dq_s[j] * scale).astype(BF16)
        dkv_ref[j, 0] = dk_s[j]
        dkv_ref[j, 1] = dv_s[j]
        for p in range(parts - 1):
            dkv_other[p][j, 0] = dk_s[(p + 1) * GROUPS + j].astype(BF16)
            dkv_other[p][j, 1] = dv_s[(p + 1) * GROUPS + j].astype(BF16)


SMEM_SPEC = pl.BlockSpec(memory_space=pltpu.SMEM)
KERNEL_VMEM = 56 * 2**20


def whole(shape):
    return pl.BlockSpec(shape, lambda i: (0,) * len(shape))


def head_of(h, shape, axis):
    place = tuple(h if k == axis else 0 for k in range(len(shape)))
    return pl.BlockSpec(tuple(1 if k == axis else n for k, n in enumerate(shape)), lambda i: place)


def attend(lay, tables, h, own, other):
    rows = own[0].shape[3]
    slots = GROUPS * lay.parts
    shape = jax.ShapeDtypeStruct
    return pl.pallas_call(
        partial(forward_kernel, lay.parts, lay.n_pairs),
        grid=(1,),
        out_shape=(
            shape((GROUPS, DH, rows), F32),
            shape((GROUPS, DH, rows), BF16),
            shape((GROUPS, 1, rows), F32),
        ),
        in_specs=[SMEM_SPEC] * 3
        + [head_of(h, a.shape, 0) for a in own]
        + [head_of(h, a.shape, 1) for a in other],
        out_specs=(whole((GROUPS, DH, rows)), whole((GROUPS, DH, rows)), whole((GROUPS, 1, rows))),
        scratch_shapes=[
            pltpu.VMEM((GROUPS, DH, rows), BF16),
            pltpu.VMEM((slots, rows, DH), BF16),
            pltpu.VMEM((slots, DH, rows), BF16),
            pltpu.VMEM((GROUPS, 1, rows), F32),
            pltpu.VMEM((GROUPS, 1, rows), F32),
            pltpu.VMEM((GROUPS, DH, rows), F32),
        ],
        compiler_params=pltpu.CompilerParams(vmem_limit_bytes=KERNEL_VMEM),
        cost_estimate=pl.CostEstimate(
            flops=4 * lay.n_pairs * rows * rows * DH,
            bytes_accessed=2 * (slots + GROUPS) * 3 * DH * rows,
            transcendentals=2 * lay.n_pairs * rows * rows,
        ),
        name="attend",
    )(*tables, *own, *other)


def attend_back(lay, tables, h, own, other, dob_head, dob, o, lse):
    rows = own[0].shape[3]
    slots = GROUPS * lay.parts
    shape = jax.ShapeDtypeStruct
    kv = (GROUPS, 2, DH, rows)
    return pl.pallas_call(
        partial(backward_kernel, lay.parts, lay.n_pairs, DH**-0.5),
        grid=(1,),
        out_shape=(shape((GROUPS, DH, rows), BF16), shape(kv, F32))
        + (shape(kv, BF16),) * (lay.parts - 1),
        in_specs=[SMEM_SPEC] * 3
        + [head_of(h, a.shape, 0) for a in own]
        + [head_of(h, a.shape, 1) for a in other]
        + [head_of(dob_head, a.shape, 0) for a in dob]
        + [whole(o.shape), whole(lse.shape)],
        out_specs=(whole((GROUPS, DH, rows)), whole(kv)) + (whole(kv),) * (lay.parts - 1),
        scratch_shapes=[
            pltpu.VMEM((GROUPS, DH, rows), BF16),
            pltpu.VMEM((slots, DH, rows), BF16),
            pltpu.VMEM((slots, rows, DH), BF16),
            pltpu.VMEM((slots, rows, DH), BF16),
            pltpu.VMEM((GROUPS, DH, rows), BF16),
            pltpu.VMEM((GROUPS, 1, rows), F32),
            pltpu.VMEM((GROUPS, 1, rows), F32),
            pltpu.VMEM((GROUPS, DH, rows), F32),
            pltpu.VMEM((slots, DH, rows), F32),
            pltpu.VMEM((slots, DH, rows), F32),
        ],
        compiler_params=pltpu.CompilerParams(vmem_limit_bytes=KERNEL_VMEM),
        cost_estimate=pl.CostEstimate(
            flops=10 * lay.n_pairs * rows * rows * DH,
            bytes_accessed=2 * (slots + GROUPS) * 5 * DH * rows,
            transcendentals=2 * lay.n_pairs * rows * rows,
        ),
        name="attend_back",
    )(*tables, *own, *other, *dob, o, lse)


TN = (((0,), (0,)), ((), ()))
GELU_ROOT, GELU_CUBE = 0.7978845608028654, 0.044715


def feed_forward_kernel(
    slab, core_bit, hn_ref, dy_ref, up, packed, y_ref, dhn_ref, *refs
):
    width = up.shape[0]
    g_s, du_s, down = refs[-3:]
    places = [
        (i, b)
        for i in range(packed.shape[0] // slab)
        for b in range(packed.shape[1] // width)
    ]
    if len(places) == 1:
        down[...] = packed[...]
    else:
        cut = [
            packed[:, b * width : (b + 1) * width].astype(F32)
            for b in range(packed.shape[1] // width)
        ]
        for n, (i, b) in enumerate(places):
            if n % 2 == 0:
                pair = [cut[q][p * slab : (p + 1) * slab] for p, q in places[n : n + 2]]
                down[pl.ds(n * slab, 2 * slab)] = jnp.concatenate(pair, axis=0).astype(BF16)

    @pl.when(pl.program_id(0) == 0)
    def _():
        y_ref[...] = jnp.zeros(y_ref.shape, F32)
        dhn_ref[...] = jnp.zeros(dhn_ref.shape, F32)

    step = hn_ref.shape[0] // 2
    for k in range(2):
        part = pl.ds(k * step, step)
        u = mm(hn_ref[part], up[...], NN)
        dg = mm(dy_ref[part], down[...], NT)
        square = u * u
        th = jnp.tanh(u * (GELU_ROOT + (GELU_ROOT * GELU_CUBE) * square))
        half = 0.5 + 0.5 * th
        slope = half + (0.5 * u) * (1.0 - th * th) * (
            GELU_ROOT + (3.0 * GELU_ROOT * GELU_CUBE) * square
        )
        g_s[part] = (u * half).astype(BF16)
        du_s[part] = (slope * dg).astype(BF16)
        y_ref[part] += mm(g_s[part], down[...], NN)
        dhn_ref[part] += mm(du_s[part], up[...], NT)
    gdown = mm(g_s[...], dy_ref[...], TN)
    gup = mm(hn_ref[...], du_s[...], TN)
    if len(places) == 1:
        gdown_ref, gup_ref = refs[:2]
        gdown_ref[...] = gdown
        gup_ref[...] = gup
        return
    gdown_keep, gdown_give, gup_keep, gup_give = refs[:4]
    lower = core_bit[0] == 0

    def sort_out(slabs, keep_ref, give_ref, cols):
        for n in range(0, len(slabs), 4):
            even, odd = (
                jnp.concatenate([slabs[n + k], slabs[n + 2 + k]], axis=0) for k in range(2)
            )
            at = pl.ds(n // 2 * slab, 2 * slab)
            keep_ref[at, cols] = jnp.where(lower, even, odd).astype(BF16)
            give_ref[at, cols] = jnp.where(lower, odd, even).astype(BF16)

    for b in range(packed.shape[1] // width):
        column = [gdown[n * slab : (n + 1) * slab] for n, at in enumerate(places) if at[1] == b]
        sort_out(column, gdown_keep, gdown_give, pl.ds(b * width, width))
    rows = [gup[n * slab : (n + 1) * slab] for n in range(width // slab)]
    sort_out(rows, gup_keep, gup_give, pl.ds(0, width))


def feed_forward(hn, dy, weights, slab, core_bit):
    rows, width = hn.shape
    tiles = weights.shape[1] // width // 2
    up_spec = pl.BlockSpec((width, width), lambda t: (0, t))
    if slab:
        down_spec = pl.BlockSpec((width // tiles, tiles * width), lambda t: (t, 0))
    else:
        down_spec = pl.BlockSpec((width, width), lambda t: (0, t))
    shape = jax.ShapeDtypeStruct
    full = pl.BlockSpec((rows, width), lambda t: (0, 0))
    if slab:
        half = width // 2
        grad_specs = [pl.BlockSpec((half // tiles, tiles * width), lambda t: (t, 0))] * 2
        grad_specs += [pl.BlockSpec((half, width), lambda t: (0, t))] * 2
        grad_shapes = [shape((half, tiles * width), BF16)] * 4
    else:
        grad_specs = [down_spec, up_spec]
        grad_shapes = [shape((width, tiles * width), F32)] * 2
    columns = pl.BlockSpec((width, width), lambda t: (0, t))
    return pl.pallas_call(
        partial(feed_forward_kernel, slab or width),
        grid=(tiles,),
        out_shape=(shape((rows, width), F32),) * 2 + tuple(grad_shapes),
        in_specs=[
            SMEM_SPEC,
            full,
            full,
            pl.BlockSpec((width, width), lambda t: (0, tiles + t)),
            down_spec,
        ],
        out_specs=(full, full) + tuple(grad_specs),
        scratch_shapes=[pltpu.VMEM((rows, width), BF16)] * 2 + [pltpu.VMEM((width, width), BF16)],
        compiler_params=pltpu.CompilerParams(vmem_limit_bytes=KERNEL_VMEM),
        cost_estimate=pl.CostEstimate(
            flops=12 * tiles * rows * width * width,
            bytes_accessed=12 * tiles * width * width,
            transcendentals=tiles * rows * width,
        ),
        name="feed_forward",
    )(core_bit, hn, dy, weights, weights)


def after(value, *others):
    return lax.optimization_barrier((value,) + others)[0]


def join(*values):
    return lax.optimization_barrier(values)


class Gather:
    def __init__(self, lay, index, shard):
        self.lay, self.index, self.rows, self.held = lay, index, shard.shape[0], shard
        self.bits, self.came, self.bit = (), None, None

    def start(self, bit, *others):
        if others:
            self.held = after(self.held, *others)
        self.bit = bit
        self.came = lax.ppermute(self.held, AXES, self.lay.bit_perm(bit))

    def finish(self, *others):
        came = after(self.came, *others) if others else self.came
        upper = ((self.index >> self.bit) & 1) == 1
        mine = self.held
        self.held = jnp.where(upper, jnp.stack([came, mine]), jnp.stack([mine, came]))
        self.bits = (self.bit,) + self.bits
        return self.held

    def step(self, bit, *others):
        self.start(bit, *others)
        return self.finish()

    def columns(self, start, stop):
        part = Gather(self.lay, self.index, self.held[..., start:stop])
        part.rows, part.bits = self.rows, self.bits
        return part

    def result(self):
        axes = tuple(self.bits.index(b) for b in sorted(self.bits, reverse=True))
        held = self.held.transpose(axes + tuple(range(len(axes), self.held.ndim)))
        return held.reshape((self.rows << len(axes),) + self.held.shape[len(axes) + 1 :])


class Scatter:
    def __init__(self, lay, index, arrays, left, kind=F32):
        self.lay, self.index, self.kind = lay, index, kind
        self.left = list(left)
        self.held, self.came, self.keep = list(arrays), None, None

    def start(self, bit, *others):
        if others:
            self.held = [after(h, *others) for h in self.held]
        axis = self.left.index(bit)
        self.left.pop(axis)
        mine = (self.index >> bit) & 1
        self.keep = [lax.dynamic_index_in_dim(h, mine, axis, keepdims=False) for h in self.held]
        give = [
            lax.dynamic_index_in_dim(h, 1 - mine, axis, keepdims=False).astype(BF16)
            for h in self.held
        ]
        give = jnp.concatenate(give, axis=-1) if len(give) > 1 else give[0]
        self.came = lax.ppermute(give, AXES, self.lay.bit_perm(bit))

    def finish(self, *others):
        came = after(self.came, *others) if others else self.came
        at, held = 0, []
        for keep in self.keep:
            total = keep.astype(F32) + came[..., at : at + keep.shape[-1]].astype(F32)
            held.append(total.astype(self.kind))
            at += keep.shape[-1]
        self.held = held
        return held

    def step(self, bit, *others):
        self.start(bit, *others)
        return self.finish()


def by_owner(array, n_bits):
    return array.reshape((2,) * n_bits + (array.shape[0] >> n_bits,) + array.shape[1:])


def unxor(items, mask):
    for bit in range((len(items) - 1).bit_length()):
        on = ((mask >> bit) & 1) == 1
        items = [jnp.where(on, items[k ^ (1 << bit)], items[k]) for k in range(len(items))]
    return items


def per_device(
    lay,
    tokens,
    cotangent,
    bounds,
    w_qkv,
    w_out,
    w_up,
    w_down,
    w_norms,
    m_qkv,
    m_out,
    m_up,
    m_down,
    m_norms,
    v_qkv,
    v_out,
    v_up,
    v_down,
    v_norms,
    a_qkv,
    a_out,
    a_up,
    a_down,
    a_norms,
):
    rows, width = tokens.shape[1], tokens.shape[2]
    n_heads = width // DH
    nh = n_heads // GROUPS
    index = lax.axis_index("seq") * lay.n_dp + lax.axis_index("dp")
    group = jnp.asarray(lay.grp_of)[index]
    blocks = jnp.asarray(lay.blocks)[index]
    pairs = jnp.asarray(lay.pairs)[index]

    if lay.moves:
        to_home = partial(lax.ppermute, axis_name=AXES, perm=lay.home_perm())
        to_owner = partial(lax.ppermute, axis_name=AXES, perm=lay.back_perm())
    else:
        to_home = to_owner = lambda v: v

    def to_groups(items):
        return [items[0]] + [
            lax.ppermute(items[m], AXES, lay.group_perm(m, 0)) for m in range(1, GROUPS)
        ]

    def for_group(array, axis, m):
        return lax.dynamic_index_in_dim(array, group ^ m, axis, keepdims=False)

    def across(array, mr):
        return lax.ppermute(array, AXES, lay.group_perm(0, mr))

    def by_head(shard):
        cut = shard.reshape(-1, 3, GROUPS, nh, DH).transpose(0, 3, 1, 2, 4)
        return cut.reshape(shard.shape)

    def from_by_head(shard):
        cut = shard.reshape(-1, nh, 3, GROUPS, DH).transpose(0, 2, 3, 1, 4)
        return cut.reshape(shard.shape)

    far, core = lay.far, lay.core

    def across_cores(array):
        return lax.ppermute(array, AXES, lay.bit_perm(core[0]))

    near_a = lay.near[0] + lay.near[1]
    near_b = lay.near[1] + lay.near[0]

    pad = jnp.zeros((w_qkv.shape[0], 128 - w_norms.shape[0]), BF16)
    low_qkv = by_head(w_qkv.astype(BF16))
    half = (3 * width // 2) // 128 * 128
    gather = Gather(
        lay, index, jnp.concatenate([low_qkv, w_norms.T.astype(BF16), pad], axis=1)
    )
    gather.start(far[-1])
    limits, gather.came = join(to_home(bounds[0]), gather.came)
    gather.finish()
    tokens_here = to_home(after(tokens[0], gather.held))
    tables = (pairs, blocks, limits)
    for bit in reversed(far[:-1]):
        gather.step(bit)
    gather_a, gather_b = gather.columns(0, half), gather.columns(half, 3 * width + 128)
    for bit_a, bit_b in zip(near_a, near_b):
        gather_a.start(bit_a)
        gather_b.start(bit_b)
        gather_a.finish()
        gather_b.finish()
    for bit in core:
        gather_a.start(bit)
        gather_b.start(bit)
        gather_a.finish()
        gather_b.finish()
    full_a, full_b = gather_a.result(), gather_b.result()
    qkv_full = jnp.concatenate([full_a, full_b[:, : 3 * width - half]], axis=1)
    gain_rows = full_b[:, 3 * width - half : 3 * width - half + 4].astype(F32).T

    own_rows, tiles = w_up.shape[0], w_up.shape[1] // width
    slab = own_rows if own_rows % 8 == 0 else 0

    def by_tile(shard):
        return shard if slab else shard.reshape(-1, width, tiles).swapaxes(1, 2).reshape(shard.shape)

    def from_by_tile(shard):
        return shard if slab else shard.reshape(-1, tiles, width).swapaxes(1, 2).reshape(shard.shape)

    def pack(shard):
        if slab:
            shard = jnp.swapaxes(shard.reshape(tiles, own_rows, width), 0, 1)
        return shard.reshape(own_rows, tiles * width)

    def unpack(shard):
        if slab:
            shard = jnp.swapaxes(shard.reshape(own_rows, tiles, width), 0, 1)
        return shard.reshape(tiles * own_rows, width)

    rest = jnp.concatenate(
        [pack(w_down.astype(BF16)), by_tile(w_up.astype(BF16)), w_out.astype(BF16)], axis=1
    )
    inputs = tokens_here.astype(F32)
    normed, first_pull = jax.vjp(layer_norm, inputs, gain_rows[0], gain_rows[1])
    normed_low = normed.astype(BF16)
    mixed = lax.dot_general(
        qkv_full, normed_low, (((0,), (1,)), ((), ())), preferred_element_type=F32
    ).astype(BF16)
    mixed = mixed.reshape(nh, 3, GROUPS, DH, rows)
    mixed = jnp.concatenate([mixed[:, :1] * jnp.asarray(DH**-0.5, BF16), mixed[:, 1:]], axis=1)

    def spread(cut):
        return to_groups([for_group(cut, 2, m) for m in range(GROUPS)])

    def both_parts(own):
        kv = jnp.stack([piece[:, 1:] for piece in own])
        return [across(kv, mr) for mr in range(1, lay.parts)]

    first_own = spread(mixed[:1])
    later_own = spread(after(mixed[1:], *first_own))
    rest_full = lax.all_gather(after(rest, *first_own), AXES, axis=0, tiled=True)
    out_full = rest_full[:, 2 * tiles * width :]
    first_other = both_parts(first_own)
    heads = [(0, first_own, first_other)]
    saved = [attend(lay, tables, *heads[0])]
    saved[0], later_own = join(saved[0], later_own)
    later_other = both_parts(later_own)
    for h in range(nh - 1):
        heads.append((h, later_own, later_other))
    grad_out = to_home(after(cotangent[0], saved[0][1]))
    saved.append(attend(lay, tables, *heads[1]))
    saved[1], grad_out = join(saved[1], grad_out)
    first_pieces = [jnp.stack([saved[h][1][m] for h in range(2)]) for m in range(GROUPS)]
    att_back = to_groups(first_pieces)
    own = [after(later_own[0], *first_pieces)] + later_own[1:]
    saved.append(attend(lay, tables, 1, own, later_other))
    saved[2], att_back = join(saved[2], att_back)
    last_pieces = to_groups([saved[2][1][m : m + 1] for m in range(GROUPS)])
    att_low = jnp.concatenate(
        [jnp.stack(unxor(att_back, group)), jnp.stack(unxor(last_pieces, group))], axis=1
    ).reshape(width, rows)

    branch = lax.dot_general(
        att_low, out_full, (((0,), (0,)), ((), ())), preferred_element_type=F32
    )
    resid_sum = inputs + branch
    hidden_norm, second_pull = jax.vjp(layer_norm, resid_sum, gain_rows[2], gain_rows[3])
    hidden_low = hidden_norm.astype(BF16)
    y, dhn, *ff_grads = feed_forward(
        hidden_low, grad_out, rest_full, slab, (index & 1).astype(jnp.int32).reshape(1)
    )
    result_low = (resid_sum + y).astype(BF16)
    descending = list(reversed(range(lay.n_bits)))
    if slab:
        down_keep, down_give, up_keep, up_give = ff_grads
    else:
        cut = [by_owner(a, lay.n_bits) for a in ff_grads]
        axis = lay.n_bits - 1
        pick = partial(lax.dynamic_index_in_dim, axis=axis, keepdims=False)
        down_keep, up_keep = (pick(a, index & 1) for a in cut)
        down_give, up_give = (pick(a, 1 - (index & 1)).astype(BF16) for a in cut)

    down_came, up_came = across_cores(down_give), across_cores(up_give)

    def after_cores(keep, came):
        total = (keep.astype(F32) + came.astype(F32)).astype(BF16)
        return by_owner(total.reshape(-1, total.shape[-1]), lay.n_bits - 1)

    back_resid, grad_gain2, grad_shift2 = second_pull(dhn)
    grad_resid = grad_out.astype(F32) + back_resid
    grad_branch = grad_resid.astype(BF16)
    dob = lax.dot_general(
        out_full, grad_branch, (((1,), (1,)), ((), ())), preferred_element_type=F32
    ).astype(BF16)
    dob = dob.reshape(GROUPS, nh, DH, rows)
    dob_pieces = to_groups([for_group(dob, 0, m) for m in range(GROUPS)])
    grad_wout = lax.dot_general(
        att_low, grad_branch, (((1,), (0,)), ((), ())), preferred_element_type=F32
    )
    scatter_out = Scatter(lay, index, [by_owner(grad_wout, lay.n_bits)], descending, BF16)
    scatter_out.step(core[0])
    scatter_d = Scatter(lay, index, [after_cores(down_keep, down_came)], scatter_out.left, BF16)
    scatter_c = Scatter(
        lay, index, [scatter_out.held[0], after_cores(up_keep, up_came)], scatter_out.left, BF16
    )
    for bit in core[1:]:
        scatter_d.step(bit)
        scatter_c.step(bit)
    scatter_d.start(near_b[0])
    scatter_c.start(near_a[0], *dob_pieces)

    def back(h, *others):
        pieces = [after(dob_pieces[0], *others)] + dob_pieces[1:]
        return attend_back(lay, tables, *heads[h], h, pieces, saved[h][0], saved[h][2])

    def share(grads):
        return [across(grads[1 + mr], mr) for mr in range(1, lay.parts)]

    def summed_pieces(grads, came):
        total = grads[1]
        for piece in came:
            total = total + piece.astype(F32)
        low = total.astype(BF16)
        return [jnp.concatenate([grads[0][m][None], low[m]], axis=0) for m in range(GROUPS)]

    def rejoin(pieces):
        return jnp.stack(unxor(pieces, group), axis=1).reshape(3 * width // nh, rows)

    first = back(0, *scatter_c.held, *scatter_d.held)
    first, scatter_c.came, scatter_d.came = join(first, scatter_c.came, scatter_d.came)
    shared = share(first)
    scatter_d.finish()
    scatter_c.finish()
    for bit_a, bit_b in zip(near_a[1:-1], near_b[1:-1]):
        scatter_c.step(bit_a)
        scatter_d.step(bit_b)
    second = back(1, *scatter_c.held, *scatter_d.held)
    scatter_d.start(near_b[-1])
    scatter_c.start(near_a[-1])
    layer_out = to_owner(after(result_low[None], *scatter_c.held, *scatter_d.held))
    second, shared, scatter_c.came, scatter_d.came, layer_out = join(
        second, shared, scatter_c.came, scatter_d.came, layer_out
    )
    scatter_d.finish()
    scatter_c.finish()
    shared_two = share(second)
    scatter_d.start(far[0])
    scatter_c.start(far[0])
    pieces = [
        jnp.stack(pair)
        for pair in zip(summed_pieces(first, shared), summed_pieces(second, shared_two))
    ]
    returned_two = to_groups(pieces)
    third = back(2, *scatter_c.held, *scatter_d.held, *pieces)
    third, returned_two, scatter_c.came, scatter_d.came = join(
        third, returned_two, scatter_c.came, scatter_d.came
    )
    returned = [[piece[h] for piece in returned_two] for h in range(2)]
    shared = share(third)
    scatter_d.finish()
    scatter_c.finish()
    for bit in far[1:-1]:
        scatter_c.step(bit)
        scatter_d.step(bit)
    scatter_d.start(far[-1])
    scatter_c.start(far[-1])
    returned.append(to_groups(summed_pieces(third, shared)))
    mixed_grads = [rejoin(pieces) for pieces in returned]
    mixed_grad = jnp.concatenate(mixed_grads, axis=0)

    def weight_grad(piece):
        return lax.dot_general(
            normed_low, piece, (((0,), (1,)), ((), ())), preferred_element_type=F32
        )

    grad_normed = lax.dot_general(
        mixed_grad, qkv_full, (((0,), (1,)), ((), ())), preferred_element_type=F32
    )
    back_input, grad_gain1, grad_shift1 = first_pull(grad_normed)
    grad_vec = jnp.stack([grad_gain1, grad_shift1, grad_gain2, grad_shift2]).T
    grad_vec = jnp.concatenate([grad_vec, jnp.zeros((width, 124), F32)], axis=1)
    wqkv_grads = [weight_grad(piece) for piece in mixed_grads]
    scatter = Scatter(
        lay, index, [by_owner(a, lay.n_bits) for a in wqkv_grads + [grad_vec]], descending
    )
    for bit in core:
        scatter.step(bit)
    one, two, three, vec = scatter.held
    split = half - 3 * width // nh
    scatter_a = Scatter(lay, index, [one, two[..., :split]], scatter.left)
    scatter_b = Scatter(lay, index, [two[..., split:], three, vec], scatter.left)
    for bit_a, bit_b in zip(near_a, near_b):
        scatter_a.start(bit_a)
        scatter_b.start(bit_b)
        scatter_a.finish()
        scatter_b.finish()
    scatter = Scatter(lay, index, scatter_a.held + scatter_b.held, scatter_a.left)
    for bit in far:
        scatter.step(bit)
    input_low = to_owner(after((grad_resid + back_input).astype(BF16), *scatter.held))
    summed_down, summed_c = scatter_d.finish()[0], scatter_c.finish()
    summed_qkv = from_by_head(jnp.concatenate(scatter.held[:4], axis=1))
    summed_out, summed_up = summed_c[0].astype(F32), from_by_tile(summed_c[1].astype(F32))
    summed_down = unpack(summed_down.astype(F32))
    summed_norms = scatter.held[4][:, :4].T
    input_grad = input_low.astype(F32)[None]

    summed = (summed_qkv, summed_out, summed_up, summed_down, summed_norms)
    square = sum((jnp.sum(member * member) for member in summed))
    for bit in range(lay.n_bits):
        square = square + lax.ppermute(square, AXES, lay.bit_perm(bit))
    grad_norm = jnp.sqrt(square)
    factor = CLIP_NORM / jnp.maximum(grad_norm, CLIP_NORM)
    upd_qkv = adamw(w_qkv, summed_qkv * factor, m_qkv, v_qkv, a_qkv, RATE_MAT, WEIGHT_DECAY)
    upd_out = adamw(w_out, summed_out * factor, m_out, v_out, a_out, RATE_OUT, WEIGHT_DECAY)
    upd_up = adamw(w_up, summed_up * factor, m_up, v_up, a_up, RATE_MAT, WEIGHT_DECAY)
    upd_down = adamw(w_down, summed_down * factor, m_down, v_down, a_down, RATE_MAT, WEIGHT_DECAY)
    upd_norms = adamw(w_norms, summed_norms * factor, m_norms, v_norms, a_norms, RATE_VEC, 0.0)
    updates = (upd_qkv, upd_out, upd_up, upd_down, upd_norms)
    return (layer_out, input_grad, grad_norm) + tuple(u[k] for k in range(4) for u in updates)


def solution(mesh):
    lay = Layout(mesh.shape["seq"], mesh.shape["dp"])
    rows = P(AXES, None)
    vecs = P(None, AXES)
    state = (rows, rows, rows, rows, vecs)
    block = P("dp", "seq", None)
    return jax.shard_map(
        partial(per_device, lay),
        mesh=mesh,
        in_specs=(block, block, P("dp", None)) + state * 4,
        out_specs=(block, block, P()) + state * 4,
        check_vma=False,
    )
```

```python
from functools import partial

import jax
import jax.numpy as jnp
import numpy as np
from jax import lax
from jax.experimental import pallas as pl
from jax.experimental.pallas import tpu as pltpu
from jax.sharding import PartitionSpec as P

DH = 64
STEP = 5

NORM_EPS = 1e-05
CLIP_NORM = 1.0
RATE_MAT = 0.03
RATE_OUT = 0.15
RATE_VEC = 0.3
WEIGHT_DECAY = 0.1
BETA_ONE = 0.5
BETA_TWO = 0.5
ADAM_EPS = 1e-08
AVERAGE = 0.8
MASKED_LOW = -1e30

AXES = ("seq", "dp")
GROUPS = 4
F32 = jnp.float32
BF16 = jnp.bfloat16
NN = (((1,), (0,)), ((), ()))
NT = (((1,), (1,)), ((), ()))


class Layout:
    def __init__(self, n_seq, n_dp):
        self.n_seq, self.n_dp, self.size = n_seq, n_dp, n_seq * n_dp
        self.parts = n_seq // GROUPS
        self.n_bits = self.size.bit_length() - 1
        planes = n_seq == 8 and n_dp == 4
        self.moves = planes
        count = self.size
        self.seq_of = np.zeros(count, np.int32)
        self.blk_of = np.zeros(count, np.int32)
        self.grp_of = np.zeros(count, np.int32)
        self.part_of = np.zeros(count, np.int32)
        self.home = np.zeros(count, np.int32)
        for s in range(n_dp):
            for b in range(n_seq):
                source = b * n_dp + s
                if planes:
                    px, pz, pc = b & 1, (b >> 1) & 1, ((b >> 2) ^ (b >> 1) ^ b) & 1
                    dev = (s & 1) * 16 + pz * 8 + px * 4 + (s >> 1) * 2 + pc
                    g, r = px * 2 + pz, pc
                else:
                    dev = source
                    low = b % (2 * self.parts)
                    r = min(low, 2 * self.parts - 1 - low)
                    g = 2 * (b // (2 * self.parts)) + int(low >= self.parts)
                self.home[source] = dev
                self.seq_of[dev], self.blk_of[dev] = s, b
                self.grp_of[dev], self.part_of[dev] = g, r
        self.dev_at = {
            (int(self.seq_of[i]), int(self.grp_of[i]), int(self.part_of[i])): i for i in range(count)
        }
        if planes:
            self.core, self.near, self.far = (0,), ((2,), (1,)), (3, 4)
        else:
            self.core, self.near, self.far = (0,), ((2, 1), (3,)), tuple(range(4, self.n_bits))
        blocks = np.zeros((count, GROUPS * self.parts), np.int32)
        lists = []
        for i in range(count):
            s, g, r = int(self.seq_of[i]), int(self.grp_of[i]), int(self.part_of[i])
            for mr in range(self.parts):
                for m in range(GROUPS):
                    blocks[i, mr * GROUPS + m] = self.blk_of[self.dev_at[(s, g ^ m, r ^ mr)]]
            pairs = [
                (qs, ks)
                for qs in range(GROUPS)
                for ks in range(GROUPS * self.parts)
                if blocks[i, ks] <= blocks[i, qs]
            ]
            lists.append(
                [p for p in pairs if p[0] != p[1]] + [p for p in pairs if p[0] == p[1]]
            )
        self.n_pairs = len(lists[0])
        self.blocks = blocks
        self.pairs = np.array(lists, np.int32).transpose(0, 2, 1)

    def bit_perm(self, bit):
        return [(i, i ^ (1 << bit)) for i in range(self.size)]

    def group_perm(self, mg, mr):
        out = []
        for i in range(self.size):
            s, g, r = int(self.seq_of[i]), int(self.grp_of[i]), int(self.part_of[i])
            out.append((i, self.dev_at[(s, g ^ mg, r ^ mr)]))
        return out

    def home_perm(self):
        return [(i, int(self.home[i])) for i in range(self.size)]

    def back_perm(self):
        return [(int(self.home[i]), i) for i in range(self.size)]


def layer_norm(values, gain_vec, shift_vec):
    centre = values - jnp.mean(values, axis=-1, keepdims=True)
    spread = jnp.mean(centre * centre, axis=-1, keepdims=True)
    return centre * lax.rsqrt(spread + NORM_EPS) * gain_vec + shift_vec


def adamw(weight, grad, first, second, average, rate, decay):
    first_new = BETA_ONE * first + (1.0 - BETA_ONE) * grad
    second_new = BETA_TWO * second + (1.0 - BETA_TWO) * grad * grad
    unbiased_one = first_new / (1.0 - BETA_ONE**STEP)
    unbiased_two = second_new / (1.0 - BETA_TWO**STEP)
    weight_new = weight - rate * (
        unbiased_one / (jnp.sqrt(unbiased_two) + ADAM_EPS) + decay * weight
    )
    average_new = AVERAGE * average + (1.0 - AVERAGE) * weight_new
    return (weight_new, first_new, second_new, average_new)


def mm(a, b, dims):
    return lax.dot_general(a, b, dims, preferred_element_type=F32)


LOG2E = 1.4426950408889634
TILE = 256
PLAIN_LIMIT, PLAIN_TOP = 90.0, 30.0


def seen(diagonal, rows, cols, qplace, kplace, low, high):
    qi = lax.broadcasted_iota(jnp.int32, (1, cols), 1) + qplace
    opening = jnp.where(qi >= high, high, jnp.where(qi >= low, low, 0)) - kplace
    ki = lax.broadcasted_iota(jnp.int32, (rows, cols), 0)
    ok = ki >= opening
    if diagonal:
        ok = ok & (ki <= (qi - kplace))
    return ok


def each_pair(info, pos, n_pairs, rows, count, work):
    def run(first, steps, size, diagonal):
        def step(p, carried):
            pairs = []
            for u in range(size):
                qs, ks = info[0, first + p * size + u], info[1, first + p * size + u]
                pairs.append((qs, ks, pos[qs] * rows, pos[ks] * rows))
            work(diagonal, pairs)
            return carried

        lax.fori_loop(0, steps, step, 0)

    plain = n_pairs - GROUPS
    run(0, plain // count, count, False)
    if plain % count:
        run(plain - plain % count, 1, plain % count, False)
    run(plain, GROUPS // count, count, True)


def tiles_of(rows, diagonal, size):
    return [
        (u, c, j)
        for u in range(size)
        for j in range(0, rows, TILE)
        for c in range(0, rows, TILE)
        if not (diagonal and j >= c + TILE)
    ]


def forward_kernel(parts, n_pairs, info, pos, lim, *refs):
    own = refs[:GROUPS]
    other = refs[GROUPS : GROUPS + parts - 1]
    o_ref, ob_ref, l_ref, q_s, k_s, v_s, m_s, z_s, n_s = refs[GROUPS + parts - 1 :]
    rows = o_ref.shape[2]
    low, high = lim[0], lim[1]
    q_top = jnp.zeros((1, rows), F32)
    k_top = jnp.zeros((1, rows), F32)

    def squares(a):
        a = a.astype(F32)
        return jnp.sum(a * a, axis=0, keepdims=True)

    for j in range(GROUPS):
        q_s[j] = own[j][0, 0]
        v_s[j] = own[j][0, 2]
        k_s[j] = own[j][0, 1].T
        q_top = jnp.maximum(q_top, squares(own[j][0, 0]))
        k_top = jnp.maximum(k_top, squares(own[j][0, 1]))
    for p in range(parts - 1):
        for j in range(GROUPS):
            at = (p + 1) * GROUPS + j
            v_s[at] = other[p][j, 0, 1]
            k_s[at] = other[p][j, 0, 0].T
            k_top = jnp.maximum(k_top, squares(other[p][j, 0, 0]))
    z_s[...] = jnp.zeros(z_s.shape, F32)
    n_s[...] = jnp.zeros(n_s.shape, F32)
    top = jnp.sqrt(jnp.max(q_top, keepdims=True) * jnp.max(k_top, keepdims=True) + 1.0)
    base = jnp.maximum(top - PLAIN_TOP, 0.0)
    base_two = base * LOG2E
    plain = jnp.max(top) <= PLAIN_LIMIT

    def work_plain(diagonal, pairs):
        tiles = tiles_of(rows, diagonal, len(pairs))

        def score(tile):
            u, c, j = tile
            qs, ks, _, _ = pairs[u]
            return mm(k_s[ks, pl.ds(j, TILE)], q_s[qs, :, pl.ds(c, TILE)], NN)

        totals, sums = {}, {}
        ahead = [score(tile) for tile in tiles[:2]]
        for at, (u, c, j) in enumerate(tiles):
            if at + 2 < len(tiles):
                ahead.append(score(tiles[at + 2]))
            s = ahead[at]
            ahead[at] = None
            qs, ks, qplace, kplace = pairs[u]
            x = s * s + 1.0
            r = lax.rsqrt(x)
            e = jnp.exp2(x * r * LOG2E - base_two)
            ok = seen(diagonal and j == c, TILE, TILE, qplace + c, kplace + j, low, high)
            e = jnp.where(ok, e, 0.0)
            w = (e * (s * r)).astype(BF16)
            z = jnp.sum(e, axis=0, keepdims=True)
            n = mm(v_s[ks, :, pl.ds(j, TILE)], w, NN)
            totals[u, c] = totals[u, c] + z if (u, c) in totals else z
            sums[u, c] = sums[u, c] + n if (u, c) in sums else n
        for u, c in totals:
            qs = pairs[u][0]
            z_s[qs, :, pl.ds(c, TILE)] += totals[u, c]
            n_s[qs, :, pl.ds(c, TILE)] += sums[u, c]

    def work_running(diagonal, pairs):
        for qs, ks, qplace, kplace in pairs:
            s = mm(k_s[ks], q_s[qs], NN)
            x = s * s + 1.0
            r = lax.rsqrt(x)
            ok = seen(diagonal, rows, rows, qplace, kplace, low, high)
            m = jnp.where(ok, x * r, MASKED_LOW)
            m_old = m_s[qs]
            m_new = jnp.maximum(m_old, jnp.max(m, axis=0, keepdims=True))
            fade = jnp.exp(m_old - m_new)
            e = jnp.exp(m - jnp.maximum(m_new, 0.0))
            w = (e * (s * r)).astype(BF16)
            z_s[qs] = z_s[qs] * fade + jnp.sum(e, axis=0, keepdims=True)
            n_s[qs] = n_s[qs] * fade + mm(v_s[ks], w, NN)
            m_s[qs] = m_new

    @pl.when(plain)
    def _():
        m_s[...] = jnp.broadcast_to(base, m_s.shape)
        each_pair(info, pos, n_pairs, rows, 2, work_plain)

    @pl.when(jnp.logical_not(plain))
    def _():
        m_s[...] = jnp.full(m_s.shape, MASKED_LOW, F32)
        each_pair(info, pos, n_pairs, rows, 1, work_running)

    for j in range(GROUPS):
        z = z_s[j]
        o = n_s[j] * (1.0 / z)
        o_ref[j] = o
        ob_ref[j] = o.astype(BF16)
        l_ref[j] = m_s[j] + jnp.log(z)


def backward_kernel(parts, n_pairs, scale, info, pos, lim, *refs):
    own = refs[:GROUPS]
    other = refs[GROUPS : GROUPS + parts - 1]
    refs = refs[GROUPS + parts - 1 :]
    dob = refs[:GROUPS]
    o_ref, l_ref = refs[GROUPS : GROUPS + 2]
    refs = refs[GROUPS + 2 :]
    dq_ref, dkv_ref = refs[:2]
    dkv_other = refs[2 : 1 + parts]
    q_s, kt_s, k_s, v_s, do_s, l_s, d_s, dq_s, dk_s, dv_s = refs[1 + parts :]
    rows = o_ref.shape[2]
    low, high = lim[0], lim[1]
    for j in range(GROUPS):
        q_s[j] = own[j][0, 0]
        kt_s[j] = own[j][0, 1]
        do_s[j] = dob[j][0]
        k_s[j] = own[j][0, 1].T
        v_s[j] = own[j][0, 2].T
        d_s[j] = jnp.sum(dob[j][0].astype(F32) * o_ref[j], axis=0, keepdims=True)
        l_s[j] = l_ref[j] * LOG2E
    for p in range(parts - 1):
        for j in range(GROUPS):
            at = (p + 1) * GROUPS + j
            kt_s[at] = other[p][j, 0, 0]
            k_s[at] = other[p][j, 0, 0].T
            v_s[at] = other[p][j, 0, 1].T
    dq_s[...] = jnp.zeros(dq_s.shape, F32)
    dk_s[...] = jnp.zeros(dk_s.shape, F32)
    dv_s[...] = jnp.zeros(dv_s.shape, F32)

    def work(diagonal, pairs):
        tiles = tiles_of(rows, diagonal, len(pairs))

        def score(tile):
            u, c, j = tile
            qs, ks, _, _ = pairs[u]
            keys, cols = pl.ds(j, TILE), pl.ds(c, TILE)
            return (
                mm(k_s[ks, keys], q_s[qs, :, cols], NN),
                mm(v_s[ks, keys], do_s[qs, :, cols], NN),
            )

        dqs, dks, dvs = {}, {}, {}

        def add(sums, key, value):
            sums[key] = sums[key] + value if key in sums else value

        ahead = [score(tile) for tile in tiles[:2]]
        for at, (u, c, j) in enumerate(tiles):
            if at + 2 < len(tiles):
                ahead.append(score(tiles[at + 2]))
            s, gw = ahead[at]
            ahead[at] = None
            qs, ks, qplace, kplace = pairs[u]
            keys, cols = pl.ds(j, TILE), pl.ds(c, TILE)
            x = s * s + 1.0
            r = lax.rsqrt(x)
            prob = jnp.exp2(x * r * LOG2E - l_s[qs, :, cols])
            ok = seen(diagonal and j == c, TILE, TILE, qplace + c, kplace + j, low, high)
            prob = jnp.where(ok, prob, 0.0)
            pt = prob * (s * r)
            gs = prob * (gw * (1.0 - r * r * (1.0 - r))) - pt * d_s[qs, :, cols]
            gs_low, pt_low = gs.astype(BF16), pt.astype(BF16)
            add(dvs, (u, j), mm(do_s[qs, :, cols], pt_low, NT))
            add(dks, (u, j), mm(q_s[qs, :, cols], gs_low, NT))
            add(dqs, (u, c), mm(kt_s[ks, :, keys], gs_low, NN))
        for u, j in dvs:
            ks = pairs[u][1]
            dv_s[ks, :, pl.ds(j, TILE)] += dvs[u, j]
            dk_s[ks, :, pl.ds(j, TILE)] += dks[u, j]
        for u, c in dqs:
            dq_s[pairs[u][0], :, pl.ds(c, TILE)] += dqs[u, c]

    each_pair(info, pos, n_pairs, rows, 2, work)
    for j in range(GROUPS):
        dq_ref[j] = (dq_s[j] * scale).astype(BF16)
        dkv_ref[j, 0] = dk_s[j]
        dkv_ref[j, 1] = dv_s[j]
        for p in range(parts - 1):
            dkv_other[p][j, 0] = dk_s[(p + 1) * GROUPS + j].astype(BF16)
            dkv_other[p][j, 1] = dv_s[(p + 1) * GROUPS + j].astype(BF16)


SMEM_SPEC = pl.BlockSpec(memory_space=pltpu.SMEM)
KERNEL_VMEM = 56 * 2**20


def whole(shape):
    return pl.BlockSpec(shape, lambda i: (0,) * len(shape))


def head_of(h, shape, axis):
    place = tuple(h if k == axis else 0 for k in range(len(shape)))
    return pl.BlockSpec(tuple(1 if k == axis else n for k, n in enumerate(shape)), lambda i: place)


def attend(lay, tables, h, own, other):
    rows = own[0].shape[3]
    slots = GROUPS * lay.parts
    shape = jax.ShapeDtypeStruct
    return pl.pallas_call(
        partial(forward_kernel, lay.parts, lay.n_pairs),
        grid=(1,),
        out_shape=(
            shape((GROUPS, DH, rows), F32),
            shape((GROUPS, DH, rows), BF16),
            shape((GROUPS, 1, rows), F32),
        ),
        in_specs=[SMEM_SPEC] * 3
        + [head_of(h, a.shape, 0) for a in own]
        + [head_of(h, a.shape, 1) for a in other],
        out_specs=(whole((GROUPS, DH, rows)), whole((GROUPS, DH, rows)), whole((GROUPS, 1, rows))),
        scratch_shapes=[
            pltpu.VMEM((GROUPS, DH, rows), BF16),
            pltpu.VMEM((slots, rows, DH), BF16),
            pltpu.VMEM((slots, DH, rows), BF16),
            pltpu.VMEM((GROUPS, 1, rows), F32),
            pltpu.VMEM((GROUPS, 1, rows), F32),
            pltpu.VMEM((GROUPS, DH, rows), F32),
        ],
        compiler_params=pltpu.CompilerParams(vmem_limit_bytes=KERNEL_VMEM),
        cost_estimate=pl.CostEstimate(
            flops=4 * lay.n_pairs * rows * rows * DH,
            bytes_accessed=2 * (slots + GROUPS) * 3 * DH * rows,
            transcendentals=2 * lay.n_pairs * rows * rows,
        ),
        name="attend",
    )(*tables, *own, *other)


def attend_back(lay, tables, h, own, other, dob_head, dob, o, lse):
    rows = own[0].shape[3]
    slots = GROUPS * lay.parts
    shape = jax.ShapeDtypeStruct
    kv = (GROUPS, 2, DH, rows)
    return pl.pallas_call(
        partial(backward_kernel, lay.parts, lay.n_pairs, DH**-0.5),
        grid=(1,),
        out_shape=(shape((GROUPS, DH, rows), BF16), shape(kv, F32))
        + (shape(kv, BF16),) * (lay.parts - 1),
        in_specs=[SMEM_SPEC] * 3
        + [head_of(h, a.shape, 0) for a in own]
        + [head_of(h, a.shape, 1) for a in other]
        + [head_of(dob_head, a.shape, 0) for a in dob]
        + [whole(o.shape), whole(lse.shape)],
        out_specs=(whole((GROUPS, DH, rows)), whole(kv)) + (whole(kv),) * (lay.parts - 1),
        scratch_shapes=[
            pltpu.VMEM((GROUPS, DH, rows), BF16),
            pltpu.VMEM((slots, DH, rows), BF16),
            pltpu.VMEM((slots, rows, DH), BF16),
            pltpu.VMEM((slots, rows, DH), BF16),
            pltpu.VMEM((GROUPS, DH, rows), BF16),
            pltpu.VMEM((GROUPS, 1, rows), F32),
            pltpu.VMEM((GROUPS, 1, rows), F32),
            pltpu.VMEM((GROUPS, DH, rows), F32),
            pltpu.VMEM((slots, DH, rows), F32),
            pltpu.VMEM((slots, DH, rows), F32),
        ],
        compiler_params=pltpu.CompilerParams(vmem_limit_bytes=KERNEL_VMEM),
        cost_estimate=pl.CostEstimate(
            flops=10 * lay.n_pairs * rows * rows * DH,
            bytes_accessed=2 * (slots + GROUPS) * 5 * DH * rows,
            transcendentals=2 * lay.n_pairs * rows * rows,
        ),
        name="attend_back",
    )(*tables, *own, *other, *dob, o, lse)


TN = (((0,), (0,)), ((), ()))
GELU_ROOT, GELU_CUBE = 0.7978845608028654, 0.044715


def feed_forward_kernel(
    slab, core_bit, hn_ref, dy_ref, up, packed, y_ref, dhn_ref, *refs
):
    width = up.shape[0]
    g_s, du_s, down = refs[-3:]
    places = [
        (i, b)
        for i in range(packed.shape[0] // slab)
        for b in range(packed.shape[1] // width)
    ]
    if len(places) == 1:
        down[...] = packed[...]
    else:
        cut = [
            packed[:, b * width : (b + 1) * width].astype(F32)
            for b in range(packed.shape[1] // width)
        ]
        for n, (i, b) in enumerate(places):
            if n % 2 == 0:
                pair = [cut[q][p * slab : (p + 1) * slab] for p, q in places[n : n + 2]]
                down[pl.ds(n * slab, 2 * slab)] = jnp.concatenate(pair, axis=0).astype(BF16)

    @pl.when(pl.program_id(0) == 0)
    def _():
        y_ref[...] = jnp.zeros(y_ref.shape, F32)
        dhn_ref[...] = jnp.zeros(dhn_ref.shape, F32)

    step = hn_ref.shape[0]
    for k in range(1):
        part = pl.ds(k * step, step)
        u = mm(hn_ref[part], up[...], NN)
        dg = mm(dy_ref[part], down[...], NT)
        square = u * u
        th = jnp.tanh(u * (GELU_ROOT + (GELU_ROOT * GELU_CUBE) * square))
        half = 0.5 + 0.5 * th
        slope = half + (0.5 * u) * (1.0 - th * th) * (
            GELU_ROOT + (3.0 * GELU_ROOT * GELU_CUBE) * square
        )
        g_s[part] = (u * half).astype(BF16)
        du_s[part] = (slope * dg).astype(BF16)
        y_ref[part] += mm(g_s[part], down[...], NN)
        dhn_ref[part] += mm(du_s[part], up[...], NT)
    gdown = mm(g_s[...], dy_ref[...], TN)
    gup = mm(hn_ref[...], du_s[...], TN)
    if len(places) == 1:
        gdown_ref, gup_ref = refs[:2]
        gdown_ref[...] = gdown
        gup_ref[...] = gup
        return
    gdown_keep, gdown_give, gup_keep, gup_give = refs[:4]
    lower = core_bit[0] == 0

    def sort_out(slabs, keep_ref, give_ref, cols):
        for n in range(0, len(slabs), 4):
            even, odd = (
                jnp.concatenate([slabs[n + k], slabs[n + 2 + k]], axis=0) for k in range(2)
            )
            at = pl.ds(n // 2 * slab, 2 * slab)
            keep_ref[at, cols] = jnp.where(lower, even, odd).astype(BF16)
            give_ref[at, cols] = jnp.where(lower, odd, even).astype(BF16)

    for b in range(packed.shape[1] // width):
        column = [gdown[n * slab : (n + 1) * slab] for n, at in enumerate(places) if at[1] == b]
        sort_out(column, gdown_keep, gdown_give, pl.ds(b * width, width))
    rows = [gup[n * slab : (n + 1) * slab] for n in range(width // slab)]
    sort_out(rows, gup_keep, gup_give, pl.ds(0, width))


def feed_forward(hn, dy, weights, slab, core_bit):
    rows, width = hn.shape
    tiles = weights.shape[1] // width // 2
    up_spec = pl.BlockSpec((width, width), lambda t: (0, t))
    if slab:
        down_spec = pl.BlockSpec((width // tiles, tiles * width), lambda t: (t, 0))
    else:
        down_spec = pl.BlockSpec((width, width), lambda t: (0, t))
    shape = jax.ShapeDtypeStruct
    full = pl.BlockSpec((rows, width), lambda t: (0, 0))
    if slab:
        half = width // 2
        grad_specs = [pl.BlockSpec((half // tiles, tiles * width), lambda t: (t, 0))] * 2
        grad_specs += [pl.BlockSpec((half, width), lambda t: (0, t))] * 2
        grad_shapes = [shape((half, tiles * width), BF16)] * 4
    else:
        grad_specs = [down_spec, up_spec]
        grad_shapes = [shape((width, tiles * width), F32)] * 2
    columns = pl.BlockSpec((width, width), lambda t: (0, t))
    return pl.pallas_call(
        partial(feed_forward_kernel, slab or width),
        grid=(tiles,),
        out_shape=(shape((rows, width), F32),) * 2 + tuple(grad_shapes),
        in_specs=[
            SMEM_SPEC,
            full,
            full,
            pl.BlockSpec((width, width), lambda t: (0, tiles + t)),
            down_spec,
        ],
        out_specs=(full, full) + tuple(grad_specs),
        scratch_shapes=[pltpu.VMEM((rows, width), BF16)] * 2 + [pltpu.VMEM((width, width), BF16)],
        compiler_params=pltpu.CompilerParams(vmem_limit_bytes=KERNEL_VMEM),
        cost_estimate=pl.CostEstimate(
            flops=12 * tiles * rows * width * width,
            bytes_accessed=12 * tiles * width * width,
            transcendentals=tiles * rows * width,
        ),
        name="feed_forward",
    )(core_bit, hn, dy, weights, weights)


def after(value, *others):
    return lax.optimization_barrier((value,) + others)[0]


def join(*values):
    return lax.optimization_barrier(values)


class Gather:
    def __init__(self, lay, index, shard):
        self.lay, self.index, self.rows, self.held = lay, index, shard.shape[0], shard
        self.bits, self.came, self.bit = (), None, None

    def start(self, bit, *others):
        if others:
            self.held = after(self.held, *others)
        self.bit = bit
        self.came = lax.ppermute(self.held, AXES, self.lay.bit_perm(bit))

    def finish(self, *others):
        came = after(self.came, *others) if others else self.came
        upper = ((self.index >> self.bit) & 1) == 1
        mine = self.held
        self.held = jnp.where(upper, jnp.stack([came, mine]), jnp.stack([mine, came]))
        self.bits = (self.bit,) + self.bits
        return self.held

    def step(self, bit, *others):
        self.start(bit, *others)
        return self.finish()

    def columns(self, start, stop):
        part = Gather(self.lay, self.index, self.held[..., start:stop])
        part.rows, part.bits = self.rows, self.bits
        return part

    def result(self):
        axes = tuple(self.bits.index(b) for b in sorted(self.bits, reverse=True))
        held = self.held.transpose(axes + tuple(range(len(axes), self.held.ndim)))
        return held.reshape((self.rows << len(axes),) + self.held.shape[len(axes) + 1 :])


class Scatter:
    def __init__(self, lay, index, arrays, left, kind=F32):
        self.lay, self.index, self.kind = lay, index, kind
        self.left = list(left)
        self.held, self.came, self.keep = list(arrays), None, None

    def start(self, bit, *others):
        if others:
            self.held = [after(h, *others) for h in self.held]
        axis = self.left.index(bit)
        self.left.pop(axis)
        mine = (self.index >> bit) & 1
        self.keep = [lax.dynamic_index_in_dim(h, mine, axis, keepdims=False) for h in self.held]
        give = [
            lax.dynamic_index_in_dim(h, 1 - mine, axis, keepdims=False).astype(BF16)
            for h in self.held
        ]
        give = jnp.concatenate(give, axis=-1) if len(give) > 1 else give[0]
        self.came = lax.ppermute(give, AXES, self.lay.bit_perm(bit))

    def finish(self, *others):
        came = after(self.came, *others) if others else self.came
        at, held = 0, []
        for keep in self.keep:
            total = keep.astype(F32) + came[..., at : at + keep.shape[-1]].astype(F32)
            held.append(total.astype(self.kind))
            at += keep.shape[-1]
        self.held = held
        return held

    def step(self, bit, *others):
        self.start(bit, *others)
        return self.finish()


def by_owner(array, n_bits):
    return array.reshape((2,) * n_bits + (array.shape[0] >> n_bits,) + array.shape[1:])


def unxor(items, mask):
    for bit in range((len(items) - 1).bit_length()):
        on = ((mask >> bit) & 1) == 1
        items = [jnp.where(on, items[k ^ (1 << bit)], items[k]) for k in range(len(items))]
    return items


def per_device(
    lay,
    tokens,
    cotangent,
    bounds,
    w_qkv,
    w_out,
    w_up,
    w_down,
    w_norms,
    m_qkv,
    m_out,
    m_up,
    m_down,
    m_norms,
    v_qkv,
    v_out,
    v_up,
    v_down,
    v_norms,
    a_qkv,
    a_out,
    a_up,
    a_down,
    a_norms,
):
    rows, width = tokens.shape[1], tokens.shape[2]
    n_heads = width // DH
    nh = n_heads // GROUPS
    index = lax.axis_index("seq") * lay.n_dp + lax.axis_index("dp")
    group = jnp.asarray(lay.grp_of)[index]
    blocks = jnp.asarray(lay.blocks)[index]
    pairs = jnp.asarray(lay.pairs)[index]

    if lay.moves:
        to_home = partial(lax.ppermute, axis_name=AXES, perm=lay.home_perm())
        to_owner = partial(lax.ppermute, axis_name=AXES, perm=lay.back_perm())
    else:
        to_home = to_owner = lambda v: v

    def to_groups(items):
        return [items[0]] + [
            lax.ppermute(items[m], AXES, lay.group_perm(m, 0)) for m in range(1, GROUPS)
        ]

    def for_group(array, axis, m):
        return lax.dynamic_index_in_dim(array, group ^ m, axis, keepdims=False)

    def across(array, mr):
        return lax.ppermute(array, AXES, lay.group_perm(0, mr))

    def by_head(shard):
        cut = shard.reshape(-1, 3, GROUPS, nh, DH).transpose(0, 3, 1, 2, 4)
        return cut.reshape(shard.shape)

    def from_by_head(shard):
        cut = shard.reshape(-1, nh, 3, GROUPS, DH).transpose(0, 2, 3, 1, 4)
        return cut.reshape(shard.shape)

    far, core = lay.far, lay.core

    def across_cores(array):
        return lax.ppermute(array, AXES, lay.bit_perm(core[0]))

    near_a = lay.near[0] + lay.near[1]
    near_b = lay.near[1] + lay.near[0]

    pad = jnp.zeros((w_qkv.shape[0], 128 - w_norms.shape[0]), BF16)
    low_qkv = by_head(w_qkv.astype(BF16))
    half = (3 * width // 2) // 128 * 128
    gather = Gather(
        lay, index, jnp.concatenate([low_qkv, w_norms.T.astype(BF16), pad], axis=1)
    )
    gather.start(far[-1])
    limits, gather.came = join(to_home(bounds[0]), gather.came)
    gather.finish()
    tokens_here = to_home(after(tokens[0], gather.held))
    tables = (pairs, blocks, limits)
    for bit in reversed(far[:-1]):
        gather.step(bit)
    gather_a, gather_b = gather.columns(0, half), gather.columns(half, 3 * width + 128)
    for bit_a, bit_b in zip(near_a, near_b):
        gather_a.start(bit_a)
        gather_b.start(bit_b)
        gather_a.finish()
        gather_b.finish()
    for bit in core:
        gather_a.start(bit)
        gather_b.start(bit)
        gather_a.finish()
        gather_b.finish()
    full_a, full_b = gather_a.result(), gather_b.result()
    qkv_full = jnp.concatenate([full_a, full_b[:, : 3 * width - half]], axis=1)
    gain_rows = full_b[:, 3 * width - half : 3 * width - half + 4].astype(F32).T

    own_rows, tiles = w_up.shape[0], w_up.shape[1] // width
    slab = own_rows if own_rows % 8 == 0 else 0

    def by_tile(shard):
        return shard if slab else shard.reshape(-1, width, tiles).swapaxes(1, 2).reshape(shard.shape)

    def from_by_tile(shard):
        return shard if slab else shard.reshape(-1, tiles, width).swapaxes(1, 2).reshape(shard.shape)

    def pack(shard):
        if slab:
            shard = jnp.swapaxes(shard.reshape(tiles, own_rows, width), 0, 1)
        return shard.reshape(own_rows, tiles * width)

    def unpack(shard):
        if slab:
            shard = jnp.swapaxes(shard.reshape(own_rows, tiles, width), 0, 1)
        return shard.reshape(tiles * own_rows, width)

    rest = jnp.concatenate(
        [pack(w_down.astype(BF16)), by_tile(w_up.astype(BF16)), w_out.astype(BF16)], axis=1
    )
    inputs = tokens_here.astype(F32)
    normed, first_pull = jax.vjp(layer_norm, inputs, gain_rows[0], gain_rows[1])
    normed_low = normed.astype(BF16)
    mixed = lax.dot_general(
        qkv_full, normed_low, (((0,), (1,)), ((), ())), preferred_element_type=F32
    ).astype(BF16)
    mixed = mixed.reshape(nh, 3, GROUPS, DH, rows)
    mixed = jnp.concatenate([mixed[:, :1] * jnp.asarray(DH**-0.5, BF16), mixed[:, 1:]], axis=1)

    def spread(cut):
        return to_groups([for_group(cut, 2, m) for m in range(GROUPS)])

    def both_parts(own):
        kv = jnp.stack([piece[:, 1:] for piece in own])
        return [across(kv, mr) for mr in range(1, lay.parts)]

    first_own = spread(mixed[:1])
    later_own = spread(after(mixed[1:], *first_own))
    rest_full = lax.all_gather(after(rest, *first_own), AXES, axis=0, tiled=True)
    out_full = rest_full[:, 2 * tiles * width :]
    first_other = both_parts(first_own)
    heads = [(0, first_own, first_other)]
    saved = [attend(lay, tables, *heads[0])]
    saved[0], later_own = join(saved[0], later_own)
    later_other = both_parts(later_own)
    for h in range(nh - 1):
        heads.append((h, later_own, later_other))
    grad_out = to_home(after(cotangent[0], saved[0][1]))
    saved.append(attend(lay, tables, *heads[1]))
    saved[1], grad_out = join(saved[1], grad_out)
    saved.append(attend(lay, tables, *heads[2]))
    att_back = to_groups([jnp.stack([saved[h][1][m] for h in range(nh)]) for m in range(GROUPS)])
    att_low = jnp.stack(unxor(att_back, group)).reshape(width, rows)

    branch = lax.dot_general(
        att_low, out_full, (((0,), (0,)), ((), ())), preferred_element_type=F32
    )
    resid_sum = inputs + branch
    hidden_norm, second_pull = jax.vjp(layer_norm, resid_sum, gain_rows[2], gain_rows[3])
    hidden_low = hidden_norm.astype(BF16)
    y, dhn, *ff_grads = feed_forward(
        hidden_low, grad_out, rest_full, slab, (index & 1).astype(jnp.int32).reshape(1)
    )
    result_low = (resid_sum + y).astype(BF16)
    descending = list(reversed(range(lay.n_bits)))
    if slab:
        down_keep, down_give, up_keep, up_give = ff_grads
    else:
        cut = [by_owner(a, lay.n_bits) for a in ff_grads]
        axis = lay.n_bits - 1
        pick = partial(lax.dynamic_index_in_dim, axis=axis, keepdims=False)
        down_keep, up_keep = (pick(a, index & 1) for a in cut)
        down_give, up_give = (pick(a, 1 - (index & 1)).astype(BF16) for a in cut)

    down_came, up_came = across_cores(down_give), across_cores(up_give)

    def after_cores(keep, came):
        total = (keep.astype(F32) + came.astype(F32)).astype(BF16)
        return by_owner(total.reshape(-1, total.shape[-1]), lay.n_bits - 1)

    back_resid, grad_gain2, grad_shift2 = second_pull(dhn)
    grad_resid = grad_out.astype(F32) + back_resid
    grad_branch = grad_resid.astype(BF16)
    dob = lax.dot_general(
        out_full, grad_branch, (((1,), (1,)), ((), ())), preferred_element_type=F32
    ).astype(BF16)
    dob = dob.reshape(GROUPS, nh, DH, rows)
    dob_pieces = to_groups([for_group(dob, 0, m) for m in range(GROUPS)])
    grad_wout = lax.dot_general(
        att_low, grad_branch, (((1,), (0,)), ((), ())), preferred_element_type=F32
    )
    scatter_out = Scatter(lay, index, [by_owner(grad_wout, lay.n_bits)], descending, BF16)
    scatter_out.step(core[0])
    scatter_d = Scatter(lay, index, [after_cores(down_keep, down_came)], scatter_out.left, BF16)
    scatter_c = Scatter(
        lay, index, [scatter_out.held[0], after_cores(up_keep, up_came)], scatter_out.left, BF16
    )
    for bit in core[1:]:
        scatter_d.step(bit)
        scatter_c.step(bit)
    scatter_d.start(near_b[0])
    scatter_c.start(near_a[0], *dob_pieces)

    def back(h, *others):
        pieces = [after(dob_pieces[0], *others)] + dob_pieces[1:]
        return attend_back(lay, tables, *heads[h], h, pieces, saved[h][0], saved[h][2])

    def share(grads):
        return [across(grads[1 + mr], mr) for mr in range(1, lay.parts)]

    def summed_pieces(grads, came):
        total = grads[1]
        for piece in came:
            total = total + piece.astype(F32)
        low = total.astype(BF16)
        return [jnp.concatenate([grads[0][m][None], low[m]], axis=0) for m in range(GROUPS)]

    def rejoin(pieces):
        return jnp.stack(unxor(pieces, group), axis=1).reshape(3 * width // nh, rows)

    first = back(0, *scatter_c.held, *scatter_d.held)
    first, scatter_c.came, scatter_d.came = join(first, scatter_c.came, scatter_d.came)
    shared = share(first)
    scatter_d.finish()
    scatter_c.finish()
    for bit_a, bit_b in zip(near_a[1:-1], near_b[1:-1]):
        scatter_c.step(bit_a)
        scatter_d.step(bit_b)
    second = back(1, *scatter_c.held, *scatter_d.held)
    scatter_d.start(near_b[-1])
    scatter_c.start(near_a[-1])
    layer_out = to_owner(after(result_low[None], *scatter_c.held, *scatter_d.held))
    second, shared, scatter_c.came, scatter_d.came, layer_out = join(
        second, shared, scatter_c.came, scatter_d.came, layer_out
    )
    scatter_d.finish()
    scatter_c.finish()
    shared_two = share(second)
    scatter_d.start(far[0])
    scatter_c.start(far[0])
    pieces = [
        jnp.stack(pair)
        for pair in zip(summed_pieces(first, shared), summed_pieces(second, shared_two))
    ]
    returned_two = to_groups(pieces)
    third = back(2, *scatter_c.held, *scatter_d.held, *pieces)
    third, returned_two, scatter_c.came, scatter_d.came = join(
        third, returned_two, scatter_c.came, scatter_d.came
    )
    returned = [[piece[h] for piece in returned_two] for h in range(2)]
    shared = share(third)
    scatter_d.finish()
    scatter_c.finish()
    for bit in far[1:-1]:
        scatter_c.step(bit)
        scatter_d.step(bit)
    scatter_d.start(far[-1])
    scatter_c.start(far[-1])
    returned.append(to_groups(summed_pieces(third, shared)))
    mixed_grads = [rejoin(pieces) for pieces in returned]
    mixed_grad = jnp.concatenate(mixed_grads, axis=0)

    def weight_grad(piece):
        return lax.dot_general(
            normed_low, piece, (((0,), (1,)), ((), ())), preferred_element_type=F32
        )

    grad_normed = lax.dot_general(
        mixed_grad, qkv_full, (((0,), (1,)), ((), ())), preferred_element_type=F32
    )
    back_input, grad_gain1, grad_shift1 = first_pull(grad_normed)
    grad_vec = jnp.stack([grad_gain1, grad_shift1, grad_gain2, grad_shift2]).T
    grad_vec = jnp.concatenate([grad_vec, jnp.zeros((width, 124), F32)], axis=1)
    wqkv_grads = [weight_grad(piece) for piece in mixed_grads]
    scatter = Scatter(
        lay, index, [by_owner(a, lay.n_bits) for a in wqkv_grads + [grad_vec]], descending
    )
    for bit in core:
        scatter.step(bit)
    one, two, three, vec = scatter.held
    split = half - 3 * width // nh
    scatter_a = Scatter(lay, index, [one, two[..., :split]], scatter.left)
    scatter_b = Scatter(lay, index, [two[..., split:], three, vec], scatter.left)
    for bit_a, bit_b in zip(near_a, near_b):
        scatter_a.start(bit_a)
        scatter_b.start(bit_b)
        scatter_a.finish()
        scatter_b.finish()
    scatter = Scatter(lay, index, scatter_a.held + scatter_b.held, scatter_a.left)
    for bit in far:
        scatter.step(bit)
    input_low = to_owner(after((grad_resid + back_input).astype(BF16), *scatter.held))
    summed_down, summed_c = scatter_d.finish()[0], scatter_c.finish()
    summed_qkv = from_by_head(jnp.concatenate(scatter.held[:4], axis=1))
    summed_out, summed_up = summed_c[0].astype(F32), from_by_tile(summed_c[1].astype(F32))
    summed_down = unpack(summed_down.astype(F32))
    summed_norms = scatter.held[4][:, :4].T
    input_grad = input_low.astype(F32)[None]

    summed = (summed_qkv, summed_out, summed_up, summed_down, summed_norms)
    square = sum((jnp.sum(member * member) for member in summed))
    for bit in range(lay.n_bits):
        square = square + lax.ppermute(square, AXES, lay.bit_perm(bit))
    grad_norm = jnp.sqrt(square)
    factor = CLIP_NORM / jnp.maximum(grad_norm, CLIP_NORM)
    upd_qkv = adamw(w_qkv, summed_qkv * factor, m_qkv, v_qkv, a_qkv, RATE_MAT, WEIGHT_DECAY)
    upd_out = adamw(w_out, summed_out * factor, m_out, v_out, a_out, RATE_OUT, WEIGHT_DECAY)
    upd_up = adamw(w_up, summed_up * factor, m_up, v_up, a_up, RATE_MAT, WEIGHT_DECAY)
    upd_down = adamw(w_down, summed_down * factor, m_down, v_down, a_down, RATE_MAT, WEIGHT_DECAY)
    upd_norms = adamw(w_norms, summed_norms * factor, m_norms, v_norms, a_norms, RATE_VEC, 0.0)
    updates = (upd_qkv, upd_out, upd_up, upd_down, upd_norms)
    return (layer_out, input_grad, grad_norm) + tuple(u[k] for k in range(4) for u in updates)


def solution(mesh):
    lay = Layout(mesh.shape["seq"], mesh.shape["dp"])
    rows = P(AXES, None)
    vecs = P(None, AXES)
    state = (rows, rows, rows, rows, vecs)
    block = P("dp", "seq", None)
    return jax.shard_map(
        partial(per_device, lay),
        mesh=mesh,
        in_specs=(block, block, P("dp", None)) + state * 4,
        out_specs=(block, block, P()) + state * 4,
        check_vma=False,
    )
```

```python
from functools import partial

import jax
import jax.numpy as jnp
import numpy as np
from jax import lax
from jax.experimental import pallas as pl
from jax.experimental.pallas import tpu as pltpu
from jax.sharding import PartitionSpec as P

DH = 64
STEP = 5

NORM_EPS = 1e-05
CLIP_NORM = 1.0
RATE_MAT = 0.03
RATE_OUT = 0.15
RATE_VEC = 0.3
WEIGHT_DECAY = 0.1
BETA_ONE = 0.5
BETA_TWO = 0.5
ADAM_EPS = 1e-08
AVERAGE = 0.8
MASKED_LOW = -1e30

AXES = ("seq", "dp")
GROUPS = 4
F32 = jnp.float32
BF16 = jnp.bfloat16
NN = (((1,), (0,)), ((), ()))
NT = (((1,), (1,)), ((), ()))


class Layout:
    def __init__(self, n_seq, n_dp):
        self.n_seq, self.n_dp, self.size = n_seq, n_dp, n_seq * n_dp
        self.parts = n_seq // GROUPS
        self.n_bits = self.size.bit_length() - 1
        planes = n_seq == 8 and n_dp == 4
        self.moves = planes
        count = self.size
        self.seq_of = np.zeros(count, np.int32)
        self.blk_of = np.zeros(count, np.int32)
        self.grp_of = np.zeros(count, np.int32)
        self.part_of = np.zeros(count, np.int32)
        self.home = np.zeros(count, np.int32)
        for s in range(n_dp):
            for b in range(n_seq):
                source = b * n_dp + s
                if planes:
                    px, pz, pc = b & 1, (b >> 1) & 1, ((b >> 2) ^ (b >> 1) ^ b) & 1
                    dev = (s & 1) * 16 + pz * 8 + px * 4 + (s >> 1) * 2 + pc
                    g, r = px * 2 + pz, pc
                else:
                    dev = source
                    low = b % (2 * self.parts)
                    r = min(low, 2 * self.parts - 1 - low)
                    g = 2 * (b // (2 * self.parts)) + int(low >= self.parts)
                self.home[source] = dev
                self.seq_of[dev], self.blk_of[dev] = s, b
                self.grp_of[dev], self.part_of[dev] = g, r
        self.dev_at = {
            (int(self.seq_of[i]), int(self.grp_of[i]), int(self.part_of[i])): i for i in range(count)
        }
        if planes:
            self.core, self.near, self.far = (0,), ((2,), (1,)), (3, 4)
        else:
            self.core, self.near, self.far = (0,), ((2, 1), (3,)), tuple(range(4, self.n_bits))
        blocks = np.zeros((count, GROUPS * self.parts), np.int32)
        lists = []
        for i in range(count):
            s, g, r = int(self.seq_of[i]), int(self.grp_of[i]), int(self.part_of[i])
            for mr in range(self.parts):
                for m in range(GROUPS):
                    blocks[i, mr * GROUPS + m] = self.blk_of[self.dev_at[(s, g ^ m, r ^ mr)]]
            pairs = [
                (qs, ks)
                for qs in range(GROUPS)
                for ks in range(GROUPS * self.parts)
                if blocks[i, ks] <= blocks[i, qs]
            ]
            lists.append(
                [p for p in pairs if p[0] != p[1]] + [p for p in pairs if p[0] == p[1]]
            )
        self.n_pairs = len(lists[0])
        self.blocks = blocks
        self.pairs = np.array(lists, np.int32).transpose(0, 2, 1)

    def bit_perm(self, bit):
        return [(i, i ^ (1 << bit)) for i in range(self.size)]

    def group_perm(self, mg, mr):
        out = []
        for i in range(self.size):
            s, g, r = int(self.seq_of[i]), int(self.grp_of[i]), int(self.part_of[i])
            out.append((i, self.dev_at[(s, g ^ mg, r ^ mr)]))
        return out

    def home_perm(self):
        return [(i, int(self.home[i])) for i in range(self.size)]

    def back_perm(self):
        return [(int(self.home[i]), i) for i in range(self.size)]


def layer_norm(values, gain_vec, shift_vec):
    centre = values - jnp.mean(values, axis=-1, keepdims=True)
    spread = jnp.mean(centre * centre, axis=-1, keepdims=True)
    return centre * lax.rsqrt(spread + NORM_EPS) * gain_vec + shift_vec


def adamw(weight, grad, first, second, average, rate, decay):
    first_new = BETA_ONE * first + (1.0 - BETA_ONE) * grad
    second_new = BETA_TWO * second + (1.0 - BETA_TWO) * grad * grad
    unbiased_one = first_new / (1.0 - BETA_ONE**STEP)
    unbiased_two = second_new / (1.0 - BETA_TWO**STEP)
    weight_new = weight - rate * (
        unbiased_one / (jnp.sqrt(unbiased_two) + ADAM_EPS) + decay * weight
    )
    average_new = AVERAGE * average + (1.0 - AVERAGE) * weight_new
    return (weight_new, first_new, second_new, average_new)


def mm(a, b, dims):
    return lax.dot_general(a, b, dims, preferred_element_type=F32)


LOG2E = 1.4426950408889634
TILE = 256
PLAIN_LIMIT, PLAIN_TOP = 90.0, 30.0


def seen(diagonal, rows, cols, qplace, kplace, low, high):
    qi = lax.broadcasted_iota(jnp.int32, (1, cols), 1) + qplace
    opening = jnp.where(qi >= high, high, jnp.where(qi >= low, low, 0)) - kplace
    ki = lax.broadcasted_iota(jnp.int32, (rows, cols), 0)
    ok = ki >= opening
    if diagonal:
        ok = ok & (ki <= (qi - kplace))
    return ok


def each_pair(info, pos, n_pairs, rows, count, work):
    def run(first, steps, size, diagonal):
        def step(p, carried):
            pairs = []
            for u in range(size):
                qs, ks = info[0, first + p * size + u], info[1, first + p * size + u]
                pairs.append((qs, ks, pos[qs] * rows, pos[ks] * rows))
            work(diagonal, pairs)
            return carried

        lax.fori_loop(0, steps, step, 0)

    plain = n_pairs - GROUPS
    run(0, plain // count, count, False)
    if plain % count:
        run(plain - plain % count, 1, plain % count, False)
    run(plain, GROUPS // count, count, True)


def tiles_of(rows, diagonal, size):
    return [
        (u, c, j)
        for u in range(size)
        for j in range(0, rows, TILE)
        for c in range(0, rows, TILE)
        if not (diagonal and j >= c + TILE)
    ]


def forward_kernel(parts, n_pairs, info, pos, lim, *refs):
    own = refs[:GROUPS]
    other = refs[GROUPS : GROUPS + parts - 1]
    o_ref, ob_ref, l_ref, q_s, k_s, v_s, m_s, z_s, n_s = refs[GROUPS + parts - 1 :]
    rows = o_ref.shape[2]
    low, high = lim[0], lim[1]
    q_top = jnp.zeros((1, rows), F32)
    k_top = jnp.zeros((1, rows), F32)

    def squares(a):
        a = a.astype(F32)
        return jnp.sum(a * a, axis=0, keepdims=True)

    for j in range(GROUPS):
        q_s[j] = own[j][0, 0]
        v_s[j] = own[j][0, 2]
        k_s[j] = own[j][0, 1].T
        q_top = jnp.maximum(q_top, squares(own[j][0, 0]))
        k_top = jnp.maximum(k_top, squares(own[j][0, 1]))
    for p in range(parts - 1):
        for j in range(GROUPS):
            at = (p + 1) * GROUPS + j
            v_s[at] = other[p][j, 0, 1]
            k_s[at] = other[p][j, 0, 0].T
            k_top = jnp.maximum(k_top, squares(other[p][j, 0, 0]))
    z_s[...] = jnp.zeros(z_s.shape, F32)
    n_s[...] = jnp.zeros(n_s.shape, F32)
    top = jnp.sqrt(jnp.max(q_top, keepdims=True) * jnp.max(k_top, keepdims=True) + 1.0)
    base = jnp.maximum(top - PLAIN_TOP, 0.0)
    base_two = base * LOG2E
    plain = jnp.max(top) <= PLAIN_LIMIT

    def work_plain(diagonal, pairs):
        tiles = tiles_of(rows, diagonal, len(pairs))

        def score(tile):
            u, c, j = tile
            qs, ks, _, _ = pairs[u]
            return mm(k_s[ks, pl.ds(j, TILE)], q_s[qs, :, pl.ds(c, TILE)], NN)

        totals, sums = {}, {}
        ahead = [score(tile) for tile in tiles[:2]]
        for at, (u, c, j) in enumerate(tiles):
            if at + 2 < len(tiles):
                ahead.append(score(tiles[at + 2]))
            s = ahead[at]
            ahead[at] = None
            qs, ks, qplace, kplace = pairs[u]
            x = s * s + 1.0
            r = lax.rsqrt(x)
            e = jnp.exp2(x * r * LOG2E - base_two)
            ok = seen(diagonal and j == c, TILE, TILE, qplace + c, kplace + j, low, high)
            e = jnp.where(ok, e, 0.0)
            w = (e * (s * r)).astype(BF16)
            z = jnp.sum(e, axis=0, keepdims=True)
            n = mm(v_s[ks, :, pl.ds(j, TILE)], w, NN)
            totals[u, c] = totals[u, c] + z if (u, c) in totals else z
            sums[u, c] = sums[u, c] + n if (u, c) in sums else n
        for u, c in totals:
            qs = pairs[u][0]
            z_s[qs, :, pl.ds(c, TILE)] += totals[u, c]
            n_s[qs, :, pl.ds(c, TILE)] += sums[u, c]

    def work_running(diagonal, pairs):
        for qs, ks, qplace, kplace in pairs:
            s = mm(k_s[ks], q_s[qs], NN)
            x = s * s + 1.0
            r = lax.rsqrt(x)
            ok = seen(diagonal, rows, rows, qplace, kplace, low, high)
            m = jnp.where(ok, x * r, MASKED_LOW)
            m_old = m_s[qs]
            m_new = jnp.maximum(m_old, jnp.max(m, axis=0, keepdims=True))
            fade = jnp.exp(m_old - m_new)
            e = jnp.exp(m - jnp.maximum(m_new, 0.0))
            w = (e * (s * r)).astype(BF16)
            z_s[qs] = z_s[qs] * fade + jnp.sum(e, axis=0, keepdims=True)
            n_s[qs] = n_s[qs] * fade + mm(v_s[ks], w, NN)
            m_s[qs] = m_new

    @pl.when(plain)
    def _():
        m_s[...] = jnp.broadcast_to(base, m_s.shape)
        each_pair(info, pos, n_pairs, rows, 2, work_plain)

    @pl.when(jnp.logical_not(plain))
    def _():
        m_s[...] = jnp.full(m_s.shape, MASKED_LOW, F32)
        each_pair(info, pos, n_pairs, rows, 1, work_running)

    for j in range(GROUPS):
        z = z_s[j]
        o = n_s[j] * (1.0 / z)
        o_ref[j] = o
        ob_ref[j] = o.astype(BF16)
        l_ref[j] = m_s[j] + jnp.log(z)


def backward_kernel(parts, n_pairs, scale, info, pos, lim, *refs):
    own = refs[:GROUPS]
    other = refs[GROUPS : GROUPS + parts - 1]
    refs = refs[GROUPS + parts - 1 :]
    dob = refs[:GROUPS]
    o_ref, l_ref = refs[GROUPS : GROUPS + 2]
    refs = refs[GROUPS + 2 :]
    dq_ref, dkv_ref = refs[:2]
    dkv_other = refs[2 : 1 + parts]
    q_s, kt_s, k_s, v_s, do_s, l_s, d_s, dq_s, dk_s, dv_s = refs[1 + parts :]
    rows = o_ref.shape[2]
    low, high = lim[0], lim[1]
    for j in range(GROUPS):
        q_s[j] = own[j][0, 0]
        kt_s[j] = own[j][0, 1]
        do_s[j] = dob[j][0]
        k_s[j] = own[j][0, 1].T
        v_s[j] = own[j][0, 2].T
        d_s[j] = jnp.sum(dob[j][0].astype(F32) * o_ref[j], axis=0, keepdims=True)
        l_s[j] = l_ref[j] * LOG2E
    for p in range(parts - 1):
        for j in range(GROUPS):
            at = (p + 1) * GROUPS + j
            kt_s[at] = other[p][j, 0, 0]
            k_s[at] = other[p][j, 0, 0].T
            v_s[at] = other[p][j, 0, 1].T
    dq_s[...] = jnp.zeros(dq_s.shape, F32)
    dk_s[...] = jnp.zeros(dk_s.shape, F32)
    dv_s[...] = jnp.zeros(dv_s.shape, F32)

    def work(diagonal, pairs):
        tiles = tiles_of(rows, diagonal, len(pairs))

        def score(tile):
            u, c, j = tile
            qs, ks, _, _ = pairs[u]
            keys, cols = pl.ds(j, TILE), pl.ds(c, TILE)
            return (
                mm(k_s[ks, keys], q_s[qs, :, cols], NN),
                mm(v_s[ks, keys], do_s[qs, :, cols], NN),
            )

        dqs, dks, dvs = {}, {}, {}

        def add(sums, key, value):
            sums[key] = sums[key] + value if key in sums else value

        ahead = [score(tile) for tile in tiles[:2]]
        for at, (u, c, j) in enumerate(tiles):
            if at + 2 < len(tiles):
                ahead.append(score(tiles[at + 2]))
            s, gw = ahead[at]
            ahead[at] = None
            qs, ks, qplace, kplace = pairs[u]
            keys, cols = pl.ds(j, TILE), pl.ds(c, TILE)
            x = s * s + 1.0
            r = lax.rsqrt(x)
            prob = jnp.exp2(x * r * LOG2E - l_s[qs, :, cols])
            ok = seen(diagonal and j == c, TILE, TILE, qplace + c, kplace + j, low, high)
            prob = jnp.where(ok, prob, 0.0)
            pt = prob * (s * r)
            gs = prob * (gw * (1.0 - r * r * (1.0 - r))) - pt * d_s[qs, :, cols]
            gs_low, pt_low = gs.astype(BF16), pt.astype(BF16)
            add(dvs, (u, j), mm(do_s[qs, :, cols], pt_low, NT))
            add(dks, (u, j), mm(q_s[qs, :, cols], gs_low, NT))
            add(dqs, (u, c), mm(kt_s[ks, :, keys], gs_low, NN))
        for u, j in dvs:
            ks = pairs[u][1]
            dv_s[ks, :, pl.ds(j, TILE)] += dvs[u, j]
            dk_s[ks, :, pl.ds(j, TILE)] += dks[u, j]
        for u, c in dqs:
            dq_s[pairs[u][0], :, pl.ds(c, TILE)] += dqs[u, c]

    each_pair(info, pos, n_pairs, rows, 2, work)
    for j in range(GROUPS):
        dq_ref[j] = (dq_s[j] * scale).astype(BF16)
        dkv_ref[j, 0] = dk_s[j]
        dkv_ref[j, 1] = dv_s[j]
        for p in range(parts - 1):
            dkv_other[p][j, 0] = dk_s[(p + 1) * GROUPS + j].astype(BF16)
            dkv_other[p][j, 1] = dv_s[(p + 1) * GROUPS + j].astype(BF16)


SMEM_SPEC = pl.BlockSpec(memory_space=pltpu.SMEM)
KERNEL_VMEM = 56 * 2**20


def whole(shape):
    return pl.BlockSpec(shape, lambda i: (0,) * len(shape))


def head_of(h, shape, axis):
    place = tuple(h if k == axis else 0 for k in range(len(shape)))
    return pl.BlockSpec(tuple(1 if k == axis else n for k, n in enumerate(shape)), lambda i: place)


def attend(lay, tables, h, own, other):
    rows = own[0].shape[3]
    slots = GROUPS * lay.parts
    shape = jax.ShapeDtypeStruct
    return pl.pallas_call(
        partial(forward_kernel, lay.parts, lay.n_pairs),
        grid=(1,),
        out_shape=(
            shape((GROUPS, DH, rows), F32),
            shape((GROUPS, DH, rows), BF16),
            shape((GROUPS, 1, rows), F32),
        ),
        in_specs=[SMEM_SPEC] * 3
        + [head_of(h, a.shape, 0) for a in own]
        + [head_of(h, a.shape, 1) for a in other],
        out_specs=(whole((GROUPS, DH, rows)), whole((GROUPS, DH, rows)), whole((GROUPS, 1, rows))),
        scratch_shapes=[
            pltpu.VMEM((GROUPS, DH, rows), BF16),
            pltpu.VMEM((slots, rows, DH), BF16),
            pltpu.VMEM((slots, DH, rows), BF16),
            pltpu.VMEM((GROUPS, 1, rows), F32),
            pltpu.VMEM((GROUPS, 1, rows), F32),
            pltpu.VMEM((GROUPS, DH, rows), F32),
        ],
        compiler_params=pltpu.CompilerParams(vmem_limit_bytes=KERNEL_VMEM),
        cost_estimate=pl.CostEstimate(
            flops=4 * lay.n_pairs * rows * rows * DH,
            bytes_accessed=2 * (slots + GROUPS) * 3 * DH * rows,
            transcendentals=2 * lay.n_pairs * rows * rows,
        ),
        name="attend",
    )(*tables, *own, *other)


def attend_back(lay, tables, h, own, other, dob_head, dob, o, lse):
    rows = own[0].shape[3]
    slots = GROUPS * lay.parts
    shape = jax.ShapeDtypeStruct
    kv = (GROUPS, 2, DH, rows)
    return pl.pallas_call(
        partial(backward_kernel, lay.parts, lay.n_pairs, DH**-0.5),
        grid=(1,),
        out_shape=(shape((GROUPS, DH, rows), BF16), shape(kv, F32))
        + (shape(kv, BF16),) * (lay.parts - 1),
        in_specs=[SMEM_SPEC] * 3
        + [head_of(h, a.shape, 0) for a in own]
        + [head_of(h, a.shape, 1) for a in other]
        + [head_of(dob_head, a.shape, 0) for a in dob]
        + [whole(o.shape), whole(lse.shape)],
        out_specs=(whole((GROUPS, DH, rows)), whole(kv)) + (whole(kv),) * (lay.parts - 1),
        scratch_shapes=[
            pltpu.VMEM((GROUPS, DH, rows), BF16),
            pltpu.VMEM((slots, DH, rows), BF16),
            pltpu.VMEM((slots, rows, DH), BF16),
            pltpu.VMEM((slots, rows, DH), BF16),
            pltpu.VMEM((GROUPS, DH, rows), BF16),
            pltpu.VMEM((GROUPS, 1, rows), F32),
            pltpu.VMEM((GROUPS, 1, rows), F32),
            pltpu.VMEM((GROUPS, DH, rows), F32),
            pltpu.VMEM((slots, DH, rows), F32),
            pltpu.VMEM((slots, DH, rows), F32),
        ],
        compiler_params=pltpu.CompilerParams(vmem_limit_bytes=KERNEL_VMEM),
        cost_estimate=pl.CostEstimate(
            flops=10 * lay.n_pairs * rows * rows * DH,
            bytes_accessed=2 * (slots + GROUPS) * 5 * DH * rows,
            transcendentals=2 * lay.n_pairs * rows * rows,
        ),
        name="attend_back",
    )(*tables, *own, *other, *dob, o, lse)


TN = (((0,), (0,)), ((), ()))
GELU_ROOT, GELU_CUBE = 0.7978845608028654, 0.044715


def feed_forward_kernel(
    slab, core_bit, hn_ref, dy_ref, up, packed, y_ref, dhn_ref, *refs
):
    width = up.shape[0]
    g_s, du_s, down = refs[-3:]
    places = [
        (i, b)
        for i in range(packed.shape[0] // slab)
        for b in range(packed.shape[1] // width)
    ]
    if len(places) == 1:
        down[...] = packed[...]
    else:
        cut = [
            packed[:, b * width : (b + 1) * width].astype(F32)
            for b in range(packed.shape[1] // width)
        ]
        for n, (i, b) in enumerate(places):
            if n % 2 == 0:
                pair = [cut[q][p * slab : (p + 1) * slab] for p, q in places[n : n + 2]]
                down[pl.ds(n * slab, 2 * slab)] = jnp.concatenate(pair, axis=0).astype(BF16)

    @pl.when(pl.program_id(0) == 0)
    def _():
        y_ref[...] = jnp.zeros(y_ref.shape, F32)
        dhn_ref[...] = jnp.zeros(dhn_ref.shape, F32)

    step = hn_ref.shape[0]
    for k in range(1):
        part = pl.ds(k * step, step)
        u = mm(hn_ref[part], up[...], NN)
        dg = mm(dy_ref[part], down[...], NT)
        square = u * u
        th = jnp.tanh(u * (GELU_ROOT + (GELU_ROOT * GELU_CUBE) * square))
        half = 0.5 + 0.5 * th
        slope = half + (0.5 * u) * (1.0 - th * th) * (
            GELU_ROOT + (3.0 * GELU_ROOT * GELU_CUBE) * square
        )
        g_s[part] = (u * half).astype(BF16)
        du_s[part] = (slope * dg).astype(BF16)
        y_ref[part] += mm(g_s[part], down[...], NN)
        dhn_ref[part] += mm(du_s[part], up[...], NT)
    gdown = mm(g_s[...], dy_ref[...], TN)
    gup = mm(hn_ref[...], du_s[...], TN)
    if len(places) == 1:
        gdown_ref, gup_ref = refs[:2]
        gdown_ref[...] = gdown
        gup_ref[...] = gup
        return
    gdown_keep, gdown_give, gup_keep, gup_give = refs[:4]
    lower = core_bit[0] == 0

    def sort_out(slabs, keep_ref, give_ref, cols):
        for n in range(0, len(slabs), 4):
            even, odd = (
                jnp.concatenate([slabs[n + k], slabs[n + 2 + k]], axis=0) for k in range(2)
            )
            at = pl.ds(n // 2 * slab, 2 * slab)
            keep_ref[at, cols] = jnp.where(lower, even, odd).astype(BF16)
            give_ref[at, cols] = jnp.where(lower, odd, even).astype(BF16)

    for b in range(packed.shape[1] // width):
        column = [gdown[n * slab : (n + 1) * slab] for n, at in enumerate(places) if at[1] == b]
        sort_out(column, gdown_keep, gdown_give, pl.ds(b * width, width))
    rows = [gup[n * slab : (n + 1) * slab] for n in range(width // slab)]
    sort_out(rows, gup_keep, gup_give, pl.ds(0, width))


def feed_forward(hn, dy, weights, slab, core_bit):
    rows, width = hn.shape
    tiles = weights.shape[1] // width // 2
    up_spec = pl.BlockSpec((width, width), lambda t: (0, t))
    if slab:
        down_spec = pl.BlockSpec((width // tiles, tiles * width), lambda t: (t, 0))
    else:
        down_spec = pl.BlockSpec((width, width), lambda t: (0, t))
    shape = jax.ShapeDtypeStruct
    full = pl.BlockSpec((rows, width), lambda t: (0, 0))
    if slab:
        half = width // 2
        grad_specs = [pl.BlockSpec((half // tiles, tiles * width), lambda t: (t, 0))] * 2
        grad_specs += [pl.BlockSpec((half, width), lambda t: (0, t))] * 2
        grad_shapes = [shape((half, tiles * width), BF16)] * 4
    else:
        grad_specs = [down_spec, up_spec]
        grad_shapes = [shape((width, tiles * width), F32)] * 2
    columns = pl.BlockSpec((width, width), lambda t: (0, t))
    return pl.pallas_call(
        partial(feed_forward_kernel, slab or width),
        grid=(tiles,),
        out_shape=(shape((rows, width), F32),) * 2 + tuple(grad_shapes),
        in_specs=[
            SMEM_SPEC,
            full,
            full,
            pl.BlockSpec((width, width), lambda t: (0, tiles + t)),
            down_spec,
        ],
        out_specs=(full, full) + tuple(grad_specs),
        scratch_shapes=[pltpu.VMEM((rows, width), BF16)] * 2 + [pltpu.VMEM((width, width), BF16)],
        compiler_params=pltpu.CompilerParams(vmem_limit_bytes=KERNEL_VMEM),
        cost_estimate=pl.CostEstimate(
            flops=12 * tiles * rows * width * width,
            bytes_accessed=12 * tiles * width * width,
            transcendentals=tiles * rows * width,
        ),
        name="feed_forward",
    )(core_bit, hn, dy, weights, weights)


def after(value, *others):
    return lax.optimization_barrier((value,) + others)[0]


def join(*values):
    return lax.optimization_barrier(values)


class Gather:
    def __init__(self, lay, index, shard):
        self.lay, self.index, self.rows, self.held = lay, index, shard.shape[0], shard
        self.bits, self.came, self.bit = (), None, None

    def start(self, bit, *others):
        if others:
            self.held = after(self.held, *others)
        self.bit = bit
        self.came = lax.ppermute(self.held, AXES, self.lay.bit_perm(bit))

    def finish(self, *others):
        came = after(self.came, *others) if others else self.came
        upper = ((self.index >> self.bit) & 1) == 1
        mine = self.held
        self.held = jnp.where(upper, jnp.stack([came, mine]), jnp.stack([mine, came]))
        self.bits = (self.bit,) + self.bits
        return self.held

    def step(self, bit, *others):
        self.start(bit, *others)
        return self.finish()

    def columns(self, start, stop):
        part = Gather(self.lay, self.index, self.held[..., start:stop])
        part.rows, part.bits = self.rows, self.bits
        return part

    def result(self):
        axes = tuple(self.bits.index(b) for b in sorted(self.bits, reverse=True))
        held = self.held.transpose(axes + tuple(range(len(axes), self.held.ndim)))
        return held.reshape((self.rows << len(axes),) + self.held.shape[len(axes) + 1 :])


class Scatter:
    def __init__(self, lay, index, arrays, left, kind=F32):
        self.lay, self.index, self.kind = lay, index, kind
        self.left = list(left)
        self.held, self.came, self.keep = list(arrays), None, None

    def start(self, bit, *others):
        if others:
            self.held = [after(h, *others) for h in self.held]
        axis = self.left.index(bit)
        self.left.pop(axis)
        mine = (self.index >> bit) & 1
        self.keep = [lax.dynamic_index_in_dim(h, mine, axis, keepdims=False) for h in self.held]
        give = [
            lax.dynamic_index_in_dim(h, 1 - mine, axis, keepdims=False).astype(BF16)
            for h in self.held
        ]
        give = jnp.concatenate(give, axis=-1) if len(give) > 1 else give[0]
        self.came = lax.ppermute(give, AXES, self.lay.bit_perm(bit))

    def finish(self, *others):
        came = after(self.came, *others) if others else self.came
        at, held = 0, []
        for keep in self.keep:
            total = keep.astype(F32) + came[..., at : at + keep.shape[-1]].astype(F32)
            held.append(total.astype(self.kind))
            at += keep.shape[-1]
        self.held = held
        return held

    def step(self, bit, *others):
        self.start(bit, *others)
        return self.finish()


def by_owner(array, n_bits):
    return array.reshape((2,) * n_bits + (array.shape[0] >> n_bits,) + array.shape[1:])


def unxor(items, mask):
    for bit in range((len(items) - 1).bit_length()):
        on = ((mask >> bit) & 1) == 1
        items = [jnp.where(on, items[k ^ (1 << bit)], items[k]) for k in range(len(items))]
    return items


def per_device(
    lay,
    tokens,
    cotangent,
    bounds,
    w_qkv,
    w_out,
    w_up,
    w_down,
    w_norms,
    m_qkv,
    m_out,
    m_up,
    m_down,
    m_norms,
    v_qkv,
    v_out,
    v_up,
    v_down,
    v_norms,
    a_qkv,
    a_out,
    a_up,
    a_down,
    a_norms,
):
    rows, width = tokens.shape[1], tokens.shape[2]
    n_heads = width // DH
    nh = n_heads // GROUPS
    index = lax.axis_index("seq") * lay.n_dp + lax.axis_index("dp")
    group = jnp.asarray(lay.grp_of)[index]
    blocks = jnp.asarray(lay.blocks)[index]
    pairs = jnp.asarray(lay.pairs)[index]

    if lay.moves:
        to_home = partial(lax.ppermute, axis_name=AXES, perm=lay.home_perm())
        to_owner = partial(lax.ppermute, axis_name=AXES, perm=lay.back_perm())
    else:
        to_home = to_owner = lambda v: v

    def to_groups(items):
        return [items[0]] + [
            lax.ppermute(items[m], AXES, lay.group_perm(m, 0)) for m in range(1, GROUPS)
        ]

    def for_group(array, axis, m):
        return lax.dynamic_index_in_dim(array, group ^ m, axis, keepdims=False)

    def across(array, mr):
        return lax.ppermute(array, AXES, lay.group_perm(0, mr))

    def by_head(shard):
        cut = shard.reshape(-1, 3, GROUPS, nh, DH).transpose(0, 3, 1, 2, 4)
        return cut.reshape(shard.shape)

    def from_by_head(shard):
        cut = shard.reshape(-1, nh, 3, GROUPS, DH).transpose(0, 2, 3, 1, 4)
        return cut.reshape(shard.shape)

    far, core = lay.far, lay.core

    def across_cores(array):
        return lax.ppermute(array, AXES, lay.bit_perm(core[0]))

    near_a = lay.near[0] + lay.near[1]
    near_b = lay.near[1] + lay.near[0]

    pad = jnp.zeros((w_qkv.shape[0], 128 - w_norms.shape[0]), BF16)
    low_qkv = by_head(w_qkv.astype(BF16))
    half = (3 * width // 2) // 128 * 128
    gather = Gather(
        lay, index, jnp.concatenate([low_qkv, w_norms.T.astype(BF16), pad], axis=1)
    )
    gather.start(far[-1])
    limits, gather.came = join(to_home(bounds[0]), gather.came)
    gather.finish()
    tokens_here = to_home(after(tokens[0], gather.held))
    tables = (pairs, blocks, limits)
    for bit in reversed(far[:-1]):
        gather.step(bit)
    gather_a, gather_b = gather.columns(0, half), gather.columns(half, 3 * width + 128)
    for bit_a, bit_b in zip(near_a, near_b):
        gather_a.start(bit_a)
        gather_b.start(bit_b)
        gather_a.finish()
        gather_b.finish()
    for bit in core:
        gather_a.start(bit)
        gather_b.start(bit)
        gather_a.finish()
        gather_b.finish()
    full_a, full_b = gather_a.result(), gather_b.result()
    qkv_full = jnp.concatenate([full_a, full_b[:, : 3 * width - half]], axis=1)
    gain_rows = full_b[:, 3 * width - half : 3 * width - half + 4].astype(F32).T

    own_rows, tiles = w_up.shape[0], w_up.shape[1] // width
    slab = own_rows if own_rows % 8 == 0 else 0

    def by_tile(shard):
        return shard if slab else shard.reshape(-1, width, tiles).swapaxes(1, 2).reshape(shard.shape)

    def from_by_tile(shard):
        return shard if slab else shard.reshape(-1, tiles, width).swapaxes(1, 2).reshape(shard.shape)

    def pack(shard):
        if slab:
            shard = jnp.swapaxes(shard.reshape(tiles, own_rows, width), 0, 1)
        return shard.reshape(own_rows, tiles * width)

    def unpack(shard):
        if slab:
            shard = jnp.swapaxes(shard.reshape(own_rows, tiles, width), 0, 1)
        return shard.reshape(tiles * own_rows, width)

    rest = jnp.concatenate(
        [pack(w_down.astype(BF16)), by_tile(w_up.astype(BF16)), w_out.astype(BF16)], axis=1
    )
    inputs = tokens_here.astype(F32)
    normed, first_pull = jax.vjp(layer_norm, inputs, gain_rows[0], gain_rows[1])
    normed_low = normed.astype(BF16)
    mixed = lax.dot_general(
        qkv_full, normed_low, (((0,), (1,)), ((), ())), preferred_element_type=F32
    ).astype(BF16)
    mixed = mixed.reshape(nh, 3, GROUPS, DH, rows)
    mixed = jnp.concatenate([mixed[:, :1] * jnp.asarray(DH**-0.5, BF16), mixed[:, 1:]], axis=1)

    def spread(cut):
        return to_groups([for_group(cut, 2, m) for m in range(GROUPS)])

    def both_parts(own):
        kv = jnp.stack([piece[:, 1:] for piece in own])
        return [across(kv, mr) for mr in range(1, lay.parts)]

    first_own = spread(mixed[:1])
    later_own = spread(after(mixed[1:], *first_own))
    rest_full = lax.all_gather(after(rest, *first_own), AXES, axis=0, tiled=True)
    out_full = rest_full[:, 2 * tiles * width :]
    first_other = both_parts(first_own)
    heads = [(0, first_own, first_other)]
    saved = [attend(lay, tables, *heads[0])]
    saved[0], later_own = join(saved[0], later_own)
    later_other = both_parts(later_own)
    for h in range(nh - 1):
        heads.append((h, later_own, later_other))
    grad_out = to_home(after(cotangent[0], saved[0][1]))
    saved.append(attend(lay, tables, *heads[1]))
    saved[1], grad_out = join(saved[1], grad_out)
    saved.append(attend(lay, tables, *heads[2]))
    att_back = to_groups([jnp.stack([saved[h][1][m] for h in range(nh)]) for m in range(GROUPS)])
    att_low = jnp.stack(unxor(att_back, group)).reshape(width, rows)

    branch = lax.dot_general(
        att_low, out_full, (((0,), (0,)), ((), ())), preferred_element_type=F32
    )
    resid_sum = inputs + branch
    hidden_norm, second_pull = jax.vjp(layer_norm, resid_sum, gain_rows[2], gain_rows[3])
    hidden_low = hidden_norm.astype(BF16)
    y, dhn, *ff_grads = feed_forward(
        hidden_low, grad_out, rest_full, slab, (index & 1).astype(jnp.int32).reshape(1)
    )
    result_low = (resid_sum + y).astype(BF16)
    descending = list(reversed(range(lay.n_bits)))
    if slab:
        down_keep, down_give, up_keep, up_give = ff_grads
    else:
        cut = [by_owner(a, lay.n_bits) for a in ff_grads]
        axis = lay.n_bits - 1
        pick = partial(lax.dynamic_index_in_dim, axis=axis, keepdims=False)
        down_keep, up_keep = (pick(a, index & 1) for a in cut)
        down_give, up_give = (pick(a, 1 - (index & 1)).astype(BF16) for a in cut)

    down_came, up_came = across_cores(down_give), across_cores(up_give)

    def after_cores(keep, came):
        total = (keep.astype(F32) + came.astype(F32)).astype(BF16)
        return by_owner(total.reshape(-1, total.shape[-1]), lay.n_bits - 1)

    back_resid, grad_gain2, grad_shift2 = second_pull(dhn)
    grad_resid = grad_out.astype(F32) + back_resid
    grad_branch = grad_resid.astype(BF16)
    dob = lax.dot_general(
        out_full, grad_branch, (((1,), (1,)), ((), ())), preferred_element_type=F32
    ).astype(BF16)
    dob = dob.reshape(GROUPS, nh, DH, rows)
    dob_pieces = to_groups([for_group(dob, 0, m) for m in range(GROUPS)])
    grad_wout = lax.dot_general(
        att_low, grad_branch, (((1,), (0,)), ((), ())), preferred_element_type=F32
    )
    scatter_out = Scatter(lay, index, [by_owner(grad_wout, lay.n_bits)], descending, BF16)
    scatter_out.step(core[0])
    scatter_d = Scatter(
        lay, index, [scatter_out.held[0], after_cores(down_keep, down_came)], scatter_out.left, BF16
    )
    scatter_c = Scatter(lay, index, [after_cores(up_keep, up_came)], scatter_out.left, BF16)
    for bit in core[1:]:
        scatter_d.step(bit)
        scatter_c.step(bit)
    scatter_d.start(near_b[0])
    scatter_c.start(near_a[0], *dob_pieces)

    def back(h, *others):
        pieces = [after(dob_pieces[0], *others)] + dob_pieces[1:]
        return attend_back(lay, tables, *heads[h], h, pieces, saved[h][0], saved[h][2])

    def share(grads):
        return [across(grads[1 + mr], mr) for mr in range(1, lay.parts)]

    def summed_pieces(grads, came):
        total = grads[1]
        for piece in came:
            total = total + piece.astype(F32)
        low = total.astype(BF16)
        return [jnp.concatenate([grads[0][m][None], low[m]], axis=0) for m in range(GROUPS)]

    def rejoin(pieces):
        return jnp.stack(unxor(pieces, group), axis=1).reshape(3 * width // nh, rows)

    first = back(0, *scatter_c.held, *scatter_d.held)
    first, scatter_c.came, scatter_d.came = join(first, scatter_c.came, scatter_d.came)
    shared = share(first)
    scatter_d.finish()
    scatter_c.finish()
    for bit_a, bit_b in zip(near_a[1:-1], near_b[1:-1]):
        scatter_c.step(bit_a)
        scatter_d.step(bit_b)
    second = back(1, *scatter_c.held, *scatter_d.held)
    scatter_d.start(near_b[-1])
    scatter_c.start(near_a[-1])
    layer_out = to_owner(after(result_low[None], *scatter_c.held, *scatter_d.held))
    second, shared, scatter_c.came, scatter_d.came, layer_out = join(
        second, shared, scatter_c.came, scatter_d.came, layer_out
    )
    scatter_d.finish()
    scatter_c.finish()
    shared_two = share(second)
    scatter_d.start(far[0])
    scatter_c.start(far[0])
    pieces = [
        jnp.stack(pair)
        for pair in zip(summed_pieces(first, shared), summed_pieces(second, shared_two))
    ]
    returned_two = to_groups(pieces)
    third = back(2, *scatter_c.held, *scatter_d.held, *pieces)
    third, returned_two, scatter_c.came, scatter_d.came = join(
        third, returned_two, scatter_c.came, scatter_d.came
    )
    returned = [[piece[h] for piece in returned_two] for h in range(2)]
    shared = share(third)
    scatter_d.finish()
    scatter_c.finish()
    for bit in far[1:-1]:
        scatter_c.step(bit)
        scatter_d.step(bit)
    scatter_d.start(far[-1])
    scatter_c.start(far[-1])
    returned.append(to_groups(summed_pieces(third, shared)))
    mixed_grads = [rejoin(pieces) for pieces in returned]
    mixed_grad = jnp.concatenate(mixed_grads, axis=0)

    def weight_grad(piece):
        return lax.dot_general(
            normed_low, piece, (((0,), (1,)), ((), ())), preferred_element_type=F32
        )

    grad_normed = lax.dot_general(
        mixed_grad, qkv_full, (((0,), (1,)), ((), ())), preferred_element_type=F32
    )
    back_input, grad_gain1, grad_shift1 = first_pull(grad_normed)
    grad_vec = jnp.stack([grad_gain1, grad_shift1, grad_gain2, grad_shift2]).T
    grad_vec = jnp.concatenate([grad_vec, jnp.zeros((width, 124), F32)], axis=1)
    wqkv_grads = [weight_grad(piece) for piece in mixed_grads]
    scatter = Scatter(
        lay, index, [by_owner(a, lay.n_bits) for a in wqkv_grads + [grad_vec]], descending
    )
    for bit in core:
        scatter.step(bit)
    one, two, three, vec = scatter.held
    split = half - 3 * width // nh
    scatter_a = Scatter(lay, index, [one, two[..., :split]], scatter.left)
    scatter_b = Scatter(lay, index, [two[..., split:], three, vec], scatter.left)
    for bit_a, bit_b in zip(near_a, near_b):
        scatter_a.start(bit_a)
        scatter_b.start(bit_b)
        scatter_a.finish()
        scatter_b.finish()
    scatter = Scatter(lay, index, scatter_a.held + scatter_b.held, scatter_a.left)
    for bit in far:
        scatter.step(bit)
    input_low = to_owner(after((grad_resid + back_input).astype(BF16), *scatter.held))
    (summed_out, summed_down), (summed_up,) = scatter_d.finish(), scatter_c.finish()
    summed_qkv = from_by_head(jnp.concatenate(scatter.held[:4], axis=1))
    summed_out, summed_up = summed_out.astype(F32), from_by_tile(summed_up.astype(F32))
    summed_down = unpack(summed_down.astype(F32))
    summed_norms = scatter.held[4][:, :4].T
    input_grad = input_low.astype(F32)[None]

    summed = (summed_qkv, summed_out, summed_up, summed_down, summed_norms)
    square = sum((jnp.sum(member * member) for member in summed))
    for bit in range(lay.n_bits):
        square = square + lax.ppermute(square, AXES, lay.bit_perm(bit))
    grad_norm = jnp.sqrt(square)
    factor = CLIP_NORM / jnp.maximum(grad_norm, CLIP_NORM)
    upd_qkv = adamw(w_qkv, summed_qkv * factor, m_qkv, v_qkv, a_qkv, RATE_MAT, WEIGHT_DECAY)
    upd_out = adamw(w_out, summed_out * factor, m_out, v_out, a_out, RATE_OUT, WEIGHT_DECAY)
    upd_up = adamw(w_up, summed_up * factor, m_up, v_up, a_up, RATE_MAT, WEIGHT_DECAY)
    upd_down = adamw(w_down, summed_down * factor, m_down, v_down, a_down, RATE_MAT, WEIGHT_DECAY)
    upd_norms = adamw(w_norms, summed_norms * factor, m_norms, v_norms, a_norms, RATE_VEC, 0.0)
    updates = (upd_qkv, upd_out, upd_up, upd_down, upd_norms)
    return (layer_out, input_grad, grad_norm) + tuple(u[k] for k in range(4) for u in updates)


def solution(mesh):
    lay = Layout(mesh.shape["seq"], mesh.shape["dp"])
    rows = P(AXES, None)
    vecs = P(None, AXES)
    state = (rows, rows, rows, rows, vecs)
    block = P("dp", "seq", None)
    return jax.shard_map(
        partial(per_device, lay),
        mesh=mesh,
        in_specs=(block, block, P("dp", None)) + state * 4,
        out_specs=(block, block, P()) + state * 4,
        check_vma=False,
    )
```
